128 devices in a mesh: row: 16 (over x, z), col: 8 (over y, core).
Axes of the slice: x: 4, y: 4, z: 4, core: 2. Of those that a mesh axis runs over, the one named last changes fastest.
Arguments:
- roughness: float32 [8192, 8192], P('row', 'col'), may hold values from -6 to 6
- transfer_real: float32 [8192, 8192], P(('row', 'col')), may hold values from -6 to 6
- transfer_imag: float32 [8192, 8192], P(('row', 'col')), may hold values from -6 to 6
- station_cells: int32 [2, 65536], P(None, ('row', 'col')), may hold values from 0 to 8191, as said below
- station_weights: float32 [4, 65536], P(None, ('row', 'col')), may hold values from 0.1 to 1
- station_means: float32 [65536], P(('row', 'col')), may hold values from -6 to 6
- station_counts: int32 [128], P(('row', 'col')), may hold values from 64 to 512, as said below
Outputs:
- gradient: float32 [8192, 8192], P('row', 'col')
- misfit: float32 [65536], P(('row', 'col'))
The draws below stay inside these ranges and needn't reach their ends.
Inputs may be any that keep to these rules, and one draw needn't show every extreme that they name: With t = s // 512, the cell (station_cells[0, s], station_cells[1, s]) lies in tile t: its first index in [(t // 8) * 512, (t // 8 + 1) * 512), its second in [(t mod 8) * 1024, (t mod 8 + 1) * 1024), with 8 the number of tiles along the second dimension. `station_counts`: some tile holds exactly 512 live stations.
All inputs are finite; a program needn't handle non-finite values.
Results may differ from the reference program's by a relative error of at most 0.000098.
Values sent between devices are 32-bit elements; how exact they have to be, the bound alone decides.
No kernel may reach another device: no remote copies, remote signals or barrier semaphores. Data moves between devices by JAX's collectives and lax.ppermute only.
A program may use at most 128 MiB of HBM per device.

```python
import math
import jax
import jax.numpy as jnp

N = 8192
STAT_DEV = 512
TILES = 128
STATIONS = 65536
TILE_ROWS = 512
TILE_COLS = 1024
N_COL = 8


def draw_station_counts(key, part):
    keys = jax.random.split(key, 2)
    halvings = jax.random.randint(keys[0], (TILES,), 0, 4)
    counts = STAT_DEV // jnp.left_shift(jnp.int32(1), halvings)
    busiest = jax.random.randint(keys[1], (), 0, TILES)
    return jnp.where(jnp.arange(TILES) == busiest, STAT_DEV, counts).astype(jnp.int32)


def draw_station_cells(key, part):
    keys = jax.random.split(jax.random.fold_in(key, 17), 2)
    slots = jnp.arange(STATIONS, dtype=jnp.int32)
    tiles = slots // STAT_DEV
    tile_row = tiles // N_COL
    tile_col = tiles % N_COL
    local_rows = jax.random.randint(keys[0], (STATIONS,), 0, TILE_ROWS)
    local_cols = jax.random.randint(keys[1], (STATIONS,), 0, TILE_COLS)
    kind = slots % STAT_DEV % 8
    local_rows = jnp.where((kind == 0) | (kind == 2), TILE_ROWS - 1, local_rows)
    local_cols = jnp.where((kind == 1) | (kind == 2), TILE_COLS - 1, local_cols)
    local_rows = jnp.where(kind == 3, 0, local_rows)
    local_cols = jnp.where(kind == 3, 0, local_cols)
    first = tile_row * TILE_ROWS + local_rows
    second = tile_col * TILE_COLS + local_cols
    return jnp.stack([first, second]).astype(jnp.int32)


def levels(stream_key, extent, cuts, low, largest):
    level, own = 1.0, jax.random.fold_in(stream_key, 6)
    for position, parts in cuts:
        draws = jnp.exp(jax.random.uniform(jax.random.fold_in(own, position), (parts,), jnp.float32, low / len(cuts), largest / len(cuts)))
        level = level * jnp.repeat(draws, extent[position] // parts).reshape([-1 if axis == position else 1 for axis in range(len(extent))])
    return level


def noise(stream_key, dims, deviation, limit, cuts=(), kind=jnp.bfloat16):
    result = jax.random.normal(stream_key, dims, jnp.float32) * deviation
    if len(cuts) > 0:
        result = levels(stream_key, dims, cuts, -0.22, 0.18) * result
    return jnp.clip(result, min=-limit, max=limit).astype(kind)


def setup_inputs(seed: int = 0) -> dict:
    streams_of = jax.random.split(jax.random.key(seed), 8)
    return {
        "roughness": noise(streams_of[0], (N, N), 1.0, 6.0, ((0, 16), (1, 8)), jnp.float32),
        "transfer_real": noise(streams_of[1], (N, N), 1.0, 6.0, ((0, 128),), jnp.float32),
        "transfer_imag": noise(streams_of[2], (N, N), 1.0, 6.0, ((0, 128),), jnp.float32),
        "station_cells": draw_station_cells(jax.random.fold_in(streams_of[7], 71), 0),
        "station_weights": jnp.clip(0.1 + 0.9 * jax.random.uniform(streams_of[4], (4, STATIONS), jnp.float32) ** levels(streams_of[4], (4, STATIONS), ((1, 128),), -0.2, 0.2), 0.1, 1.0),
        "station_means": noise(streams_of[5], (STATIONS,), 1.0, 6.0, ((0, 128),), jnp.float32),
        "station_counts": draw_station_counts(jax.random.fold_in(streams_of[7], 71), 0),
    }


def reference(roughness, transfer_real, transfer_imag, station_cells, station_weights, station_means, station_counts):
    side = roughness.shape[0]
    transfer = jnp.transpose(transfer_real + 1j * transfer_imag)
    response = jnp.real(jnp.fft.ifft2(jnp.fft.fft2(roughness) * transfer))
    cell_rows = station_cells[0]
    cell_cols = station_cells[1]
    interp = jnp.zeros(cell_rows.shape, jnp.float32)
    for which in range(4):
        rows_at = (cell_rows + which // 2) % side
        cols_at = (cell_cols + which % 2) % side
        interp = interp + station_weights[which] * response[rows_at, cols_at]
    slots = jnp.arange(STATIONS, dtype=jnp.int32)
    live = slots % STAT_DEV < station_counts[slots // STAT_DEV]
    misfit = jnp.where(live, interp - station_means, jnp.float32(0.0))
    forcing = jnp.zeros((side, side), jnp.float32)
    for which in range(4):
        rows_at = (cell_rows + which // 2) % side
        cols_at = (cell_cols + which % 2) % side
        forcing = forcing.at[rows_at, cols_at].add(station_weights[which] * misfit)
    scale = math.sqrt(side * side / STATIONS)
    gradient = jnp.real(jnp.fft.ifft2(jnp.fft.fft2(forcing) * jnp.conj(transfer))) * scale
    return (gradient.astype(jnp.float32), misfit)
```

```python
import functools
import math

import jax
import jax.numpy as jnp
import numpy as np
from jax import lax
from jax.experimental import pallas as pl
from jax.experimental.pallas import tpu as pltpu
from jax.sharding import PartitionSpec as P

F32 = jnp.float32
BF16 = jnp.bfloat16

N = 8192
LANES = 128
SHORT = 64
PAIRS = 17
ROWS = 2 * PAIRS
VMEM_LIMIT = 40 * 1024 * 1024


def split_np(table):
    hi = table.astype(np.float32).astype(jnp.bfloat16)
    lo = (table - hi.astype(np.float64)).astype(np.float32).astype(jnp.bfloat16)
    return np.stack([hi, lo])


def complex_table(length, copies, sign):
    index = np.arange(length)
    angles = 2.0 * np.pi * (index[:, None] * index[None, :] % length) / length
    cos = np.kron(np.eye(copies), np.cos(angles))
    sin = sign * np.kron(np.eye(copies), np.sin(angles))
    return np.block([[cos, -sin], [sin, cos]])


def twiddle_table(left, right, sign):
    angles = 2.0 * np.pi * (left[:, None] * right[None, :] % N) / N
    return np.stack([np.cos(angles), sign * np.sin(angles)]).astype(np.float32)


def split(x):
    hi = x.astype(BF16)
    lo = (x - hi.astype(F32)).astype(BF16)
    return hi, lo


def mm(a, b, dims):
    return lax.dot_general(a, b, (dims, ((), ())), preferred_element_type=F32)


NN = ((1,), (0,))
NT = ((1,), (1,))


def table_times(tab, data, dims):
    hi, lo = split(data)
    return mm(tab[0], hi, dims) + (mm(tab[1], hi, dims) + mm(tab[0], lo, dims))


def times_table(data, tab, dims):
    hi, lo = split(data)
    return mm(hi, tab[0], dims) + (mm(hi, tab[1], dims) + mm(lo, tab[0], dims))


RT = math.sqrt(0.5)


def cadd(a, b):
    return (a[0] + b[0], a[1] + b[1])


def csub(a, b):
    return (a[0] - b[0], a[1] - b[1])


def cmul(a, b):
    return (a[0] * b[0] - a[1] * b[1], a[0] * b[1] + a[1] * b[0])


def times_i(a, sign):
    return (-a[1], a[0]) if sign > 0 else (a[1], -a[0])


def turn(a, angle):
    c, s = math.cos(angle), math.sin(angle)
    return (a[0] * c - a[1] * s, a[0] * s + a[1] * c)


def dft4(x, sign):
    a, b = cadd(x[0], x[2]), csub(x[0], x[2])
    c, d = cadd(x[1], x[3]), times_i(csub(x[1], x[3]), sign)
    return [cadd(a, c), cadd(b, d), csub(a, c), csub(b, d)]


def eighth(a, sign):
    if sign > 0:
        return ((a[0] - a[1]) * RT, (a[0] + a[1]) * RT)
    return ((a[0] + a[1]) * RT, (a[1] - a[0]) * RT)


def dft8(x, sign):
    even = dft4(x[0::2], sign)
    odd = dft4(x[1::2], sign)
    odd[1] = eighth(odd[1], sign)
    odd[2] = times_i(odd[2], sign)
    odd[3] = times_i(eighth(odd[3], sign), sign)
    return [cadd(even[i], odd[i]) for i in range(4)] + [csub(even[i], odd[i]) for i in range(4)]


def real_dft8(x):
    a, b = x[0] + x[4], x[0] - x[4]
    c, d = x[2] + x[6], x[2] - x[6]
    e, f = x[1] + x[5], x[1] - x[5]
    g, h = x[3] + x[7], x[3] - x[7]
    even, odd = a + c, e + g
    u, v = (f - h) * RT, (f + h) * RT
    return [(even + odd, None), (b + u, -(d + v)), (a - c, g - e), (b - u, d - v), (even - odd, None)]


def real_fft64(x):
    first = [real_dft8([x[8 * u + v] for u in range(8)]) for v in range(8)]
    out = [None] * 33
    zero_part = real_dft8([first[v][0][0] for v in range(8)])
    for t in range(5):
        out[8 * t] = zero_part[t]
    for s in range(1, 4):
        turned = [first[0][s]] + [turn(first[v][s], -2 * math.pi * v * s / 64) for v in range(1, 8)]
        done = dft8(turned, -1)
        for t in range(8):
            p = s + 8 * t
            if p <= 32:
                out[p] = done[t]
            else:
                out[64 - p] = (done[t][0], -done[t][1])
    real = [first[v][4][0] for v in range(8)]
    turned = []
    for v in range(8):
        c, s = math.cos(2 * math.pi * v / 16), -math.sin(2 * math.pi * v / 16)
        turned.append((real[v] * c, real[v] * s))
    turned[0] = (real[0], jnp.zeros_like(real[0]))
    done = dft8(turned, -1)
    for t in range(4):
        out[4 + 8 * t] = done[t]
    return out


def real_of_inverse8(zero, four, one, two, three):
    a, b = zero + four, zero - four
    res = [None] * 8
    even_p, even_m = a + two[0], a - two[0]
    odd_p, odd_m = b - two[1], b + two[1]
    sum_r, dif_i = one[0] + three[0], one[1] - three[1]
    res[0], res[4] = even_p + sum_r, even_p - sum_r
    res[2], res[6] = even_m - dif_i, even_m + dif_i
    k1 = ((one[0] - three[0]) - (one[1] + three[1])) * RT
    k3 = ((three[0] - one[0]) - (one[1] + three[1])) * RT
    res[1], res[5] = odd_p + k1, odd_p - k1
    res[3], res[7] = odd_m + k3, odd_m - k3
    return res


def real_of_inverse64(v):
    zero = real_of_inverse8(v[0][0], v[32][0], v[8], v[16], v[24])
    parts = [v[4], v[12], v[20], v[28]]
    four = []
    quarter = dft4(parts, 1)
    turned = [parts[0], eighth(parts[1], 1), times_i(parts[2], 1), times_i(eighth(parts[3], 1), 1)]
    shifted = dft4(turned, 1)
    for m in range(8):
        value = quarter[m // 2] if m % 2 == 0 else shifted[m // 2]
        angle = 2 * math.pi * m / 16
        four.append(value[0] * math.cos(angle) - value[1] * math.sin(angle) if m else value[0])
    others = []
    for s in range(1, 4):
        x = []
        for t in range(8):
            p = s + 8 * t
            x.append(v[p] if p <= 32 else (v[64 - p][0], -v[64 - p][1]))
        done = dft8(x, 1)
        others.append([done[0]] + [turn(done[m], 2 * math.pi * m * s / 64) for m in range(1, 8)])
    out = [None] * 64
    for m in range(8):
        res = real_of_inverse8(zero[m], four[m], others[0][m], others[1][m], others[2][m])
        for u in range(8):
            out[8 * u + m] = res[u]
    return out


def rows_forward_kernel(has_carry, *refs):
    if has_carry:
        strip, carry, tab, tw, out, z = refs
    else:
        strip, tab, tw, out, z = refs

    def lines(t, _):
        x0 = pl.multiple_of(t * 8, 8)
        x = []
        for m in range(64):
            value = strip[m // 8, pl.ds(x0, 8), (m % 8) * LANES : (m % 8 + 1) * LANES]
            if has_carry:
                here = (lax.broadcasted_iota(jnp.int32, (8, LANES), 0) + x0) == 0
                value = value + jnp.where(here, carry[m : m + 1, :], 0.0)
            x.append(value)
        done = real_fft64(x)
        for p in range(33):
            re, im = done[p]
            c, s = tw[0, p : p + 1, :], tw[1, p : p + 1, :]
            if im is None:
                new_re, new_im = re * c, re * s
            else:
                new_re, new_im = re * c - im * s, re * s + im * c
            z[pl.ds(p * 64 + x0, 8), 0:LANES] = new_re
            z[pl.ds(p * 64 + x0, 8), LANES : 2 * LANES] = new_im
        return 0

    lax.fori_loop(0, 8, lines, 0)
    z[33 * 64 :, :] = jnp.zeros((64, 2 * LANES), F32)

    def pair(j, _):
        data = z[pl.ds(pl.multiple_of(j * 128, 128), 128), :]
        res = table_times(tab, data, NT)
        out[pl.ds(2 * j, 128, stride=ROWS), :] = res[:128]
        out[pl.ds(2 * j + 1, 128, stride=ROWS), :] = res[128:]
        return 0

    lax.fori_loop(0, PAIRS, pair, 0, unroll=True)


def columns_kernel(conj, moved, g_re, g_im, tab1, tab2, tab2i, tab1i, tw, twt, out):
    def pair(j, _):
        data = jnp.concatenate(
            [moved[pl.ds(2 * j, 128, stride=ROWS), :], moved[pl.ds(2 * j + 1, 128, stride=ROWS), :]], axis=0
        )
        y = table_times(tab1, data, NN)
        re, im = cmul((y[:128], y[128:]), (tw[0], tw[1]))
        spec = table_times(tab2, jnp.concatenate([re, im], axis=1), NT)
        gr = g_re[pl.ds(2 * j, 2)].reshape(128, LANES)
        gi = g_im[pl.ds(2 * j, 2)].reshape(128, LANES)
        if conj:
            gi = -gi
        re, im = cmul((spec[:128], spec[128:]), (gr, gi))
        w = table_times(tab2i, jnp.concatenate([re, im], axis=0), NN)
        re, im = cmul((w[:128], w[128:]), (twt[0], twt[1]))
        res = table_times(tab1i, jnp.concatenate([re, im], axis=1), NT)
        out[pl.ds(2 * j, 128, stride=ROWS), :] = res[:128]
        out[pl.ds(2 * j + 1, 128, stride=ROWS), :] = res[128:]
        return 0

    lax.fori_loop(0, PAIRS, pair, 0, unroll=True)


def rows_inverse_kernel(scale, home, tab, tw, out, v):
    def pair(j, _):
        re = home[pl.ds(2 * j, 128, stride=ROWS), :].T
        im = home[pl.ds(2 * j + 1, 128, stride=ROWS), :].T
        y = times_table(jnp.concatenate([re, im], axis=1), tab, NT)
        re, im = y[:, :LANES], y[:, LANES:]
        for half in range(2):
            p = 2 * j + half
            c, s = tw[0, pl.ds(p, 1), :] * scale, tw[1, pl.ds(p, 1), :] * scale
            a, b = re[half * 64 : half * 64 + 64], im[half * 64 : half * 64 + 64]
            rows = pl.ds(pl.multiple_of(j * 128 + half * 64, 64), 64)
            v[rows, 0:LANES] = a * c - b * s
            v[rows, LANES : 2 * LANES] = a * s + b * c
        return 0

    lax.fori_loop(0, PAIRS, pair, 0, unroll=True)

    def lines(t, _):
        x0 = pl.multiple_of(t * 8, 8)
        values = []
        for p in range(33):
            rows = pl.ds(p * 64 + x0, 8)
            values.append((v[rows, 0:LANES], v[rows, LANES : 2 * LANES]))
        done = real_of_inverse64(values)
        for m in range(64):
            out[m // 8, pl.ds(x0, 8), (m % 8) * LANES : (m % 8 + 1) * LANES] = done[m]
        return 0

    lax.fori_loop(0, 8, lines, 0)


def stations_kernel(r, edge, st, stt, force, spill, mis_out, r4, f4):
    lane64 = lax.broadcasted_iota(jnp.int32, (64, LANES), 1)
    row64 = lax.broadcasted_iota(jnp.int32, (64, LANES), 0)
    eye = lax.broadcasted_iota(jnp.int32, (128, 128), 0) == lax.broadcasted_iota(jnp.int32, (128, 128), 1)

    def shifted(t, _):
        after = lax.rem(t + 1, 8)
        own, down = [], []
        for m in range(9):
            a = r[t, :, m * LANES : (m + 1) * LANES] if m < 8 else r[after, :, 0:LANES]
            line = edge[pl.ds(t * 8 + m, 1), :] if m < 8 else edge[pl.ds(after * 8, 1), :]
            own.append(a)
            down.append(jnp.where(row64 == 63, line, pltpu.roll(a, 63, 0)))
        own_l = [pltpu.roll(a, LANES - 1, 1) for a in own]
        down_l = [pltpu.roll(a, LANES - 1, 1) for a in down]
        for m in range(8):
            rows = pl.ds(pl.multiple_of(t * 512 + m * 64, 64), 64)
            four = [
                own[m],
                jnp.where(lane64 == LANES - 1, own_l[m + 1], own_l[m]),
                down[m],
                jnp.where(lane64 == LANES - 1, down_l[m + 1], down_l[m]),
            ]
            for k in range(4):
                hi, lo = split(four[k])
                r4[0, rows, k * LANES : (k + 1) * LANES] = hi
                r4[1, rows, k * LANES : (k + 1) * LANES] = lo
        return 0

    lax.fori_loop(0, 8, shifted, 0)

    lane512 = lax.broadcasted_iota(jnp.int32, (512, LANES), 1).astype(F32)
    key_cols = lax.broadcasted_iota(jnp.int32, (512, 512), 1).astype(F32)
    key_rows = lax.broadcasted_iota(jnp.int32, (512, 512), 0).astype(F32)

    def tile(t, _):
        col = stt[t]
        key, low = col[:, 0:1], col[:, 1:2]
        pick = jnp.where(key_cols == key, 1.0, 0.0).astype(BF16)
        rows = pl.ds(pl.multiple_of(t * 512, 512), 512)
        got = mm(pick, r4[0, rows, :], NN) + mm(pick, r4[1, rows, :], NN)
        value = col[:, 2:3] * got[:, 0:LANES]
        for k in range(1, 4):
            value = value + col[:, 2 + k : 3 + k] * got[:, k * LANES : (k + 1) * LANES]
        here = lane512 == low
        interp = jnp.sum(jnp.where(here, value, 0.0), axis=1, keepdims=True)
        misfit = jnp.where(col[:, 7:8] > 0.5, interp - col[:, 6:7], 0.0)
        for i in range(4):
            part = jnp.where(eye, misfit[i * 128 : (i + 1) * 128], 0.0)
            mis_out[t, :, i * 128 : (i + 1) * 128] = jnp.sum(part, axis=0, keepdims=True)
        spread = jnp.where(here, misfit, 0.0)
        values = jnp.concatenate([spread * col[:, 2 + k : 3 + k] for k in range(4)], axis=1)
        hi, lo = split(values)
        back = jnp.where(key_rows == st[t, 0:1, :], 1.0, 0.0).astype(BF16)
        f4[rows, :] = mm(back, hi, NN) + mm(back, lo, NN)
        return 0

    lax.fori_loop(0, 8, tile, 0)

    def assemble(t, _):
        before = lax.rem(t + 7, 8)
        last = []
        for m in range(-1, 8):
            start = before * 512 + 448 if m < 0 else t * 512 + m * 64
            rows = pl.ds(pl.multiple_of(start, 64), 64)
            last.append([pltpu.roll(f4[rows, k * LANES : (k + 1) * LANES], 1, 1) for k in (1, 3)])
        for m in range(8):
            rows = pl.ds(pl.multiple_of(t * 512 + m * 64, 64), 64)
            same = f4[rows, 0:LANES] + jnp.where(lane64 == 0, last[m][0], last[m + 1][0])
            below = f4[rows, 2 * LANES : 3 * LANES] + jnp.where(lane64 == 0, last[m][1], last[m + 1][1])
            spill[pl.ds(t * 8 + m, 1), :] = below[63:64, :]
            force[t, :, m * LANES : (m + 1) * LANES] = same + jnp.where(row64 == 0, 0.0, pltpu.roll(below, 1, 0))
        return 0

    lax.fori_loop(0, 8, assemble, 0)


def mirror_kernel(t_re, t_im, m_re, m_im, rows_tab, lane_tab, g_re, g_im):
    lane = lax.broadcasted_iota(jnp.int32, (64, LANES), 1)
    g_re[0], g_im[0] = t_re[0], t_im[0]
    g_re[32], g_im[32] = t_re[32], t_im[32]
    g_re[33], g_im[33] = jnp.zeros((64, LANES), F32), jnp.zeros((64, LANES), F32)

    def one(p, _):
        both = jnp.concatenate([m_re[31 - p], m_im[31 - p]], axis=1)
        total = []
        for part in split(both):
            flipped = mm(rows_tab[...], part, NN).astype(BF16)
            total.append([mm(flipped[:, :LANES], lane_tab[...], NN), mm(flipped[:, LANES:], lane_tab[...], NN)])
        re, im = total[0][0] + total[1][0], total[0][1] + total[1][1]
        g_re[p] = t_re[p] + jnp.where(lane == 0, re[64:], re[:64])
        g_im[p] = t_im[p] - jnp.where(lane == 0, im[64:], im[:64])
        return 0

    lax.fori_loop(1, 32, one, 0)


def call(kernel, out_shape, scratch, *args, name, cost=None):
    single = isinstance(out_shape, jax.ShapeDtypeStruct)
    vmem = pl.BlockSpec(memory_space=pltpu.VMEM)
    return pl.pallas_call(
        kernel,
        out_shape=out_shape,
        in_specs=[vmem] * len(args),
        out_specs=vmem if single else [vmem] * len(out_shape),
        scratch_shapes=scratch,
        compiler_params=pltpu.CompilerParams(vmem_limit_bytes=VMEM_LIMIT),
        cost_estimate=cost,
        name=name,
    )(*args)


def cost(us):
    return pl.CostEstimate(flops=int(us * 1.0e9), bytes_accessed=4 * 1024 * 1024, transcendentals=0)


def shape(*dims, dtype=F32):
    return jax.ShapeDtypeStruct(dims, dtype)


def tables():
    n = np.arange(LANES)
    p = np.minimum(np.arange(ROWS), 32)
    x1 = np.arange(128) % 64
    fwd, inv = complex_table(128, 1, -1.0), complex_table(128, 1, 1.0)
    fwd2, inv2 = complex_table(64, 2, -1.0), complex_table(64, 2, 1.0)
    return {
        "fwd": split_np(fwd),
        "inv": split_np(inv),
        "fwd2": split_np(fwd2),
        "inv2": split_np(inv2),
        "row_fwd": twiddle_table(p, n, -1.0),
        "row_inv": twiddle_table(p, n, 1.0),
        "col_fwd": twiddle_table(n, x1, -1.0),
        "col_inv": twiddle_table(x1, n, 1.0),
    }


def rows_forward(strip, carry, tabs):
    args = [strip] + ([] if carry is None else [carry]) + [tabs["fwd"], tabs["row_fwd"]]
    return call(
        functools.partial(rows_forward_kernel, carry is not None),
        shape(128 * ROWS, LANES),
        [pltpu.VMEM((ROWS * 64, 2 * LANES), F32)],
        *args,
        name="rows_forward",
        cost=cost(6),
    )


def columns(moved, g_re, g_im, conj, tabs):
    return call(
        functools.partial(columns_kernel, conj),
        shape(128 * ROWS, LANES),
        [],
        moved,
        g_re,
        g_im,
        tabs["fwd"],
        tabs["fwd2"],
        tabs["inv2"],
        tabs["inv"],
        tabs["col_fwd"],
        tabs["col_inv"],
        name="columns",
        cost=cost(8),
    )


def rows_inverse(home, scale, tabs):
    return call(
        functools.partial(rows_inverse_kernel, scale),
        shape(8, 64, 1024),
        [pltpu.VMEM((ROWS * 64, 2 * LANES), F32)],
        home,
        tabs["inv"],
        tabs["row_inv"],
        name="rows_inverse",
        cost=cost(6),
    )


def stations(r, edge, st, stt):
    return call(
        stations_kernel,
        (shape(8, 64, 1024), shape(64, LANES), shape(8, 1, 512)),
        [pltpu.VMEM((2, 4096, 512), BF16), pltpu.VMEM((4096, 512), F32)],
        r,
        edge,
        st,
        stt,
        name="stations",
        cost=cost(15),
    )


def mirror(t_re, t_im, m_re, m_im):
    b = np.arange(64)
    rows = np.zeros((128, 64), np.float32)
    rows[b, 63 - b] = 1.0
    rows[64 + b, (64 - b) % 64] = 1.0
    a = np.arange(128)
    lanes = np.zeros((128, 128), np.float32)
    lanes[(128 - a) % 128, a] = 1.0
    return call(
        mirror_kernel,
        (shape(ROWS, 64, LANES), shape(ROWS, 64, LANES)),
        [],
        t_re,
        t_im,
        m_re,
        m_im,
        jnp.asarray(rows, BF16),
        jnp.asarray(lanes, BF16),
        name="mirror",
        cost=cost(6),
    )


BOTH = ("row", "col")


def swap(array):
    return lax.all_to_all(array, BOTH, split_axis=0, concat_axis=0, tiled=True)


def across(array):
    return lax.all_to_all(array, "col", split_axis=0, concat_axis=0, tiled=True)


def ring(array, by):
    return lax.ppermute(array, BOTH, [(i, (i + by) % 128) for i in range(128)])


def station_fields(cells, weights, means, counts):
    slots = means.shape[0]
    local_x = cells[0] - lax.axis_index("row") * 512
    local_y = cells[1] - lax.axis_index("col") * 1024
    live = jnp.arange(slots, dtype=jnp.int32) < counts[0]
    fields = jnp.stack(
        [local_x.astype(F32), local_y.astype(F32)]
        + [weights[k] for k in range(4)]
        + [means, live.astype(F32)]
    )
    gathered = lax.all_gather(fields, "col", axis=0, tiled=False)
    x = gathered[:, 0] - lax.axis_index("col").astype(F32) * 64.0
    y = gathered[:, 1]
    high = jnp.floor(y * (1.0 / 128.0))
    inside = (x >= 0.0) & (x < 64.0)
    key = jnp.where(inside, high * 64.0 + x, -1.0)
    live_here = jnp.where(inside, gathered[:, 7], 0.0)
    rest = [gathered[:, k] for k in range(2, 7)]
    return jnp.stack([key, y - high * 128.0] + rest + [live_here], axis=1)


def local(
    roughness,
    transfer_real,
    transfer_imag,
    station_cells,
    station_weights,
    station_means,
    station_counts,
):
    tabs = tables()
    t_re = transfer_real.reshape(64, 64, 128)
    t_im = transfer_imag.reshape(64, 64, 128)
    mirrored = [(i, 127 - i) for i in range(128)]
    m_re = lax.ppermute(t_re[33:], BOTH, mirrored)
    m_im = lax.ppermute(t_im[33:], BOTH, mirrored)
    st = station_fields(station_cells, station_weights, station_means, station_counts)
    stt = jnp.swapaxes(st, 1, 2)

    strip = across(roughness.reshape(8, 64, 1024))
    moved = swap(rows_forward(strip, None, tabs))
    g_re, g_im = mirror(t_re, t_im, m_re, m_im)
    home = swap(columns(moved, g_re, g_im, False, tabs))
    response = rows_inverse(home, 1.0 / (N * N), tabs)

    edge = ring(response[:, 0, :].reshape(64, 128), -1)
    force, spill, misfits = stations(response, edge, st, stt)
    carry = ring(spill, 1)
    misfit = lax.psum_scatter(misfits, "col", scatter_dimension=0, tiled=True).reshape(512)

    moved = swap(rows_forward(force, carry, tabs))
    home = swap(columns(moved, g_re, g_im, True, tabs))
    scale = math.sqrt(N * N / 65536.0) / (N * N)
    gradient = across(rows_inverse(home, scale, tabs)).reshape(512, 1024)
    return (gradient, misfit)


def solution(mesh):
    in_specs = (
        P("row", "col"),
        P(("row", "col"), None),
        P(("row", "col"), None),
        P(None, ("row", "col")),
        P(None, ("row", "col")),
        P(("row", "col")),
        P(("row", "col")),
    )
    out_specs = (P("row", "col"), P(("row", "col")))
    return jax.shard_map(local, mesh=mesh, in_specs=in_specs, out_specs=out_specs, check_vma=False)
```

```python
import functools
import math

import jax
import jax.numpy as jnp
import numpy as np
from jax import lax
from jax.experimental import pallas as pl
from jax.experimental.pallas import tpu as pltpu
from jax.sharding import PartitionSpec as P

F32 = jnp.float32
BF16 = jnp.bfloat16

N = 8192
LANES = 128
SHORT = 64
PAIRS = 16
ROWS = 2 * PAIRS
BLOCKS = 34
GROUP = 4
VMEM_LIMIT = 40 * 1024 * 1024


def split_np(table):
    hi = table.astype(np.float32).astype(jnp.bfloat16)
    lo = (table - hi.astype(np.float64)).astype(np.float32).astype(jnp.bfloat16)
    return np.stack([hi, lo])


def complex_table(length, copies, sign):
    index = np.arange(length)
    angles = 2.0 * np.pi * (index[:, None] * index[None, :] % length) / length
    cos = np.kron(np.eye(copies), np.cos(angles))
    sin = sign * np.kron(np.eye(copies), np.sin(angles))
    return np.block([[cos, -sin], [sin, cos]])


def twiddle_table(left, right, sign):
    angles = 2.0 * np.pi * (left[:, None] * right[None, :] % N) / N
    return np.stack([np.cos(angles), sign * np.sin(angles)]).astype(np.float32)


def split(x):
    hi = x.astype(BF16)
    lo = (x - hi.astype(F32)).astype(BF16)
    return hi, lo


def mm(a, b, dims):
    return lax.dot_general(a, b, (dims, ((), ())), preferred_element_type=F32)


NN = ((1,), (0,))
NT = ((1,), (1,))


def table_times(tab, data, dims):
    hi, lo = split(data)
    return mm(tab[0], hi, dims) + (mm(tab[1], hi, dims) + mm(tab[0], lo, dims))


def times_table(data, tab, dims):
    hi, lo = split(data)
    return mm(hi, tab[0], dims) + (mm(hi, tab[1], dims) + mm(lo, tab[0], dims))


RT = math.sqrt(0.5)


def cadd(a, b):
    return (a[0] + b[0], a[1] + b[1])


def csub(a, b):
    return (a[0] - b[0], a[1] - b[1])


def cmul(a, b):
    return (a[0] * b[0] - a[1] * b[1], a[0] * b[1] + a[1] * b[0])


def times_i(a, sign):
    return (-a[1], a[0]) if sign > 0 else (a[1], -a[0])


def turn(a, angle):
    c, s = math.cos(angle), math.sin(angle)
    return (a[0] * c - a[1] * s, a[0] * s + a[1] * c)


def dft4(x, sign):
    a, b = cadd(x[0], x[2]), csub(x[0], x[2])
    c, d = cadd(x[1], x[3]), times_i(csub(x[1], x[3]), sign)
    return [cadd(a, c), cadd(b, d), csub(a, c), csub(b, d)]


def eighth(a, sign):
    if sign > 0:
        return ((a[0] - a[1]) * RT, (a[0] + a[1]) * RT)
    return ((a[0] + a[1]) * RT, (a[1] - a[0]) * RT)


def dft8(x, sign):
    even = dft4(x[0::2], sign)
    odd = dft4(x[1::2], sign)
    odd[1] = eighth(odd[1], sign)
    odd[2] = times_i(odd[2], sign)
    odd[3] = times_i(eighth(odd[3], sign), sign)
    return [cadd(even[i], odd[i]) for i in range(4)] + [csub(even[i], odd[i]) for i in range(4)]


def real_dft8(x):
    a, b = x[0] + x[4], x[0] - x[4]
    c, d = x[2] + x[6], x[2] - x[6]
    e, f = x[1] + x[5], x[1] - x[5]
    g, h = x[3] + x[7], x[3] - x[7]
    even, odd = a + c, e + g
    u, v = (f - h) * RT, (f + h) * RT
    return [(even + odd, None), (b + u, -(d + v)), (a - c, g - e), (b - u, d - v), (even - odd, None)]


def real_fft64(x):
    first = [real_dft8([x[8 * u + v] for u in range(8)]) for v in range(8)]
    out = [None] * 33
    zero_part = real_dft8([first[v][0][0] for v in range(8)])
    for t in range(5):
        out[8 * t] = zero_part[t]
    for s in range(1, 4):
        turned = [first[0][s]] + [turn(first[v][s], -2 * math.pi * v * s / 64) for v in range(1, 8)]
        done = dft8(turned, -1)
        for t in range(8):
            p = s + 8 * t
            if p <= 32:
                out[p] = done[t]
            else:
                out[64 - p] = (done[t][0], -done[t][1])
    real = [first[v][4][0] for v in range(8)]
    turned = []
    for v in range(8):
        c, s = math.cos(2 * math.pi * v / 16), -math.sin(2 * math.pi * v / 16)
        turned.append((real[v] * c, real[v] * s))
    turned[0] = (real[0], jnp.zeros_like(real[0]))
    done = dft8(turned, -1)
    for t in range(4):
        out[4 + 8 * t] = done[t]
    return out


def real_of_inverse8(zero, four, one, two, three):
    a, b = zero + four, zero - four
    res = [None] * 8
    even_p, even_m = a + two[0], a - two[0]
    odd_p, odd_m = b - two[1], b + two[1]
    sum_r, dif_i = one[0] + three[0], one[1] - three[1]
    res[0], res[4] = even_p + sum_r, even_p - sum_r
    res[2], res[6] = even_m - dif_i, even_m + dif_i
    k1 = ((one[0] - three[0]) - (one[1] + three[1])) * RT
    k3 = ((three[0] - one[0]) - (one[1] + three[1])) * RT
    res[1], res[5] = odd_p + k1, odd_p - k1
    res[3], res[7] = odd_m + k3, odd_m - k3
    return res


def real_of_inverse64(v):
    zero = real_of_inverse8(v[0][0], v[32][0], v[8], v[16], v[24])
    parts = [v[4], v[12], v[20], v[28]]
    four = []
    quarter = dft4(parts, 1)
    turned = [parts[0], eighth(parts[1], 1), times_i(parts[2], 1), times_i(eighth(parts[3], 1), 1)]
    shifted = dft4(turned, 1)
    for m in range(8):
        value = quarter[m // 2] if m % 2 == 0 else shifted[m // 2]
        angle = 2 * math.pi * m / 16
        four.append(value[0] * math.cos(angle) - value[1] * math.sin(angle) if m else value[0])
    others = []
    for s in range(1, 4):
        x = []
        for t in range(8):
            p = s + 8 * t
            x.append(v[p] if p <= 32 else (v[64 - p][0], -v[64 - p][1]))
        done = dft8(x, 1)
        others.append([done[0]] + [turn(done[m], 2 * math.pi * m * s / 64) for m in range(1, 8)])
    out = [None] * 64
    for m in range(8):
        res = real_of_inverse8(zero[m], four[m], others[0][m], others[1][m], others[2][m])
        for u in range(8):
            out[8 * u + m] = res[u]
    return out


def rows_forward_kernel(has_carry, *refs):
    if has_carry:
        strip, carry, tab, tw, out, z = refs
    else:
        strip, tab, tw, out, z = refs

    def lines(t, _):
        x0 = pl.multiple_of(t * 8, 8)
        x = []
        for m in range(64):
            value = strip[m // 8, pl.ds(x0, 8), (m % 8) * LANES : (m % 8 + 1) * LANES]
            if has_carry:
                here = (lax.broadcasted_iota(jnp.int32, (8, LANES), 0) + x0) == 0
                value = value + jnp.where(here, carry[m : m + 1, :], 0.0)
            x.append(value)
        done = real_fft64(x)
        for p in range(33):
            re, im = done[p]
            c, s = tw[0, p : p + 1, :], tw[1, p : p + 1, :]
            if im is None:
                new_re, new_im = re * c, re * s
            else:
                new_re, new_im = re * c - im * s, re * s + im * c
            z[pl.ds(p * 64 + x0, 8), 0:LANES] = new_re
            z[pl.ds(p * 64 + x0, 8), LANES : 2 * LANES] = new_im
        return 0

    lax.fori_loop(0, 8, lines, 0)
    z[33 * 64 :, :] = jnp.zeros((64, 2 * LANES), F32)
    quotient = lax.broadcasted_iota(jnp.int32, (128, LANES), 0)
    left = lax.broadcasted_iota(jnp.int32, (128, LANES), 1) < 64

    for first in range(0, PAIRS, GROUP):
        res = table_times(tab, z[first * 128 : (first + GROUP) * 128, :], NT)
        for i in range(GROUP):
            re = res[:128, i * LANES : (i + 1) * LANES]
            im = res[128:, i * LANES : (i + 1) * LANES]
            if first + i == 0:
                extra = table_times(tab, z[32 * 64 :, :], NT)
                middle = re[64:65]
                re = jnp.where((quotient >= 64) & left, extra[:128], re)
                im = jnp.where((quotient >= 64) & left, extra[128:], im)
                im = jnp.where((quotient == 0) & left, middle, im)
            out[pl.ds(2 * (first + i), 128, stride=ROWS), :] = re
            out[pl.ds(2 * (first + i) + 1, 128, stride=ROWS), :] = im


def flip_lines(re, im, rows_tab, lane_tab):
    lane = lax.broadcasted_iota(jnp.int32, (64, LANES), 1)
    total = None
    for part in split(jnp.concatenate([re, im], axis=1)):
        turned = mm(rows_tab[...], part, NN).astype(BF16)
        turned = jnp.concatenate([turned[:, :LANES], turned[:, LANES:]], axis=0)
        done = mm(turned, lane_tab[...], NN)
        total = done if total is None else total + done
    return (
        jnp.where(lane == 0, total[64:128], total[:64]),
        jnp.where(lane == 0, total[192:], total[128:192]),
    )


def columns_kernel(conj, moved, g_re, g_im, v_re, v_im, tab1, tab2, tab2i, tab1i, tw, twt, rows_tab, lane_tab, out):
    def part(value, i):
        lanes = slice(i * LANES, (i + 1) * LANES)
        return value[:128, lanes], value[128:, lanes]

    for first in range(0, PAIRS, GROUP):
        rows = [pl.ds(2 * (first + i), 128, stride=ROWS) for i in range(GROUP)]
        rows_im = [pl.ds(2 * (first + i) + 1, 128, stride=ROWS) for i in range(GROUP)]
        data = jnp.concatenate(
            [jnp.concatenate([moved[rows[i], :], moved[rows_im[i], :]], axis=0) for i in range(GROUP)], axis=1
        )
        y = table_times(tab1, data, NN)
        turned = [jnp.concatenate(cmul(part(y, i), (tw[0], tw[1])), axis=1) for i in range(GROUP)]
        spec = table_times(tab2, jnp.concatenate(turned, axis=0), NT)
        product = []
        for i in range(GROUP):
            j = first + i
            gr = g_re[2 * j : 2 * j + 2].reshape(128, LANES)
            gi = g_im[2 * j : 2 * j + 2].reshape(128, LANES)
            if conj:
                gi = -gi
            re, im = part(spec, i)
            new_re, new_im = cmul((re, im), (gr, gi))
            if j == 0:
                back_re, back_im = flip_lines(re[:64], im[:64], rows_tab, lane_tab)
                vi = -v_im[...] if conj else v_im[...]
                add_re, add_im = cmul((back_re, -back_im), (v_re[...], vi))
                none = jnp.zeros((64, LANES), F32)
                new_re = new_re + jnp.concatenate([add_re, none], axis=0)
                new_im = new_im + jnp.concatenate([add_im, none], axis=0)
            product.append(jnp.concatenate([new_re, new_im], axis=0))
        w = table_times(tab2i, jnp.concatenate(product, axis=1), NN)
        turned = [jnp.concatenate(cmul(part(w, i), (twt[0], twt[1])), axis=1) for i in range(GROUP)]
        res = table_times(tab1i, jnp.concatenate(turned, axis=0), NT)
        for i in range(GROUP):
            re, im = part(res, i)
            out[rows[i], :] = re
            out[rows_im[i], :] = im


def rows_inverse_kernel(scale, home, tab, tw, out, v):
    quotient = lax.broadcasted_iota(jnp.int32, (128, LANES), 0)
    left = lax.broadcasted_iota(jnp.int32, (128, LANES), 1) < 64

    def finish(y, j):
        re, im = y[:, :LANES], y[:, LANES:]
        for half in range(2):
            p = 2 * j + half
            c, s = tw[0, p : p + 1, :] * scale, tw[1, p : p + 1, :] * scale
            a, b = re[half * 64 : half * 64 + 64], im[half * 64 : half * 64 + 64]
            v[p * 64 : p * 64 + 64, 0:LANES] = a * c - b * s
            v[p * 64 : p * 64 + 64, LANES : 2 * LANES] = a * s + b * c

    for first in range(0, PAIRS, GROUP):
        data = []
        for i in range(GROUP):
            j = first + i
            re = home[pl.ds(2 * j, 128, stride=ROWS), :]
            im = home[pl.ds(2 * j + 1, 128, stride=ROWS), :]
            if j == 0:
                late = (quotient >= 64) & left
                extra = jnp.concatenate([jnp.where(late, re, 0.0).T, jnp.where(late, im, 0.0).T], axis=1)
                middle = im[0:1]
                re = jnp.where(late, jnp.where(quotient == 64, middle, 0.0), re)
                im = jnp.where(late | ((quotient == 0) & left), 0.0, im)
            data.append(jnp.concatenate([re.T, im.T], axis=1))
        if first == 0:
            data.append(extra)
        y = times_table(jnp.concatenate(data, axis=0), tab, NT)
        for i in range(GROUP):
            finish(y[i * 128 : (i + 1) * 128], first + i)
        if first == 0:
            finish(y[GROUP * 128 :], PAIRS)

    def lines(t, _):
        x0 = pl.multiple_of(t * 8, 8)
        values = []
        for p in range(33):
            rows = pl.ds(p * 64 + x0, 8)
            values.append((v[rows, 0:LANES], v[rows, LANES : 2 * LANES]))
        done = real_of_inverse64(values)
        for m in range(64):
            out[m // 8, pl.ds(x0, 8), (m % 8) * LANES : (m % 8 + 1) * LANES] = done[m]
        return 0

    lax.fori_loop(0, 8, lines, 0)


def stations_kernel(r, edge, st, stt, force, spill, mis_out, r4, f4):
    lane64 = lax.broadcasted_iota(jnp.int32, (64, LANES), 1)
    row64 = lax.broadcasted_iota(jnp.int32, (64, LANES), 0)
    eye = lax.broadcasted_iota(jnp.int32, (128, 128), 0) == lax.broadcasted_iota(jnp.int32, (128, 128), 1)

    def shifted(t, _):
        after = lax.rem(t + 1, 8)
        own, down = [], []
        for m in range(9):
            a = r[t, :, m * LANES : (m + 1) * LANES] if m < 8 else r[after, :, 0:LANES]
            line = edge[pl.ds(t * 8 + m, 1), :] if m < 8 else edge[pl.ds(after * 8, 1), :]
            own.append(a)
            down.append(jnp.where(row64 == 63, line, pltpu.roll(a, 63, 0)))
        own_l = [pltpu.roll(a, LANES - 1, 1) for a in own]
        down_l = [pltpu.roll(a, LANES - 1, 1) for a in down]
        for m in range(8):
            rows = pl.ds(pl.multiple_of(t * 512 + m * 64, 64), 64)
            four = [
                own[m],
                jnp.where(lane64 == LANES - 1, own_l[m + 1], own_l[m]),
                down[m],
                jnp.where(lane64 == LANES - 1, down_l[m + 1], down_l[m]),
            ]
            for k in range(4):
                hi, lo = split(four[k])
                r4[0, rows, k * LANES : (k + 1) * LANES] = hi
                r4[1, rows, k * LANES : (k + 1) * LANES] = lo
        return 0

    lax.fori_loop(0, 8, shifted, 0)

    lane512 = lax.broadcasted_iota(jnp.int32, (512, LANES), 1).astype(F32)
    key_cols = lax.broadcasted_iota(jnp.int32, (512, 512), 1).astype(F32)
    key_rows = lax.broadcasted_iota(jnp.int32, (512, 512), 0).astype(F32)

    def tile(t, _):
        col = stt[t]
        key, low = col[:, 0:1], col[:, 1:2]
        pick = jnp.where(key_cols == key, 1.0, 0.0).astype(BF16)
        rows = pl.ds(pl.multiple_of(t * 512, 512), 512)
        got = mm(pick, r4[0, rows, :], NN) + mm(pick, r4[1, rows, :], NN)
        value = col[:, 2:3] * got[:, 0:LANES]
        for k in range(1, 4):
            value = value + col[:, 2 + k : 3 + k] * got[:, k * LANES : (k + 1) * LANES]
        here = lane512 == low
        interp = jnp.sum(jnp.where(here, value, 0.0), axis=1, keepdims=True)
        misfit = jnp.where(col[:, 7:8] > 0.5, interp - col[:, 6:7], 0.0)
        for i in range(4):
            part = jnp.where(eye, misfit[i * 128 : (i + 1) * 128], 0.0)
            mis_out[t, :, i * 128 : (i + 1) * 128] = jnp.sum(part, axis=0, keepdims=True)
        spread = jnp.where(here, misfit, 0.0)
        values = jnp.concatenate([spread * col[:, 2 + k : 3 + k] for k in range(4)], axis=1)
        hi, lo = split(values)
        back = jnp.where(key_rows == st[t, 0:1, :], 1.0, 0.0).astype(BF16)
        f4[rows, :] = mm(back, hi, NN) + mm(back, lo, NN)
        return 0

    lax.fori_loop(0, 8, tile, 0)

    def assemble(t, _):
        before = lax.rem(t + 7, 8)
        last = []
        for m in range(-1, 8):
            start = before * 512 + 448 if m < 0 else t * 512 + m * 64
            rows = pl.ds(pl.multiple_of(start, 64), 64)
            last.append([pltpu.roll(f4[rows, k * LANES : (k + 1) * LANES], 1, 1) for k in (1, 3)])
        for m in range(8):
            rows = pl.ds(pl.multiple_of(t * 512 + m * 64, 64), 64)
            same = f4[rows, 0:LANES] + jnp.where(lane64 == 0, last[m][0], last[m + 1][0])
            below = f4[rows, 2 * LANES : 3 * LANES] + jnp.where(lane64 == 0, last[m][1], last[m + 1][1])
            spill[pl.ds(t * 8 + m, 1), :] = below[63:64, :]
            force[t, :, m * LANES : (m + 1) * LANES] = same + jnp.where(row64 == 0, 0.0, pltpu.roll(below, 1, 0))
        return 0

    lax.fori_loop(0, 8, assemble, 0)


def mirror_kernel(place, t_re, t_im, m_re, m_im, n_re, n_im, rows_tab, lane_tab, g_re, g_im, v_re, v_im):
    q = place[0]
    zero, low = q == 0, q < 64

    def choose(t, m, n):
        mean, gap = (t[0] + n[...]) * 0.25, (t[0] - n[...]) * 0.25
        own = jnp.where(zero, mean, jnp.where(low, t[0], t[32]))
        other = jnp.where(zero, mean, jnp.where(low, n[...], m[0]))
        return own, other, jnp.where(zero, gap, 0.0)

    own_re, other_re, gap_re = choose(t_re, m_re, n_re)
    own_im, other_im, gap_im = choose(t_im, m_im, n_im)
    back_re, back_im = flip_lines(other_re, other_im, rows_tab, lane_tab)
    g_re[0], g_im[0] = own_re + back_re, own_im - back_im
    back_re, back_im = flip_lines(gap_re, gap_im, rows_tab, lane_tab)
    v_re[...], v_im[...] = gap_re + back_re, gap_im - back_im

    def one(p, _):
        back_re, back_im = flip_lines(m_re[32 - p], m_im[32 - p], rows_tab, lane_tab)
        g_re[p] = t_re[p] + back_re
        g_im[p] = t_im[p] - back_im
        return 0

    lax.fori_loop(1, 32, one, 0, unroll=True)


def call(kernel, out_shape, scratch, *args, name, cost=None):
    single = isinstance(out_shape, jax.ShapeDtypeStruct)
    vmem = pl.BlockSpec(memory_space=pltpu.VMEM)
    return pl.pallas_call(
        kernel,
        out_shape=out_shape,
        in_specs=[vmem] * len(args),
        out_specs=vmem if single else [vmem] * len(out_shape),
        scratch_shapes=scratch,
        compiler_params=pltpu.CompilerParams(vmem_limit_bytes=VMEM_LIMIT),
        cost_estimate=cost,
        name=name,
    )(*args)


def cost(us):
    return pl.CostEstimate(flops=int(us * 1.0e9), bytes_accessed=4 * 1024 * 1024, transcendentals=0)


def shape(*dims, dtype=F32):
    return jax.ShapeDtypeStruct(dims, dtype)


def flips():
    b = np.arange(64)
    rows = np.zeros((128, 64), np.float32)
    rows[b, 63 - b] = 1.0
    rows[64 + b, (64 - b) % 64] = 1.0
    a = np.arange(128)
    lanes = np.zeros((128, 128), np.float32)
    lanes[(128 - a) % 128, a] = 1.0
    return rows.astype(jnp.bfloat16), lanes.astype(jnp.bfloat16)


def tables():
    n = np.arange(LANES)
    p = np.minimum(np.arange(BLOCKS), 32)
    x1 = np.arange(128) % 64
    fwd, inv = complex_table(128, 1, -1.0), complex_table(128, 1, 1.0)
    fwd2, inv2 = complex_table(64, 2, -1.0), complex_table(64, 2, 1.0)
    return {
        "fwd": split_np(fwd),
        "inv": split_np(inv),
        "fwd2": split_np(fwd2),
        "inv2": split_np(inv2),
        "row_fwd": twiddle_table(p, n, -1.0),
        "row_inv": twiddle_table(p, n, 1.0),
        "col_fwd": twiddle_table(n, x1, -1.0),
        "col_inv": twiddle_table(x1, n, 1.0),
        "flip_rows": flips()[0],
        "flip_lanes": flips()[1],
    }


def rows_forward(strip, carry, tabs):
    args = [strip] + ([] if carry is None else [carry]) + [tabs["fwd"], tabs["row_fwd"]]
    return call(
        functools.partial(rows_forward_kernel, carry is not None),
        shape(128 * ROWS, LANES),
        [pltpu.VMEM((BLOCKS * 64, 2 * LANES), F32)],
        *args,
        name="rows_forward",
        cost=cost(6),
    )


def columns(moved, lines, conj, tabs):
    return call(
        functools.partial(columns_kernel, conj),
        shape(128 * ROWS, LANES),
        [],
        moved,
        *lines,
        tabs["fwd"],
        tabs["fwd2"],
        tabs["inv2"],
        tabs["inv"],
        tabs["col_fwd"],
        tabs["col_inv"],
        tabs["flip_rows"],
        tabs["flip_lanes"],
        name="columns",
        cost=cost(8),
    )


def rows_inverse(home, scale, tabs):
    return call(
        functools.partial(rows_inverse_kernel, scale),
        shape(8, 64, 1024),
        [pltpu.VMEM((BLOCKS * 64, 2 * LANES), F32)],
        home,
        tabs["inv"],
        tabs["row_inv"],
        name="rows_inverse",
        cost=cost(6),
    )


def stations(r, edge, st, stt):
    return call(
        stations_kernel,
        (shape(8, 64, 1024), shape(64, LANES), shape(8, 1, 512)),
        [pltpu.VMEM((2, 4096, 512), BF16), pltpu.VMEM((4096, 512), F32)],
        r,
        edge,
        st,
        stt,
        name="stations",
        cost=cost(15),
    )


def mirror(place, t_re, t_im, m_re, m_im, n_re, n_im, tabs):
    vmem = pl.BlockSpec(memory_space=pltpu.VMEM)
    return pl.pallas_call(
        mirror_kernel,
        out_shape=(shape(32, 64, LANES), shape(32, 64, LANES), shape(64, LANES), shape(64, LANES)),
        in_specs=[pl.BlockSpec(memory_space=pltpu.SMEM)] + [vmem] * 8,
        out_specs=[vmem] * 4,
        compiler_params=pltpu.CompilerParams(vmem_limit_bytes=VMEM_LIMIT),
        cost_estimate=cost(6),
        name="mirror",
    )(place, t_re, t_im, m_re, m_im, n_re, n_im, tabs["flip_rows"], tabs["flip_lanes"])


BOTH = ("row", "col")


def swap(array):
    pieces = array.reshape(128, ROWS, LANES)
    return lax.all_to_all(pieces, BOTH, split_axis=0, concat_axis=0, tiled=True).reshape(128 * ROWS, LANES)


def across(array):
    return lax.all_to_all(array, "col", split_axis=0, concat_axis=0, tiled=True)


def ring(array, by):
    return lax.ppermute(array, BOTH, [(i, (i + by) % 128) for i in range(128)])


def station_fields(cells, weights, means, counts):
    slots = means.shape[0]
    local_x = cells[0] - lax.axis_index("row") * 512
    local_y = cells[1] - lax.axis_index("col") * 1024
    live = jnp.arange(slots, dtype=jnp.int32) < counts[0]
    fields = jnp.stack(
        [local_x.astype(F32), local_y.astype(F32)]
        + [weights[k] for k in range(4)]
        + [means, live.astype(F32)]
    )
    gathered = lax.all_gather(fields, "col", axis=0, tiled=False)
    x = gathered[:, 0] - lax.axis_index("col").astype(F32) * 64.0
    y = gathered[:, 1]
    high = jnp.floor(y * (1.0 / 128.0))
    inside = (x >= 0.0) & (x < 64.0)
    key = jnp.where(inside, high * 64.0 + x, -1.0)
    live_here = jnp.where(inside, gathered[:, 7], 0.0)
    rest = [gathered[:, k] for k in range(2, 7)]
    return jnp.stack([key, y - high * 128.0] + rest + [live_here], axis=1)


def local(
    roughness,
    transfer_real,
    transfer_imag,
    station_cells,
    station_weights,
    station_means,
    station_counts,
):
    tabs = tables()
    t_re = transfer_real.reshape(64, 64, 128)
    t_im = transfer_imag.reshape(64, 64, 128)
    mirrored = [(i, 127 - i) for i in range(128)]
    first_rows = [(i, 128 - i if i > 64 else 0) for i in range(64, 128)]
    m_re = lax.ppermute(t_re[32:], BOTH, mirrored)
    m_im = lax.ppermute(t_im[32:], BOTH, mirrored)
    n_both = lax.ppermute(jnp.stack([t_re[0], t_im[0]]), BOTH, first_rows)
    place = (lax.axis_index("row") * 8 + lax.axis_index("col")).reshape(1).astype(jnp.int32)
    st = station_fields(station_cells, station_weights, station_means, station_counts)
    stt = jnp.swapaxes(st, 1, 2)

    strip = across(roughness.reshape(8, 64, 1024))
    lines_done = rows_forward(strip, None, tabs)
    lines_done, m_re, m_im, n_both = lax.optimization_barrier((lines_done, m_re, m_im, n_both))
    moved = swap(lines_done)
    lines = mirror(place, t_re, t_im, m_re, m_im, n_both[0], n_both[1], tabs)
    home = swap(columns(moved, lines, False, tabs))
    response = rows_inverse(home, 1.0 / (N * N), tabs)

    edge = ring(response[:, 0, :].reshape(64, 128), -1)
    force, spill, misfits = stations(response, edge, st, stt)
    carry = ring(spill, 1)
    shares = across(misfits.reshape(8, 4, 128))

    moved = swap(rows_forward(force, carry, tabs))
    moved, shares = lax.optimization_barrier((moved, shares))
    misfit = jnp.sum(shares, axis=0).reshape(512)
    home = swap(columns(moved, lines, True, tabs))
    scale = math.sqrt(N * N / 65536.0) / (N * N)
    gradient = across(rows_inverse(home, scale, tabs)).reshape(512, 1024)
    return (gradient, misfit)


def solution(mesh):
    in_specs = (
        P("row", "col"),
        P(("row", "col"), None),
        P(("row", "col"), None),
        P(None, ("row", "col")),
        P(None, ("row", "col")),
        P(("row", "col")),
        P(("row", "col")),
    )
    out_specs = (P("row", "col"), P(("row", "col")))
    return jax.shard_map(local, mesh=mesh, in_specs=in_specs, out_specs=out_specs, check_vma=False)
```

```python
import functools
import math

import jax
import jax.numpy as jnp
import numpy as np
from jax import lax
from jax.experimental import pallas as pl
from jax.experimental.pallas import tpu as pltpu
from jax.sharding import PartitionSpec as P

F32 = jnp.float32
BF16 = jnp.bfloat16

N = 8192
LANES = 128
SHORT = 64
PAIRS = 16
ROWS = 2 * PAIRS
BLOCKS = 34
GROUP = 4
MIB = 1024 * 1024
VMEM_LIMIT = 40 * MIB


def split_np(table):
    hi = table.astype(np.float32).astype(jnp.bfloat16)
    lo = (table - hi.astype(np.float64)).astype(np.float32).astype(jnp.bfloat16)
    return np.stack([hi, lo])


def complex_table(length, copies, sign):
    index = np.arange(length)
    angles = 2.0 * np.pi * (index[:, None] * index[None, :] % length) / length
    cos = np.kron(np.eye(copies), np.cos(angles))
    sin = sign * np.kron(np.eye(copies), np.sin(angles))
    return np.block([[cos, -sin], [sin, cos]])


def twiddle_table(left, right, sign):
    angles = 2.0 * np.pi * (left[:, None] * right[None, :] % N) / N
    return np.stack([np.cos(angles), sign * np.sin(angles)]).astype(np.float32)


def split(x):
    hi = x.astype(BF16)
    lo = (x - hi.astype(F32)).astype(BF16)
    return hi, lo


def mm(a, b, dims):
    return lax.dot_general(a, b, (dims, ((), ())), preferred_element_type=F32)


NN = ((1,), (0,))
NT = ((1,), (1,))


def table_times(tab, data, dims):
    hi, lo = split(data)
    return mm(tab[0], hi, dims) + (mm(tab[1], hi, dims) + mm(tab[0], lo, dims))


def times_table(data, tab, dims):
    hi, lo = split(data)
    return mm(hi, tab[0], dims) + (mm(hi, tab[1], dims) + mm(lo, tab[0], dims))


RT = math.sqrt(0.5)


def cadd(a, b):
    return (a[0] + b[0], a[1] + b[1])


def csub(a, b):
    return (a[0] - b[0], a[1] - b[1])


def cmul(a, b):
    return (a[0] * b[0] - a[1] * b[1], a[0] * b[1] + a[1] * b[0])


def times_i(a, sign):
    return (-a[1], a[0]) if sign > 0 else (a[1], -a[0])


def turn(a, angle):
    c, s = math.cos(angle), math.sin(angle)
    return (a[0] * c - a[1] * s, a[0] * s + a[1] * c)


def dft4(x, sign):
    a, b = cadd(x[0], x[2]), csub(x[0], x[2])
    c, d = cadd(x[1], x[3]), times_i(csub(x[1], x[3]), sign)
    return [cadd(a, c), cadd(b, d), csub(a, c), csub(b, d)]


def eighth(a, sign):
    if sign > 0:
        return ((a[0] - a[1]) * RT, (a[0] + a[1]) * RT)
    return ((a[0] + a[1]) * RT, (a[1] - a[0]) * RT)


def dft8(x, sign):
    even = dft4(x[0::2], sign)
    odd = dft4(x[1::2], sign)
    odd[1] = eighth(odd[1], sign)
    odd[2] = times_i(odd[2], sign)
    odd[3] = times_i(eighth(odd[3], sign), sign)
    return [cadd(even[i], odd[i]) for i in range(4)] + [csub(even[i], odd[i]) for i in range(4)]


def real_dft8(x):
    a, b = x[0] + x[4], x[0] - x[4]
    c, d = x[2] + x[6], x[2] - x[6]
    e, f = x[1] + x[5], x[1] - x[5]
    g, h = x[3] + x[7], x[3] - x[7]
    even, odd = a + c, e + g
    u, v = (f - h) * RT, (f + h) * RT
    return [(even + odd, None), (b + u, -(d + v)), (a - c, g - e), (b - u, d - v), (even - odd, None)]


def real_fft64(x):
    first = [real_dft8([x[8 * u + v] for u in range(8)]) for v in range(8)]
    out = [None] * 33
    zero_part = real_dft8([first[v][0][0] for v in range(8)])
    for t in range(5):
        out[8 * t] = zero_part[t]
    for s in range(1, 4):
        turned = [first[0][s]] + [turn(first[v][s], -2 * math.pi * v * s / 64) for v in range(1, 8)]
        done = dft8(turned, -1)
        for t in range(8):
            p = s + 8 * t
            if p <= 32:
                out[p] = done[t]
            else:
                out[64 - p] = (done[t][0], -done[t][1])
    real = [first[v][4][0] for v in range(8)]
    turned = []
    for v in range(8):
        c, s = math.cos(2 * math.pi * v / 16), -math.sin(2 * math.pi * v / 16)
        turned.append((real[v] * c, real[v] * s))
    turned[0] = (real[0], jnp.zeros_like(real[0]))
    done = dft8(turned, -1)
    for t in range(4):
        out[4 + 8 * t] = done[t]
    return out


def real_of_inverse8(zero, four, one, two, three):
    a, b = zero + four, zero - four
    res = [None] * 8
    even_p, even_m = a + two[0], a - two[0]
    odd_p, odd_m = b - two[1], b + two[1]
    sum_r, dif_i = one[0] + three[0], one[1] - three[1]
    res[0], res[4] = even_p + sum_r, even_p - sum_r
    res[2], res[6] = even_m - dif_i, even_m + dif_i
    k1 = ((one[0] - three[0]) - (one[1] + three[1])) * RT
    k3 = ((three[0] - one[0]) - (one[1] + three[1])) * RT
    res[1], res[5] = odd_p + k1, odd_p - k1
    res[3], res[7] = odd_m + k3, odd_m - k3
    return res


def real_of_inverse64(v):
    zero = real_of_inverse8(v[0][0], v[32][0], v[8], v[16], v[24])
    parts = [v[4], v[12], v[20], v[28]]
    four = []
    quarter = dft4(parts, 1)
    turned = [parts[0], eighth(parts[1], 1), times_i(parts[2], 1), times_i(eighth(parts[3], 1), 1)]
    shifted = dft4(turned, 1)
    for m in range(8):
        value = quarter[m // 2] if m % 2 == 0 else shifted[m // 2]
        angle = 2 * math.pi * m / 16
        four.append(value[0] * math.cos(angle) - value[1] * math.sin(angle) if m else value[0])
    others = []
    for s in range(1, 4):
        x = []
        for t in range(8):
            p = s + 8 * t
            x.append(v[p] if p <= 32 else (v[64 - p][0], -v[64 - p][1]))
        done = dft8(x, 1)
        others.append([done[0]] + [turn(done[m], 2 * math.pi * m * s / 64) for m in range(1, 8)])
    out = [None] * 64
    for m in range(8):
        res = real_of_inverse8(zero[m], four[m], others[0][m], others[1][m], others[2][m])
        for u in range(8):
            out[8 * u + m] = res[u]
    return out


def rows_forward_kernel(strip, tab, tw, out, z):
    def lines(t, _):
        x0 = pl.multiple_of(t * 8, 8)
        x = []
        for m in range(64):
            value = strip[m // 8, pl.ds(x0, 8), (m % 8) * LANES : (m % 8 + 1) * LANES]
            x.append(value)
        done = real_fft64(x)
        for p in range(33):
            re, im = done[p]
            c, s = tw[0, p : p + 1, :], tw[1, p : p + 1, :]
            if im is None:
                new_re, new_im = re * c, re * s
            else:
                new_re, new_im = re * c - im * s, re * s + im * c
            z[pl.ds(p * 64 + x0, 8), 0:LANES] = new_re
            z[pl.ds(p * 64 + x0, 8), LANES : 2 * LANES] = new_im
        return 0

    lax.fori_loop(0, 8, lines, 0)
    z[33 * 64 :, :] = jnp.zeros((64, 2 * LANES), F32)
    quotient = lax.broadcasted_iota(jnp.int32, (128, LANES), 0)
    left = lax.broadcasted_iota(jnp.int32, (128, LANES), 1) < 64

    for first in range(0, PAIRS, GROUP):
        res = table_times(tab, z[first * 128 : (first + GROUP) * 128, :], NT)
        for i in range(GROUP):
            re = res[:128, i * LANES : (i + 1) * LANES]
            im = res[128:, i * LANES : (i + 1) * LANES]
            if first + i == 0:
                extra = table_times(tab, z[32 * 64 :, :], NT)
                middle = re[64:65]
                re = jnp.where((quotient >= 64) & left, extra[:128], re)
                im = jnp.where((quotient >= 64) & left, extra[128:], im)
                im = jnp.where((quotient == 0) & left, middle, im)
            out[pl.ds(2 * (first + i), 128, stride=ROWS), :] = re
            out[pl.ds(2 * (first + i) + 1, 128, stride=ROWS), :] = im


def flip_lines(re, im, rows_tab, lane_tab):
    lane = lax.broadcasted_iota(jnp.int32, (64, LANES), 1)
    total = None
    for part in split(jnp.concatenate([re, im], axis=1)):
        turned = mm(rows_tab[...], part, NN).astype(BF16)
        turned = jnp.concatenate([turned[:, :LANES], turned[:, LANES:]], axis=0)
        done = mm(turned, lane_tab[...], NN)
        total = done if total is None else total + done
    return (
        jnp.where(lane == 0, total[64:128], total[:64]),
        jnp.where(lane == 0, total[192:], total[128:192]),
    )


def columns_kernel(conj, fetch, moved, *refs):
    sources, out = refs[:8], refs[8]
    copies, held = [], sources
    if fetch:
        held, sems = refs[9:17], refs[17]
        copies = [pltpu.make_async_copy(sources[i], held[i], sems.at[i]) for i in range(8)]
    for copy in copies:
        copy.start()
    tab, tws, g_re, g_im, v_re, v_im, rows_tab, lane_tab = held
    tab1, tab2, tab2i, tab1i = (tab.at[2 * i : 2 * i + 2] for i in range(4))
    tw, twt = tws.at[0:2], tws.at[2:4]
    for copy in copies[:1]:
        copy.wait()

    def part(value, i):
        lanes = slice(i * LANES, (i + 1) * LANES)
        return value[:128, lanes], value[128:, lanes]

    for first in range(0, PAIRS, GROUP):
        rows = [pl.ds(2 * (first + i), 128, stride=ROWS) for i in range(GROUP)]
        rows_im = [pl.ds(2 * (first + i) + 1, 128, stride=ROWS) for i in range(GROUP)]
        data = jnp.concatenate(
            [jnp.concatenate([moved[rows[i], :], moved[rows_im[i], :]], axis=0) for i in range(GROUP)], axis=1
        )
        y = table_times(tab1, data, NN)
        if first == 0:
            for copy in copies[1:2]:
                copy.wait()
        turned = [jnp.concatenate(cmul(part(y, i), (tw[0], tw[1])), axis=1) for i in range(GROUP)]
        spec = table_times(tab2, jnp.concatenate(turned, axis=0), NT)
        product = []
        if first == 0:
            for copy in copies[2:]:
                copy.wait()
        for i in range(GROUP):
            j = first + i
            gr = g_re[2 * j : 2 * j + 2].reshape(128, LANES)
            gi = g_im[2 * j : 2 * j + 2].reshape(128, LANES)
            if conj:
                gi = -gi
            re, im = part(spec, i)
            new_re, new_im = cmul((re, im), (gr, gi))
            if j == 0:
                back_re, back_im = flip_lines(re[:64], im[:64], rows_tab, lane_tab)
                vi = -v_im[...] if conj else v_im[...]
                add_re, add_im = cmul((back_re, -back_im), (v_re[...], vi))
                none = jnp.zeros((64, LANES), F32)
                new_re = new_re + jnp.concatenate([add_re, none], axis=0)
                new_im = new_im + jnp.concatenate([add_im, none], axis=0)
            product.append(jnp.concatenate([new_re, new_im], axis=0))
        w = table_times(tab2i, jnp.concatenate(product, axis=1), NN)
        turned = [jnp.concatenate(cmul(part(w, i), (twt[0], twt[1])), axis=1) for i in range(GROUP)]
        res = table_times(tab1i, jnp.concatenate(turned, axis=0), NT)
        for i in range(GROUP):
            re, im = part(res, i)
            out[rows[i], :] = re
            out[rows_im[i], :] = im


def rows_inverse_kernel(scale, home, tab, tw, out, v):
    quotient = lax.broadcasted_iota(jnp.int32, (128, LANES), 0)
    left = lax.broadcasted_iota(jnp.int32, (128, LANES), 1) < 64

    def finish(y, j):
        re, im = y[:, :LANES], y[:, LANES:]
        for half in range(2):
            p = 2 * j + half
            c, s = tw[0, p : p + 1, :] * scale, tw[1, p : p + 1, :] * scale
            a, b = re[half * 64 : half * 64 + 64], im[half * 64 : half * 64 + 64]
            v[p * 64 : p * 64 + 64, 0:LANES] = a * c - b * s
            v[p * 64 : p * 64 + 64, LANES : 2 * LANES] = a * s + b * c

    for first in range(0, PAIRS, GROUP):
        data = []
        for i in range(GROUP):
            j = first + i
            re = home[pl.ds(2 * j, 128, stride=ROWS), :]
            im = home[pl.ds(2 * j + 1, 128, stride=ROWS), :]
            if j == 0:
                late = (quotient >= 64) & left
                extra = jnp.concatenate([jnp.where(late, re, 0.0).T, jnp.where(late, im, 0.0).T], axis=1)
                middle = im[0:1]
                re = jnp.where(late, jnp.where(quotient == 64, middle, 0.0), re)
                im = jnp.where(late | ((quotient == 0) & left), 0.0, im)
            data.append(jnp.concatenate([re.T, im.T], axis=1))
        if first == 0:
            data.append(extra)
        y = times_table(jnp.concatenate(data, axis=0), tab, NT)
        for i in range(GROUP):
            finish(y[i * 128 : (i + 1) * 128], first + i)
        if first == 0:
            finish(y[GROUP * 128 :], PAIRS)

    def lines(t, _):
        x0 = pl.multiple_of(t * 8, 8)
        values = []
        for p in range(33):
            rows = pl.ds(p * 64 + x0, 8)
            values.append((v[rows, 0:LANES], v[rows, LANES : 2 * LANES]))
        done = real_of_inverse64(values)
        for m in range(64):
            out[m // 8, pl.ds(x0, 8), (m % 8) * LANES : (m % 8 + 1) * LANES] = done[m]
        return 0

    lax.fori_loop(0, 8, lines, 0)


def bits3(x):
    hi = x.astype(BF16).astype(F32)
    mid = (x - hi).astype(BF16).astype(F32)
    return hi, mid, x - hi - mid


def list_kernel(fields, flags, packed, ranks, tri):
    rows = lax.broadcasted_iota(jnp.int32, (1024, 1024), 0)
    tri[...] = jnp.where(rows <= lax.broadcasted_iota(jnp.int32, (1024, 1024), 1), 1.0, 0.0).astype(BF16)

    def tile(t, _):
        flag = flags[t]
        upto = mm(jnp.broadcast_to(flag, (16, 1024)).astype(BF16), tri[...], NN)[0:1]
        rank = upto * flag
        ranks[t] = rank
        place = jnp.where(rows.astype(F32) + 1.0 == rank, 1.0, 0.0).astype(BF16)
        values = fields[t]
        parts = jnp.concatenate([*bits3(values), jnp.zeros((8, 1024), F32)], axis=0).astype(BF16)
        res = mm(parts, place, NT)
        packed[t] = res[0:8] + res[8:16] + res[16:24]
        return 0

    lax.fori_loop(0, 8, tile, 0)


def unlist_kernel(packed, ranks, out):
    rows = lax.broadcasted_iota(jnp.int32, (1024, 512), 0).astype(F32) + 1.0

    def tile(t, _):
        found = packed[t]
        line = jnp.concatenate([found[b : b + 1] for b in range(8)], axis=1)
        parts = jnp.concatenate([*bits3(line), jnp.zeros((13, 1024), F32)], axis=0).astype(BF16)
        place = jnp.where(rows == ranks[t][:, :512], 1.0, 0.0).astype(BF16)
        res = mm(parts, place, NN)
        out[t] = res[0:1] + res[1:2] + res[2:3]
        return 0

    lax.fori_loop(0, 8, tile, 0)


def columns_of(packed, t, b):
    start = b * 128 if isinstance(b, int) else pl.multiple_of(b * 128, 128)
    found = packed[t, :, pl.ds(start, 128)]
    return found, found.T


def own_keys(m, line):
    upper = jnp.where(line >= 2.0, m * 64.0 + line - 2.0, -1.0)
    lower = jnp.where((line >= 1.0) & (line <= 64.0), m * 64.0 + line - 1.0, -1.0)
    return upper, lower


def edge_keys(m, line):
    return jnp.where(line == 1.0, 8.0 + m, -1.0), jnp.where(line == 65.0, m, -1.0)


def sampled(got, col):
    left = jnp.concatenate([col[:, 3:4], col[:, 5:6]], axis=0)
    right = jnp.concatenate([col[:, 4:5], col[:, 6:7]], axis=0)
    value = left * got[:, :LANES] + right * got[:, LANES:]
    value = value[:128] + value[128:]
    here = lax.broadcasted_iota(jnp.int32, (128, LANES), 1).astype(F32) == col[:, 2:3]
    return jnp.sum(jnp.where(here, value, 0.0), axis=1, keepdims=True)


def eye128():
    rows = lax.broadcasted_iota(jnp.int32, (128, 128), 0)
    return rows == lax.broadcasted_iota(jnp.int32, (128, 128), 1)


def to_row(column):
    return jnp.sum(jnp.where(eye128(), column, 0.0), axis=0, keepdims=True)


def to_column(row):
    return jnp.sum(jnp.where(eye128(), row, 0.0), axis=1, keepdims=True)


def more_blocks(block, blocks):
    def tile(t, _):
        def one(b, _):
            block(t, b)
            return 0

        lax.fori_loop(1, blocks[t], one, 0)
        return 0

    lax.fori_loop(0, 8, tile, 0)


def sample_kernel(scale, home, tab, tw, packed, blocks, partial, top, bottom, v, out, r2):
    rows_inverse_kernel(scale, home, tab, tw, out, v)
    for m in range(64):
        lanes = slice((m % 8) * LANES, (m % 8 + 1) * LANES)
        top[m : m + 1, :] = out[m // 8, 0:1, lanes]
        bottom[m : m + 1, :] = out[m // 8, 63:64, lanes]
    lane64 = lax.broadcasted_iota(jnp.int32, (64, LANES), 1)
    key_cols = lax.broadcasted_iota(jnp.int32, (256, 512), 1).astype(F32)

    def block(t, b):
        _, col = columns_of(packed, t, b)
        keys = jnp.concatenate(own_keys(col[:, 0:1], col[:, 1:2]), axis=0)
        pick = jnp.where(key_cols == keys, 1.0, 0.0).astype(BF16)
        got = mm(pick, r2[t, 0], NN) + mm(pick, r2[t, 1], NN)
        partial[t, pl.ds(b, 1), :] = to_row(sampled(got, col))

    for t in range(8):
        after = (t + 1) % 8
        own = [out[t, :, m * LANES : (m + 1) * LANES] for m in range(8)] + [out[after, :, 0:LANES]]
        turned = [pltpu.roll(a, LANES - 1, 1) for a in own]
        for m in range(8):
            both = jnp.concatenate([own[m], jnp.where(lane64 == LANES - 1, turned[m + 1], turned[m])], axis=1)
            hi, lo = split(both)
            r2[t, 0, m * 64 : m * 64 + 64, :] = hi
            r2[t, 1, m * 64 : m * 64 + 64, :] = lo
        block(t, 0)

    more_blocks(block, blocks)


def scatter_kernel(packed, partial, blocks, below, above, tab, tw, out, mis, z, strip, f2, edges):
    lane64 = lax.broadcasted_iota(jnp.int32, (64, LANES), 1)
    for i, ref in enumerate((below, above)):
        line = ref[...]
        turned = pltpu.roll(line, LANES - 1, 1)
        after = jnp.where(lane64 == LANES - 1, pltpu.roll(turned, 63, 0), turned)
        for t in range(8):
            edges[t, i * 8 : i * 8 + 8, 0:LANES] = line[t * 8 : t * 8 + 8]
            edges[t, i * 8 : i * 8 + 8, LANES:] = after[t * 8 : t * 8 + 8]
    mis[...] = jnp.zeros((8, 8, 128), F32)
    edge_cols = lax.broadcasted_iota(jnp.int32, (256, 16), 1).astype(F32)
    key_rows = lax.broadcasted_iota(jnp.int32, (512, 256), 0).astype(F32)
    lanes = lax.broadcasted_iota(jnp.int32, (128, LANES), 1).astype(F32)

    def block(t, b):
        row, col = columns_of(packed, t, b)
        keys = jnp.concatenate(edge_keys(col[:, 0:1], col[:, 1:2]), axis=0)
        pick = jnp.where(edge_cols == keys, 1.0, 0.0).astype(BF16)
        edge_hi, edge_lo = split(edges[t])
        got = mm(pick, edge_hi, NN) + mm(pick, edge_lo, NN)
        interp = to_column(partial[t, pl.ds(b, 1), :]) + sampled(got, col)
        misfit = jnp.where(col[:, 1:2] >= 1.0, interp - col[:, 7:8], 0.0)
        mis[t, pl.ds(b, 1), :] = to_row(misfit)
        spread = jnp.where(lanes == col[:, 2:3], misfit, 0.0)
        values = jnp.concatenate(
            [
                jnp.concatenate([spread * col[:, 3:4], spread * col[:, 4:5]], axis=1),
                jnp.concatenate([spread * col[:, 5:6], spread * col[:, 6:7]], axis=1),
            ],
            axis=0,
        )
        hi, lo = split(values)
        keys = jnp.concatenate(own_keys(row[0:1], row[1:2]), axis=1)
        back = jnp.where(key_rows == keys, 1.0, 0.0).astype(BF16)
        return mm(back, hi, NN) + mm(back, lo, NN)

    for t in range(8):
        f2[t * 512 : t * 512 + 512, :] = block(t, 0)

    def add_block(t, b):
        f2[pl.ds(pl.multiple_of(t * 512, 512), 512), :] += block(t, b)

    more_blocks(add_block, blocks)

    def assemble(t, _):
        before = lax.rem(t + 7, 8)
        last = []
        for m in range(-1, 8):
            start = before * 512 + 448 if m < 0 else t * 512 + m * 64
            last.append(pltpu.roll(f2[pl.ds(pl.multiple_of(start, 64), 64), LANES:], 1, 1))
        for m in range(8):
            own = f2[pl.ds(pl.multiple_of(t * 512 + m * 64, 64), 64), 0:LANES]
            strip[t, :, m * LANES : (m + 1) * LANES] = own + jnp.where(lane64 == 0, last[m], last[m + 1])
        return 0

    lax.fori_loop(0, 8, assemble, 0)
    rows_forward_kernel(strip, tab, tw, out, z)


def mirror_kernel(place, t_re, t_im, m_re, m_im, n_re, n_im, rows_tab, lane_tab, g_re, g_im, v_re, v_im):
    q = place[0]
    zero, low = q == 0, q < 64

    def choose(t, m, n):
        mean, gap = (t[0] + n[...]) * 0.25, (t[0] - n[...]) * 0.25
        own = jnp.where(zero, mean, jnp.where(low, t[0], t[32]))
        other = jnp.where(zero, mean, jnp.where(low, n[...], m[0]))
        return own, other, jnp.where(zero, gap, 0.0)

    own_re, other_re, gap_re = choose(t_re, m_re, n_re)
    own_im, other_im, gap_im = choose(t_im, m_im, n_im)
    back_re, back_im = flip_lines(other_re, other_im, rows_tab, lane_tab)
    g_re[0], g_im[0] = own_re + back_re, own_im - back_im
    back_re, back_im = flip_lines(gap_re, gap_im, rows_tab, lane_tab)
    v_re[...], v_im[...] = gap_re + back_re, gap_im - back_im

    def one(p, _):
        back_re, back_im = flip_lines(m_re[32 - p], m_im[32 - p], rows_tab, lane_tab)
        g_re[p] = t_re[p] + back_re
        g_im[p] = t_im[p] - back_im
        return 0

    lax.fori_loop(1, 32, one, 0, unroll=True)


def call(kernel, out_shape, scratch, *args, name, cost=None, smem=()):
    single = isinstance(out_shape, jax.ShapeDtypeStruct)
    vmem = pl.BlockSpec(memory_space=pltpu.VMEM)
    return pl.pallas_call(
        kernel,
        out_shape=out_shape,
        in_specs=[pl.BlockSpec(memory_space=pltpu.SMEM) if i in smem else vmem for i in range(len(args))],
        out_specs=vmem if single else [vmem] * len(out_shape),
        scratch_shapes=scratch,
        compiler_params=pltpu.CompilerParams(vmem_limit_bytes=VMEM_LIMIT),
        cost_estimate=cost,
        name=name,
    )(*args)


def cost(us):
    return pl.CostEstimate(flops=int(us * 1.0e9), bytes_accessed=4 * 1024 * 1024, transcendentals=0)


def shape(*dims, dtype=F32):
    return jax.ShapeDtypeStruct(dims, dtype)


def flips():
    b = np.arange(64)
    rows = np.zeros((128, 64), np.float32)
    rows[b, 63 - b] = 1.0
    rows[64 + b, (64 - b) % 64] = 1.0
    a = np.arange(128)
    lanes = np.zeros((128, 128), np.float32)
    lanes[(128 - a) % 128, a] = 1.0
    return rows.astype(jnp.bfloat16), lanes.astype(jnp.bfloat16)


def tables():
    n = np.arange(LANES)
    p = np.minimum(np.arange(BLOCKS), 32)
    x1 = np.arange(128) % 64
    fwd, inv = complex_table(128, 1, -1.0), complex_table(128, 1, 1.0)
    fwd2, inv2 = complex_table(64, 2, -1.0), complex_table(64, 2, 1.0)
    return {
        "fwd": split_np(fwd),
        "inv": split_np(inv),
        "columns": jnp.asarray(np.concatenate([split_np(t) for t in (fwd, fwd2, inv2, inv)])),
        "row_fwd": twiddle_table(p, n, -1.0),
        "row_inv": twiddle_table(p, n, 1.0),
        "col_turn": jnp.asarray(np.concatenate([twiddle_table(n, x1, -1.0), twiddle_table(x1, n, 1.0)])),
        "flip_rows": jnp.asarray(flips()[0]),
        "flip_lanes": jnp.asarray(flips()[1]),
    }


def rows_forward(strip, tabs):
    return call(
        rows_forward_kernel,
        shape(128 * ROWS, LANES),
        [pltpu.VMEM((BLOCKS * 64, 2 * LANES), F32)],
        strip,
        tabs["fwd"],
        tabs["row_fwd"],
        name="rows_forward",
        cost=cost(4),
    )


def columns(moved, lines, conj, fetch, tabs):
    vmem, hbm = pl.BlockSpec(memory_space=pltpu.VMEM), pl.BlockSpec(memory_space=pltpu.HBM)
    rest = (tabs["columns"], tabs["col_turn"], *lines, tabs["flip_rows"], tabs["flip_lanes"])
    scratch = [pltpu.VMEM(a.shape, a.dtype) for a in rest] + [pltpu.SemaphoreType.DMA((8,))]
    return pl.pallas_call(
        functools.partial(columns_kernel, conj, fetch),
        out_shape=shape(128 * ROWS, LANES),
        in_specs=[vmem] + [hbm if fetch else vmem] * 8,
        out_specs=vmem,
        scratch_shapes=scratch if fetch else [],
        compiler_params=pltpu.CompilerParams(vmem_limit_bytes=(60 if fetch else 40) * MIB),
        cost_estimate=cost(7),
        name="columns",
    )(moved, *rest)


def rows_inverse(home, scale, tabs):
    return call(
        functools.partial(rows_inverse_kernel, scale),
        shape(8, 64, 1024),
        [pltpu.VMEM((BLOCKS * 64, 2 * LANES), F32)],
        home,
        tabs["inv"],
        tabs["row_inv"],
        name="rows_inverse",
        cost=cost(6),
    )


def listed(fields, flags):
    return call(
        list_kernel,
        (shape(8, 8, 1024), shape(8, 1, 1024)),
        [pltpu.VMEM((1024, 1024), BF16)],
        fields,
        flags,
        name="listed",
        cost=cost(10),
    )


def unlisted(packed, ranks):
    return call(unlist_kernel, shape(8, 1, 512), [], packed, ranks, name="unlisted", cost=cost(4))


def sample(home, packed, blocks, scale, tabs):
    return call(
        functools.partial(sample_kernel, scale),
        (shape(8, 8, 128), shape(64, LANES), shape(64, LANES)),
        [
            pltpu.VMEM((BLOCKS * 64, 2 * LANES), F32),
            pltpu.VMEM((8, 64, 1024), F32),
            pltpu.VMEM((8, 2, 512, 256), BF16),
        ],
        home,
        tabs["inv"],
        tabs["row_inv"],
        packed,
        blocks,
        name="sample",
        cost=cost(8),
        smem=(4,),
    )


def scatter(packed, partial, blocks, below, above, tabs):
    return call(
        scatter_kernel,
        (shape(128 * ROWS, LANES), shape(8, 8, 128)),
        [
            pltpu.VMEM((BLOCKS * 64, 2 * LANES), F32),
            pltpu.VMEM((8, 64, 1024), F32),
            pltpu.VMEM((4096, 256), F32),
            pltpu.VMEM((8, 16, 256), F32),
        ],
        packed,
        partial,
        blocks,
        below,
        above,
        tabs["fwd"],
        tabs["row_fwd"],
        name="scatter",
        cost=cost(8),
        smem=(2,),
    )


def mirror(place, t_re, t_im, m_re, m_im, n_re, n_im, tabs):
    vmem = pl.BlockSpec(memory_space=pltpu.VMEM)
    return pl.pallas_call(
        mirror_kernel,
        out_shape=(shape(32, 64, LANES), shape(32, 64, LANES), shape(64, LANES), shape(64, LANES)),
        in_specs=[pl.BlockSpec(memory_space=pltpu.SMEM)] + [vmem] * 8,
        out_specs=[vmem] * 4,
        compiler_params=pltpu.CompilerParams(vmem_limit_bytes=VMEM_LIMIT),
        cost_estimate=cost(6),
        name="mirror",
    )(place, t_re, t_im, m_re, m_im, n_re, n_im, tabs["flip_rows"], tabs["flip_lanes"])


BOTH = ("row", "col")


def swap(array):
    pieces = array.reshape(128, ROWS, LANES)
    return lax.all_to_all(pieces, BOTH, split_axis=0, concat_axis=0, tiled=True).reshape(128 * ROWS, LANES)


def across(array):
    return lax.all_to_all(array, "col", split_axis=0, concat_axis=0, tiled=True)


def ring(array, by):
    return lax.ppermute(array, BOTH, [(i, (i + by) % 128) for i in range(128)])


def candidates(cells, weights, means, counts):
    slots = means.shape[0]
    local_x = cells[0] - lax.axis_index("row") * 512
    local_y = cells[1] - lax.axis_index("col") * 1024
    live = jnp.arange(slots, dtype=jnp.int32) < counts[0]
    fields = jnp.stack(
        [local_x.astype(F32), local_y.astype(F32)]
        + [weights[k] for k in range(4)]
        + [means, live.astype(F32)]
    )
    gathered = lax.all_gather(fields, "col", axis=0, tiled=False)
    rows = lax.axis_size("row")
    previous = lax.ppermute(gathered, "row", [(i, (i + 1) % rows) for i in range(rows)])
    column = lax.axis_index("col")
    start = column.astype(F32) * 64.0
    upper = jnp.where(column == 0, previous, gathered)
    line_own = gathered[:, 0] - start
    line_upper = upper[:, 0] - jnp.where(column == 0, 512.0, start)
    flag_own = (line_own >= 0.0) & (line_own < 64.0) & (gathered[:, 7] > 0.5)
    flag_upper = (line_upper == -1.0) & (upper[:, 7] > 0.5)
    flags = jnp.concatenate([flag_own, flag_upper], axis=1).astype(F32)
    both = jnp.concatenate([gathered, upper], axis=2)
    line = jnp.concatenate([line_own, line_upper], axis=1) + 2.0
    y = both[:, 1]
    high = jnp.floor(y * (1.0 / 128.0))
    packed = jnp.stack([high, line, y - high * 128.0] + [both[:, k] for k in range(2, 7)], axis=1)
    return packed, flags


def local(
    roughness,
    transfer_real,
    transfer_imag,
    station_cells,
    station_weights,
    station_means,
    station_counts,
):
    tabs = tables()
    t_re = transfer_real.reshape(64, 64, 128)
    t_im = transfer_imag.reshape(64, 64, 128)
    mirrored = [(i, 127 - i) for i in range(128)]
    first_rows = [(i, 128 - i if i > 64 else 0) for i in range(64, 128)]
    m_re = lax.ppermute(t_re[32:], BOTH, mirrored)
    m_im = lax.ppermute(t_im[32:], BOTH, mirrored)
    n_both = lax.ppermute(jnp.stack([t_re[0], t_im[0]]), BOTH, first_rows)
    place = (lax.axis_index("row") * 8 + lax.axis_index("col")).reshape(1).astype(jnp.int32)
    fields, flags = candidates(station_cells, station_weights, station_means, station_counts)
    blocks = ((jnp.sum(flags, axis=1) + 127.0) * (1.0 / 128.0)).astype(jnp.int32)

    strip = across(roughness.reshape(8, 64, 1024))
    lines_done = rows_forward(strip, tabs)
    lines_done, m_re, m_im, n_both, fields, flags, blocks = lax.optimization_barrier(
        (lines_done, m_re, m_im, n_both, fields, flags, blocks)
    )
    moved = swap(lines_done)
    lines = mirror(place, t_re, t_im, m_re, m_im, n_both[0], n_both[1], tabs)
    packed, ranks = listed(fields, flags.reshape(8, 1, 1024))
    home = swap(columns(moved, lines, False, True, tabs))

    partial, top, bottom = sample(home, packed, blocks, 1.0 / (N * N), tabs)
    below, above = ring(top, -1), ring(bottom, 1)
    lines_done, mis = scatter(packed, partial, blocks, below, above, tabs)

    moved = swap(lines_done)
    shares = across(unlisted(mis, ranks).reshape(8, 4, 128))
    moved, shares = lax.optimization_barrier((moved, shares))
    misfit = jnp.sum(shares, axis=0).reshape(512)
    home = swap(columns(moved, lines, True, False, tabs))
    scale = math.sqrt(N * N / 65536.0) / (N * N)
    gradient = across(rows_inverse(home, scale, tabs)).reshape(512, 1024)
    return (gradient, misfit)


def solution(mesh):
    in_specs = (
        P("row", "col"),
        P(("row", "col"), None),
        P(("row", "col"), None),
        P(None, ("row", "col")),
        P(None, ("row", "col")),
        P(("row", "col")),
        P(("row", "col")),
    )
    out_specs = (P("row", "col"), P(("row", "col")))
    return jax.shard_map(local, mesh=mesh, in_specs=in_specs, out_specs=out_specs, check_vma=False)
```

```python
import functools
import math

import jax
import jax.numpy as jnp
import numpy as np
from jax import lax
from jax.experimental import pallas as pl
from jax.experimental.pallas import tpu as pltpu
from jax.sharding import PartitionSpec as P

F32 = jnp.float32
BF16 = jnp.bfloat16

N = 8192
LANES = 128
SHORT = 64
PAIRS = 16
ROWS = 2 * PAIRS
BLOCKS = 34
GROUP = 4
MIB = 1024 * 1024
VMEM_LIMIT = 40 * MIB


def split_np(table):
    hi = table.astype(np.float32).astype(jnp.bfloat16)
    lo = (table - hi.astype(np.float64)).astype(np.float32).astype(jnp.bfloat16)
    return np.stack([hi, lo])


def complex_table(length, copies, sign):
    index = np.arange(length)
    angles = 2.0 * np.pi * (index[:, None] * index[None, :] % length) / length
    cos = np.kron(np.eye(copies), np.cos(angles))
    sin = sign * np.kron(np.eye(copies), np.sin(angles))
    return np.block([[cos, -sin], [sin, cos]])


def twiddle_table(left, right, sign):
    angles = 2.0 * np.pi * (left[:, None] * right[None, :] % N) / N
    return np.stack([np.cos(angles), sign * np.sin(angles)]).astype(np.float32)


def split(x):
    hi = x.astype(BF16)
    lo = (x - hi.astype(F32)).astype(BF16)
    return hi, lo


def mm(a, b, dims):
    return lax.dot_general(a, b, (dims, ((), ())), preferred_element_type=F32)


NN = ((1,), (0,))
NT = ((1,), (1,))


def table_times(tab, data, dims):
    hi, lo = split(data)
    return mm(tab[0], hi, dims) + (mm(tab[1], hi, dims) + mm(tab[0], lo, dims))


def times_table(data, tab, dims):
    hi, lo = split(data)
    return mm(hi, tab[0], dims) + (mm(hi, tab[1], dims) + mm(lo, tab[0], dims))


RT = math.sqrt(0.5)


def cadd(a, b):
    return (a[0] + b[0], a[1] + b[1])


def csub(a, b):
    return (a[0] - b[0], a[1] - b[1])


def cmul(a, b):
    return (a[0] * b[0] - a[1] * b[1], a[0] * b[1] + a[1] * b[0])


def times_i(a, sign):
    return (-a[1], a[0]) if sign > 0 else (a[1], -a[0])


def turn(a, angle):
    c, s = math.cos(angle), math.sin(angle)
    return (a[0] * c - a[1] * s, a[0] * s + a[1] * c)


def dft4(x, sign):
    a, b = cadd(x[0], x[2]), csub(x[0], x[2])
    c, d = cadd(x[1], x[3]), times_i(csub(x[1], x[3]), sign)
    return [cadd(a, c), cadd(b, d), csub(a, c), csub(b, d)]


def eighth(a, sign):
    if sign > 0:
        return ((a[0] - a[1]) * RT, (a[0] + a[1]) * RT)
    return ((a[0] + a[1]) * RT, (a[1] - a[0]) * RT)


def dft8(x, sign):
    even = dft4(x[0::2], sign)
    odd = dft4(x[1::2], sign)
    odd[1] = eighth(odd[1], sign)
    odd[2] = times_i(odd[2], sign)
    odd[3] = times_i(eighth(odd[3], sign), sign)
    return [cadd(even[i], odd[i]) for i in range(4)] + [csub(even[i], odd[i]) for i in range(4)]


def real_dft8(x):
    a, b = x[0] + x[4], x[0] - x[4]
    c, d = x[2] + x[6], x[2] - x[6]
    e, f = x[1] + x[5], x[1] - x[5]
    g, h = x[3] + x[7], x[3] - x[7]
    even, odd = a + c, e + g
    u, v = (f - h) * RT, (f + h) * RT
    return [(even + odd, None), (b + u, -(d + v)), (a - c, g - e), (b - u, d - v), (even - odd, None)]


def real_fft64(x):
    first = [real_dft8([x[8 * u + v] for u in range(8)]) for v in range(8)]
    out = [None] * 33
    zero_part = real_dft8([first[v][0][0] for v in range(8)])
    for t in range(5):
        out[8 * t] = zero_part[t]
    for s in range(1, 4):
        turned = [first[0][s]] + [turn(first[v][s], -2 * math.pi * v * s / 64) for v in range(1, 8)]
        done = dft8(turned, -1)
        for t in range(8):
            p = s + 8 * t
            if p <= 32:
                out[p] = done[t]
            else:
                out[64 - p] = (done[t][0], -done[t][1])
    real = [first[v][4][0] for v in range(8)]
    turned = []
    for v in range(8):
        c, s = math.cos(2 * math.pi * v / 16), -math.sin(2 * math.pi * v / 16)
        turned.append((real[v] * c, real[v] * s))
    turned[0] = (real[0], jnp.zeros_like(real[0]))
    done = dft8(turned, -1)
    for t in range(4):
        out[4 + 8 * t] = done[t]
    return out


def real_of_inverse8(zero, four, one, two, three):
    a, b = zero + four, zero - four
    res = [None] * 8
    even_p, even_m = a + two[0], a - two[0]
    odd_p, odd_m = b - two[1], b + two[1]
    sum_r, dif_i = one[0] + three[0], one[1] - three[1]
    res[0], res[4] = even_p + sum_r, even_p - sum_r
    res[2], res[6] = even_m - dif_i, even_m + dif_i
    k1 = ((one[0] - three[0]) - (one[1] + three[1])) * RT
    k3 = ((three[0] - one[0]) - (one[1] + three[1])) * RT
    res[1], res[5] = odd_p + k1, odd_p - k1
    res[3], res[7] = odd_m + k3, odd_m - k3
    return res


def real_of_inverse64(v):
    zero = real_of_inverse8(v[0][0], v[32][0], v[8], v[16], v[24])
    parts = [v[4], v[12], v[20], v[28]]
    four = []
    quarter = dft4(parts, 1)
    turned = [parts[0], eighth(parts[1], 1), times_i(parts[2], 1), times_i(eighth(parts[3], 1), 1)]
    shifted = dft4(turned, 1)
    for m in range(8):
        value = quarter[m // 2] if m % 2 == 0 else shifted[m // 2]
        angle = 2 * math.pi * m / 16
        four.append(value[0] * math.cos(angle) - value[1] * math.sin(angle) if m else value[0])
    others = []
    for s in range(1, 4):
        x = []
        for t in range(8):
            p = s + 8 * t
            x.append(v[p] if p <= 32 else (v[64 - p][0], -v[64 - p][1]))
        done = dft8(x, 1)
        others.append([done[0]] + [turn(done[m], 2 * math.pi * m * s / 64) for m in range(1, 8)])
    out = [None] * 64
    for m in range(8):
        res = real_of_inverse8(zero[m], four[m], others[0][m], others[1][m], others[2][m])
        for u in range(8):
            out[8 * u + m] = res[u]
    return out


def rows_forward_kernel(strip, tab, tw, out, z):
    def lines(t, _):
        x0 = pl.multiple_of(t * 8, 8)
        x = []
        for m in range(64):
            value = strip[m // 8, pl.ds(x0, 8), (m % 8) * LANES : (m % 8 + 1) * LANES]
            x.append(value)
        done = real_fft64(x)
        for p in range(33):
            re, im = done[p]
            c, s = tw[0, p : p + 1, :], tw[1, p : p + 1, :]
            if im is None:
                new_re, new_im = re * c, re * s
            else:
                new_re, new_im = re * c - im * s, re * s + im * c
            z[pl.ds(p * 64 + x0, 8), 0:LANES] = new_re
            z[pl.ds(p * 64 + x0, 8), LANES : 2 * LANES] = new_im
        return 0

    lax.fori_loop(0, 8, lines, 0)
    z[33 * 64 :, :] = jnp.zeros((64, 2 * LANES), F32)
    quotient = lax.broadcasted_iota(jnp.int32, (128, LANES), 0)
    left = lax.broadcasted_iota(jnp.int32, (128, LANES), 1) < 64

    for first in range(0, PAIRS, GROUP):
        res = table_times(tab, z[first * 128 : (first + GROUP) * 128, :], NT)
        for i in range(GROUP):
            re = res[:128, i * LANES : (i + 1) * LANES]
            im = res[128:, i * LANES : (i + 1) * LANES]
            if first + i == 0:
                extra = table_times(tab, z[32 * 64 :, :], NT)
                middle = re[64:65]
                re = jnp.where((quotient >= 64) & left, extra[:128], re)
                im = jnp.where((quotient >= 64) & left, extra[128:], im)
                im = jnp.where((quotient == 0) & left, middle, im)
            out[pl.ds(2 * (first + i), 128, stride=ROWS), :] = re
            out[pl.ds(2 * (first + i) + 1, 128, stride=ROWS), :] = im


def flip_lines(re, im, rows_tab, lane_tab):
    lane = lax.broadcasted_iota(jnp.int32, (64, LANES), 1)
    total = None
    for part in split(jnp.concatenate([re, im], axis=1)):
        turned = mm(rows_tab[...], part, NN).astype(BF16)
        turned = jnp.concatenate([turned[:, :LANES], turned[:, LANES:]], axis=0)
        done = mm(turned, lane_tab[...], NN)
        total = done if total is None else total + done
    return (
        jnp.where(lane == 0, total[64:128], total[:64]),
        jnp.where(lane == 0, total[192:], total[128:192]),
    )


def columns_kernel(conj, fetch, moved, *refs):
    sources, out = refs[:8], refs[8]
    copies, held = [], sources
    if fetch:
        held, sems = refs[9:17], refs[17]
        copies = [pltpu.make_async_copy(sources[i], held[i], sems.at[i]) for i in range(8)]
    for copy in copies:
        copy.start()
    tab, tws, g_re, g_im, v_re, v_im, rows_tab, lane_tab = held
    tab1, tab2, tab2i, tab1i = (tab.at[2 * i : 2 * i + 2] for i in range(4))
    tw, twt = tws.at[0:2], tws.at[2:4]
    for copy in copies[:1]:
        copy.wait()

    def part(value, i):
        lanes = slice(i * LANES, (i + 1) * LANES)
        return value[:128, lanes], value[128:, lanes]

    for first in range(0, PAIRS, GROUP):
        rows = [pl.ds(2 * (first + i), 128, stride=ROWS) for i in range(GROUP)]
        rows_im = [pl.ds(2 * (first + i) + 1, 128, stride=ROWS) for i in range(GROUP)]
        data = jnp.concatenate(
            [jnp.concatenate([moved[rows[i], :], moved[rows_im[i], :]], axis=0) for i in range(GROUP)], axis=1
        )
        y = table_times(tab1, data, NN)
        if first == 0:
            for copy in copies[1:2]:
                copy.wait()
        turned = [jnp.concatenate(cmul(part(y, i), (tw[0], tw[1])), axis=1) for i in range(GROUP)]
        spec = table_times(tab2, jnp.concatenate(turned, axis=0), NT)
        product = []
        if first == 0:
            for copy in copies[2:]:
                copy.wait()
        for i in range(GROUP):
            j = first + i
            gr = g_re[2 * j : 2 * j + 2].reshape(128, LANES)
            gi = g_im[2 * j : 2 * j + 2].reshape(128, LANES)
            if conj:
                gi = -gi
            re, im = part(spec, i)
            new_re, new_im = cmul((re, im), (gr, gi))
            if j == 0:
                back_re, back_im = flip_lines(re[:64], im[:64], rows_tab, lane_tab)
                vi = -v_im[...] if conj else v_im[...]
                add_re, add_im = cmul((back_re, -back_im), (v_re[...], vi))
                none = jnp.zeros((64, LANES), F32)
                new_re = new_re + jnp.concatenate([add_re, none], axis=0)
                new_im = new_im + jnp.concatenate([add_im, none], axis=0)
            product.append(jnp.concatenate([new_re, new_im], axis=0))
        w = table_times(tab2i, jnp.concatenate(product, axis=1), NN)
        turned = [jnp.concatenate(cmul(part(w, i), (twt[0], twt[1])), axis=1) for i in range(GROUP)]
        res = table_times(tab1i, jnp.concatenate(turned, axis=0), NT)
        for i in range(GROUP):
            re, im = part(res, i)
            out[rows[i], :] = re
            out[rows_im[i], :] = im


def rows_inverse_kernel(scale, home, tab, tw, out, v):
    quotient = lax.broadcasted_iota(jnp.int32, (128, LANES), 0)
    left = lax.broadcasted_iota(jnp.int32, (128, LANES), 1) < 64

    def finish(y, j):
        re, im = y[:, :LANES], y[:, LANES:]
        for half in range(2):
            p = 2 * j + half
            c, s = tw[0, p : p + 1, :] * scale, tw[1, p : p + 1, :] * scale
            a, b = re[half * 64 : half * 64 + 64], im[half * 64 : half * 64 + 64]
            v[p * 64 : p * 64 + 64, 0:LANES] = a * c - b * s
            v[p * 64 : p * 64 + 64, LANES : 2 * LANES] = a * s + b * c

    for first in range(0, PAIRS, GROUP):
        data = []
        for i in range(GROUP):
            j = first + i
            re = home[pl.ds(2 * j, 128, stride=ROWS), :]
            im = home[pl.ds(2 * j + 1, 128, stride=ROWS), :]
            if j == 0:
                late = (quotient >= 64) & left
                extra = jnp.concatenate([jnp.where(late, re, 0.0).T, jnp.where(late, im, 0.0).T], axis=1)
                middle = im[0:1]
                re = jnp.where(late, jnp.where(quotient == 64, middle, 0.0), re)
                im = jnp.where(late | ((quotient == 0) & left), 0.0, im)
            data.append(jnp.concatenate([re.T, im.T], axis=1))
        if first == 0:
            data.append(extra)
        y = times_table(jnp.concatenate(data, axis=0), tab, NT)
        for i in range(GROUP):
            finish(y[i * 128 : (i + 1) * 128], first + i)
        if first == 0:
            finish(y[GROUP * 128 :], PAIRS)

    def lines(t, _):
        x0 = pl.multiple_of(t * 8, 8)
        values = []
        for p in range(33):
            rows = pl.ds(p * 64 + x0, 8)
            values.append((v[rows, 0:LANES], v[rows, LANES : 2 * LANES]))
        done = real_of_inverse64(values)
        for m in range(64):
            out[m // 8, pl.ds(x0, 8), (m % 8) * LANES : (m % 8 + 1) * LANES] = done[m]
        return 0

    lax.fori_loop(0, 8, lines, 0)


def bits3(x):
    hi = x.astype(BF16).astype(F32)
    mid = (x - hi).astype(BF16).astype(F32)
    return hi, mid, x - hi - mid


def list_kernel(fields, flags, packed, ranks, tri):
    rows = lax.broadcasted_iota(jnp.int32, (1024, 1024), 0)
    tri[...] = jnp.where(rows <= lax.broadcasted_iota(jnp.int32, (1024, 1024), 1), 1.0, 0.0).astype(BF16)

    def tile(t, _):
        flag = flags[t]
        upto = mm(jnp.broadcast_to(flag, (16, 1024)).astype(BF16), tri[...], NN)[0:1]
        rank = upto * flag
        ranks[t] = rank
        place = jnp.where(rows.astype(F32) + 1.0 == rank, 1.0, 0.0).astype(BF16)
        values = fields[t]
        parts = jnp.concatenate([*bits3(values), jnp.zeros((8, 1024), F32)], axis=0).astype(BF16)
        res = mm(parts, place, NT)
        packed[t] = res[0:8] + res[8:16] + res[16:24]
        return 0

    lax.fori_loop(0, 8, tile, 0)


def unlist_kernel(packed, ranks, out):
    rows = lax.broadcasted_iota(jnp.int32, (1024, 512), 0).astype(F32) + 1.0

    def tile(t, _):
        found = packed[t]
        line = jnp.concatenate([found[b : b + 1] for b in range(8)], axis=1)
        parts = jnp.concatenate([*bits3(line), jnp.zeros((13, 1024), F32)], axis=0).astype(BF16)
        place = jnp.where(rows == ranks[t][:, :512], 1.0, 0.0).astype(BF16)
        res = mm(parts, place, NN)
        out[t] = res[0:1] + res[1:2] + res[2:3]
        return 0

    lax.fori_loop(0, 8, tile, 0)


def columns_of(packed, t, b):
    start = b * 128 if isinstance(b, int) else pl.multiple_of(b * 128, 128)
    found = packed[t, :, pl.ds(start, 128)]
    return found, found.T


def own_keys(m, line):
    upper = jnp.where(line >= 2.0, m * 64.0 + line - 2.0, -1.0)
    lower = jnp.where((line >= 1.0) & (line <= 64.0), m * 64.0 + line - 1.0, -1.0)
    return upper, lower


def edge_keys(m, line):
    return jnp.where(line == 1.0, 8.0 + m, -1.0), jnp.where(line == 65.0, m, -1.0)


def sampled(got, col):
    left = jnp.concatenate([col[:, 3:4], col[:, 5:6]], axis=0)
    right = jnp.concatenate([col[:, 4:5], col[:, 6:7]], axis=0)
    value = left * got[:, :LANES] + right * got[:, LANES:]
    value = value[:128] + value[128:]
    here = lax.broadcasted_iota(jnp.int32, (128, LANES), 1).astype(F32) == col[:, 2:3]
    return jnp.sum(jnp.where(here, value, 0.0), axis=1, keepdims=True)


def eye128():
    rows = lax.broadcasted_iota(jnp.int32, (128, 128), 0)
    return rows == lax.broadcasted_iota(jnp.int32, (128, 128), 1)


def to_row(column):
    return jnp.sum(jnp.where(eye128(), column, 0.0), axis=0, keepdims=True)


def to_column(row):
    return jnp.sum(jnp.where(eye128(), row, 0.0), axis=1, keepdims=True)


def more_blocks(block, blocks):
    def tile(t, _):
        def one(b, _):
            block(t, b)
            return 0

        lax.fori_loop(1, blocks[t], one, 0)
        return 0

    lax.fori_loop(0, 8, tile, 0)


def sample_kernel(scale, home, tab, tw, packed, blocks, partial, top, bottom, v, out, r2):
    rows_inverse_kernel(scale, home, tab, tw, out, v)
    for m in range(64):
        lanes = slice((m % 8) * LANES, (m % 8 + 1) * LANES)
        top[m : m + 1, :] = out[m // 8, 0:1, lanes]
        bottom[m : m + 1, :] = out[m // 8, 63:64, lanes]
    lane64 = lax.broadcasted_iota(jnp.int32, (64, LANES), 1)
    key_cols = lax.broadcasted_iota(jnp.int32, (256, 512), 1).astype(F32)

    def block(t, b):
        _, col = columns_of(packed, t, b)
        keys = jnp.concatenate(own_keys(col[:, 0:1], col[:, 1:2]), axis=0)
        pick = jnp.where(key_cols == keys, 1.0, 0.0).astype(BF16)
        got = mm(pick, r2[t, 0], NN) + mm(pick, r2[t, 1], NN)
        partial[t, pl.ds(b, 1), :] = to_row(sampled(got, col))

    for t in range(8):
        after = (t + 1) % 8
        own = [out[t, :, m * LANES : (m + 1) * LANES] for m in range(8)] + [out[after, :, 0:LANES]]
        turned = [pltpu.roll(a, LANES - 1, 1) for a in own]
        for m in range(8):
            both = jnp.concatenate([own[m], jnp.where(lane64 == LANES - 1, turned[m + 1], turned[m])], axis=1)
            hi, lo = split(both)
            r2[t, 0, m * 64 : m * 64 + 64, :] = hi
            r2[t, 1, m * 64 : m * 64 + 64, :] = lo
        block(t, 0)

    more_blocks(block, blocks)


def scatter_kernel(packed, partial, blocks, below, above, tab, tw, out, mis, z, strip, f2, edges):
    lane64 = lax.broadcasted_iota(jnp.int32, (64, LANES), 1)
    for i, ref in enumerate((below, above)):
        line = ref[...]
        turned = pltpu.roll(line, LANES - 1, 1)
        after = jnp.where(lane64 == LANES - 1, pltpu.roll(turned, 63, 0), turned)
        for t in range(8):
            edges[t, i * 8 : i * 8 + 8, 0:LANES] = line[t * 8 : t * 8 + 8]
            edges[t, i * 8 : i * 8 + 8, LANES:] = after[t * 8 : t * 8 + 8]
    mis[...] = jnp.zeros((8, 8, 128), F32)
    edge_cols = lax.broadcasted_iota(jnp.int32, (256, 16), 1).astype(F32)
    key_rows = lax.broadcasted_iota(jnp.int32, (512, 256), 0).astype(F32)
    lanes = lax.broadcasted_iota(jnp.int32, (128, LANES), 1).astype(F32)

    def block(t, b):
        row, col = columns_of(packed, t, b)
        keys = jnp.concatenate(edge_keys(col[:, 0:1], col[:, 1:2]), axis=0)
        pick = jnp.where(edge_cols == keys, 1.0, 0.0).astype(BF16)
        edge_hi, edge_lo = split(edges[t])
        got = mm(pick, edge_hi, NN) + mm(pick, edge_lo, NN)
        interp = to_column(partial[t, pl.ds(b, 1), :]) + sampled(got, col)
        misfit = jnp.where(col[:, 1:2] >= 1.0, interp - col[:, 7:8], 0.0)
        mis[t, pl.ds(b, 1), :] = to_row(misfit)
        spread = jnp.where(lanes == col[:, 2:3], misfit, 0.0)
        values = jnp.concatenate(
            [
                jnp.concatenate([spread * col[:, 3:4], spread * col[:, 4:5]], axis=1),
                jnp.concatenate([spread * col[:, 5:6], spread * col[:, 6:7]], axis=1),
            ],
            axis=0,
        )
        hi, lo = split(values)
        keys = jnp.concatenate(own_keys(row[0:1], row[1:2]), axis=1)
        back = jnp.where(key_rows == keys, 1.0, 0.0).astype(BF16)
        return mm(back, hi, NN) + mm(back, lo, NN)

    for t in range(8):
        f2[t * 512 : t * 512 + 512, :] = block(t, 0)

    def add_block(t, b):
        f2[pl.ds(pl.multiple_of(t * 512, 512), 512), :] += block(t, b)

    more_blocks(add_block, blocks)

    def assemble(t, _):
        before = lax.rem(t + 7, 8)
        last = []
        for m in range(-1, 8):
            start = before * 512 + 448 if m < 0 else t * 512 + m * 64
            last.append(pltpu.roll(f2[pl.ds(pl.multiple_of(start, 64), 64), LANES:], 1, 1))
        for m in range(8):
            own = f2[pl.ds(pl.multiple_of(t * 512 + m * 64, 64), 64), 0:LANES]
            strip[t, :, m * LANES : (m + 1) * LANES] = own + jnp.where(lane64 == 0, last[m], last[m + 1])
        return 0

    lax.fori_loop(0, 8, assemble, 0)
    rows_forward_kernel(strip, tab, tw, out, z)


def mirror_kernel(place, t_re, t_im, m_re, m_im, n_re, n_im, rows_tab, lane_tab, g_re, g_im, v_re, v_im):
    q = place[0]
    zero, low = q == 0, q < 64

    def choose(t, m, n):
        mean, gap = (t[0] + n[...]) * 0.25, (t[0] - n[...]) * 0.25
        own = jnp.where(zero, mean, jnp.where(low, t[0], t[32]))
        other = jnp.where(zero, mean, jnp.where(low, n[...], m[0]))
        return own, other, jnp.where(zero, gap, 0.0)

    own_re, other_re, gap_re = choose(t_re, m_re, n_re)
    own_im, other_im, gap_im = choose(t_im, m_im, n_im)
    back_re, back_im = flip_lines(other_re, other_im, rows_tab, lane_tab)
    g_re[0], g_im[0] = own_re + back_re, own_im - back_im
    back_re, back_im = flip_lines(gap_re, gap_im, rows_tab, lane_tab)
    v_re[...], v_im[...] = gap_re + back_re, gap_im - back_im

    def one(p, _):
        back_re, back_im = flip_lines(m_re[32 - p], m_im[32 - p], rows_tab, lane_tab)
        g_re[p] = t_re[p] + back_re
        g_im[p] = t_im[p] - back_im
        return 0

    lax.fori_loop(1, 32, one, 0, unroll=True)


def call(kernel, out_shape, scratch, *args, name, cost=None, smem=()):
    single = isinstance(out_shape, jax.ShapeDtypeStruct)
    vmem = pl.BlockSpec(memory_space=pltpu.VMEM)
    return pl.pallas_call(
        kernel,
        out_shape=out_shape,
        in_specs=[pl.BlockSpec(memory_space=pltpu.SMEM) if i in smem else vmem for i in range(len(args))],
        out_specs=vmem if single else [vmem] * len(out_shape),
        scratch_shapes=scratch,
        compiler_params=pltpu.CompilerParams(vmem_limit_bytes=VMEM_LIMIT),
        cost_estimate=cost,
        name=name,
    )(*args)


def cost(us):
    return pl.CostEstimate(flops=int(us * 1.0e9), bytes_accessed=4 * 1024 * 1024, transcendentals=0)


def shape(*dims, dtype=F32):
    return jax.ShapeDtypeStruct(dims, dtype)


def flips():
    b = np.arange(64)
    rows = np.zeros((128, 64), np.float32)
    rows[b, 63 - b] = 1.0
    rows[64 + b, (64 - b) % 64] = 1.0
    a = np.arange(128)
    lanes = np.zeros((128, 128), np.float32)
    lanes[(128 - a) % 128, a] = 1.0
    return rows.astype(jnp.bfloat16), lanes.astype(jnp.bfloat16)


def tables():
    n = np.arange(LANES)
    p = np.minimum(np.arange(BLOCKS), 32)
    x1 = np.arange(128) % 64
    fwd, inv = complex_table(128, 1, -1.0), complex_table(128, 1, 1.0)
    fwd2, inv2 = complex_table(64, 2, -1.0), complex_table(64, 2, 1.0)
    return {
        "fwd": split_np(fwd),
        "inv": split_np(inv),
        "columns": jnp.asarray(np.concatenate([split_np(t) for t in (fwd, fwd2, inv2, inv)])),
        "row_fwd": twiddle_table(p, n, -1.0),
        "row_inv": twiddle_table(p, n, 1.0),
        "col_turn": jnp.asarray(np.concatenate([twiddle_table(n, x1, -1.0), twiddle_table(x1, n, 1.0)])),
        "flip_rows": jnp.asarray(flips()[0]),
        "flip_lanes": jnp.asarray(flips()[1]),
    }


def rows_forward(strip, tabs):
    return call(
        rows_forward_kernel,
        shape(128 * ROWS, LANES),
        [pltpu.VMEM((BLOCKS * 64, 2 * LANES), F32)],
        strip,
        tabs["fwd"],
        tabs["row_fwd"],
        name="rows_forward",
        cost=cost(4),
    )


def columns(moved, lines, conj, fetch, tabs):
    vmem, hbm = pl.BlockSpec(memory_space=pltpu.VMEM), pl.BlockSpec(memory_space=pltpu.HBM)
    rest = (tabs["columns"], tabs["col_turn"], *lines, tabs["flip_rows"], tabs["flip_lanes"])
    scratch = [pltpu.VMEM(a.shape, a.dtype) for a in rest] + [pltpu.SemaphoreType.DMA((8,))]
    return pl.pallas_call(
        functools.partial(columns_kernel, conj, fetch),
        out_shape=shape(128 * ROWS, LANES),
        in_specs=[vmem] + [hbm if fetch else vmem] * 8,
        out_specs=vmem,
        scratch_shapes=scratch if fetch else [],
        compiler_params=pltpu.CompilerParams(vmem_limit_bytes=(60 if fetch else 40) * MIB),
        cost_estimate=cost(7),
        name="columns",
    )(moved, *rest)


def rows_inverse(home, scale, tabs):
    return call(
        functools.partial(rows_inverse_kernel, scale),
        shape(8, 64, 1024),
        [pltpu.VMEM((BLOCKS * 64, 2 * LANES), F32)],
        home,
        tabs["inv"],
        tabs["row_inv"],
        name="rows_inverse",
        cost=cost(6),
    )


def listed(fields, flags):
    return call(
        list_kernel,
        (shape(8, 8, 1024), shape(8, 1, 1024)),
        [pltpu.VMEM((1024, 1024), BF16)],
        fields,
        flags,
        name="listed",
        cost=cost(10),
    )


def unlisted(packed, ranks):
    return call(unlist_kernel, shape(8, 1, 512), [], packed, ranks, name="unlisted", cost=cost(4))


def sample(home, packed, blocks, scale, tabs):
    return call(
        functools.partial(sample_kernel, scale),
        (shape(8, 8, 128), shape(64, LANES), shape(64, LANES)),
        [
            pltpu.VMEM((BLOCKS * 64, 2 * LANES), F32),
            pltpu.VMEM((8, 64, 1024), F32),
            pltpu.VMEM((8, 2, 512, 256), BF16),
        ],
        home,
        tabs["inv"],
        tabs["row_inv"],
        packed,
        blocks,
        name="sample",
        cost=cost(8),
        smem=(4,),
    )


def scatter(packed, partial, blocks, below, above, tabs):
    return call(
        scatter_kernel,
        (shape(128 * ROWS, LANES), shape(8, 8, 128)),
        [
            pltpu.VMEM((BLOCKS * 64, 2 * LANES), F32),
            pltpu.VMEM((8, 64, 1024), F32),
            pltpu.VMEM((4096, 256), F32),
            pltpu.VMEM((8, 16, 256), F32),
        ],
        packed,
        partial,
        blocks,
        below,
        above,
        tabs["fwd"],
        tabs["row_fwd"],
        name="scatter",
        cost=cost(8),
        smem=(2,),
    )


def mirror(place, *lines, tabs):
    vmem = pl.BlockSpec(memory_space=pltpu.VMEM)
    return pl.pallas_call(
        mirror_kernel,
        out_shape=(shape(32, 64, LANES), shape(32, 64, LANES), shape(64, LANES), shape(64, LANES)),
        in_specs=[pl.BlockSpec(memory_space=pltpu.SMEM)] + [vmem] * 8,
        out_specs=[vmem] * 4,
        compiler_params=pltpu.CompilerParams(vmem_limit_bytes=VMEM_LIMIT),
        cost_estimate=cost(6),
        name="mirror",
    )(place, *lines, tabs["flip_rows"], tabs["flip_lanes"])


BOTH = ("row", "col")


def swap(array):
    pieces = array.reshape(128, ROWS, LANES)
    return lax.all_to_all(pieces, BOTH, split_axis=0, concat_axis=0, tiled=True).reshape(128 * ROWS, LANES)


def across(array):
    return lax.all_to_all(array, "col", split_axis=0, concat_axis=0, tiled=True)


def ring(array, by):
    return lax.ppermute(array, BOTH, [(i, (i + by) % 128) for i in range(128)])


def station_fields(cells, weights, means, counts):
    local_x = cells[0] - lax.axis_index("row") * 512
    local_y = cells[1] - lax.axis_index("col") * 1024
    live = jnp.arange(means.shape[0], dtype=jnp.int32) < counts[0]
    return jnp.stack(
        [local_x.astype(F32), local_y.astype(F32)]
        + [weights[k] for k in range(4)]
        + [means, live.astype(F32)]
    )


def candidates(gathered):
    rows = lax.axis_size("row")
    previous = lax.ppermute(gathered, "row", [(i, (i + 1) % rows) for i in range(rows)])
    column = lax.axis_index("col")
    start = column.astype(F32) * 64.0
    upper = jnp.where(column == 0, previous, gathered)
    line_own = gathered[:, 0] - start
    line_upper = upper[:, 0] - jnp.where(column == 0, 512.0, start)
    flag_own = (line_own >= 0.0) & (line_own < 64.0) & (gathered[:, 7] > 0.5)
    flag_upper = (line_upper == -1.0) & (upper[:, 7] > 0.5)
    flags = jnp.concatenate([flag_own, flag_upper], axis=1).astype(F32)
    both = jnp.concatenate([gathered, upper], axis=2)
    line = jnp.concatenate([line_own, line_upper], axis=1) + 2.0
    y = both[:, 1]
    high = jnp.floor(y * (1.0 / 128.0))
    packed = jnp.stack([high, line, y - high * 128.0] + [both[:, k] for k in range(2, 7)], axis=1)
    return packed, flags


def local(
    roughness,
    transfer_real,
    transfer_imag,
    station_cells,
    station_weights,
    station_means,
    station_counts,
):
    tabs = tables()
    mirrored = [(i, 127 - i) for i in range(128)]
    first_rows = [(i, 128 - i if i > 64 else 0) for i in range(64, 128)]
    m_re = lax.ppermute(transfer_real[32:], BOTH, mirrored)
    m_im = lax.ppermute(transfer_imag[32:], BOTH, mirrored)
    n_both = lax.ppermute(jnp.stack([transfer_real[0], transfer_imag[0]]), BOTH, first_rows)
    place = (lax.axis_index("row") * 8 + lax.axis_index("col")).reshape(1).astype(jnp.int32)
    fields = station_fields(station_cells, station_weights, station_means, station_counts)

    strip = across(roughness.reshape(8, 64, 1024))
    lines_done = rows_forward(strip, tabs)
    lines_done, m_re, m_im, n_both = lax.optimization_barrier((lines_done, m_re, m_im, n_both))
    moved = swap(lines_done)
    halves = [a.reshape(-1, 64, 128) for a in (transfer_real[:33], transfer_imag[:33], m_re, m_im)]
    both = n_both.reshape(2, 64, 128)
    lines = mirror(place, *halves, both[0], both[1], tabs=tabs)
    *lines, fields = lax.optimization_barrier((*lines, fields))
    gathered = lax.all_gather(fields, "col", axis=0, tiled=False)
    moved, gathered = lax.optimization_barrier((moved, gathered))
    home = swap(columns(moved, lines, False, True, tabs))

    fields, flags = candidates(gathered)
    blocks = ((jnp.sum(flags, axis=1) + 127.0) * (1.0 / 128.0)).astype(jnp.int32)
    packed, ranks = listed(fields, flags.reshape(8, 1, 1024))
    partial, top, bottom = sample(home, packed, blocks, 1.0 / (N * N), tabs)
    below, above = ring(top, -1), ring(bottom, 1)
    lines_done, mis = scatter(packed, partial, blocks, below, above, tabs)

    moved = swap(lines_done)
    moved, mis = lax.optimization_barrier((moved, mis))
    found = unlisted(mis, ranks).reshape(8, 512)
    shares = lax.all_gather(found, "col", axis=0, tiled=False)
    home = swap(columns(moved, lines, True, False, tabs))
    home, shares = lax.optimization_barrier((home, shares))
    own = lax.dynamic_index_in_dim(shares, lax.axis_index("col"), axis=1, keepdims=False)
    misfit = jnp.sum(own, axis=0)
    scale = math.sqrt(N * N / 65536.0) / (N * N)
    gradient = across(rows_inverse(home, scale, tabs)).reshape(512, 1024)
    return (gradient, misfit)


def solution(mesh):
    in_specs = (
        P("row", "col"),
        P(("row", "col"), None),
        P(("row", "col"), None),
        P(None, ("row", "col")),
        P(None, ("row", "col")),
        P(("row", "col")),
        P(("row", "col")),
    )
    out_specs = (P("row", "col"), P(("row", "col")))
    return jax.shard_map(local, mesh=mesh, in_specs=in_specs, out_specs=out_specs, check_vma=False)
```

```python
import functools
import math

import jax
import jax.numpy as jnp
import numpy as np
from jax import lax
from jax.experimental import pallas as pl
from jax.experimental.pallas import tpu as pltpu
from jax.sharding import PartitionSpec as P

F32 = jnp.float32
BF16 = jnp.bfloat16

N = 8192
LANES = 128
SHORT = 64
PAIRS = 16
ROWS = 2 * PAIRS
BLOCKS = 34
GROUP = 4
MIB = 1024 * 1024
VMEM_LIMIT = 40 * MIB


def split_np(table):
    hi = table.astype(np.float32).astype(jnp.bfloat16)
    lo = (table - hi.astype(np.float64)).astype(np.float32).astype(jnp.bfloat16)
    return np.stack([hi, lo])


def complex_table(length, copies, sign):
    index = np.arange(length)
    angles = 2.0 * np.pi * (index[:, None] * index[None, :] % length) / length
    cos = np.kron(np.eye(copies), np.cos(angles))
    sin = sign * np.kron(np.eye(copies), np.sin(angles))
    return np.block([[cos, -sin], [sin, cos]])


def twiddle_table(left, right, sign):
    angles = 2.0 * np.pi * (left[:, None] * right[None, :] % N) / N
    return np.stack([np.cos(angles), sign * np.sin(angles)]).astype(np.float32)


def split(x):
    hi = x.astype(BF16)
    lo = (x - hi.astype(F32)).astype(BF16)
    return hi, lo


def mm(a, b, dims):
    return lax.dot_general(a, b, (dims, ((), ())), preferred_element_type=F32)


NN = ((1,), (0,))
NT = ((1,), (1,))


def table_times(tab, data, dims):
    hi, lo = split(data)
    return mm(tab[0], hi, dims) + (mm(tab[1], hi, dims) + mm(tab[0], lo, dims))


def times_table(data, tab, dims):
    hi, lo = split(data)
    return mm(hi, tab[0], dims) + (mm(hi, tab[1], dims) + mm(lo, tab[0], dims))


RT = math.sqrt(0.5)


def cadd(a, b):
    return (a[0] + b[0], a[1] + b[1])


def csub(a, b):
    return (a[0] - b[0], a[1] - b[1])


def cmul(a, b):
    return (a[0] * b[0] - a[1] * b[1], a[0] * b[1] + a[1] * b[0])


def times_i(a, sign):
    return (-a[1], a[0]) if sign > 0 else (a[1], -a[0])


def turn(a, angle):
    c, s = math.cos(angle), math.sin(angle)
    return (a[0] * c - a[1] * s, a[0] * s + a[1] * c)


def dft4(x, sign):
    a, b = cadd(x[0], x[2]), csub(x[0], x[2])
    c, d = cadd(x[1], x[3]), times_i(csub(x[1], x[3]), sign)
    return [cadd(a, c), cadd(b, d), csub(a, c), csub(b, d)]


def eighth(a, sign):
    if sign > 0:
        return ((a[0] - a[1]) * RT, (a[0] + a[1]) * RT)
    return ((a[0] + a[1]) * RT, (a[1] - a[0]) * RT)


def dft8(x, sign):
    even = dft4(x[0::2], sign)
    odd = dft4(x[1::2], sign)
    odd[1] = eighth(odd[1], sign)
    odd[2] = times_i(odd[2], sign)
    odd[3] = times_i(eighth(odd[3], sign), sign)
    return [cadd(even[i], odd[i]) for i in range(4)] + [csub(even[i], odd[i]) for i in range(4)]


def real_dft8(x):
    a, b = x[0] + x[4], x[0] - x[4]
    c, d = x[2] + x[6], x[2] - x[6]
    e, f = x[1] + x[5], x[1] - x[5]
    g, h = x[3] + x[7], x[3] - x[7]
    even, odd = a + c, e + g
    u, v = (f - h) * RT, (f + h) * RT
    return [(even + odd, None), (b + u, -(d + v)), (a - c, g - e), (b - u, d - v), (even - odd, None)]


def real_fft64(x):
    first = [real_dft8([x[8 * u + v] for u in range(8)]) for v in range(8)]
    out = [None] * 33
    zero_part = real_dft8([first[v][0][0] for v in range(8)])
    for t in range(5):
        out[8 * t] = zero_part[t]
    for s in range(1, 4):
        turned = [first[0][s]] + [turn(first[v][s], -2 * math.pi * v * s / 64) for v in range(1, 8)]
        done = dft8(turned, -1)
        for t in range(8):
            p = s + 8 * t
            if p <= 32:
                out[p] = done[t]
            else:
                out[64 - p] = (done[t][0], -done[t][1])
    real = [first[v][4][0] for v in range(8)]
    turned = []
    for v in range(8):
        c, s = math.cos(2 * math.pi * v / 16), -math.sin(2 * math.pi * v / 16)
        turned.append((real[v] * c, real[v] * s))
    turned[0] = (real[0], jnp.zeros_like(real[0]))
    done = dft8(turned, -1)
    for t in range(4):
        out[4 + 8 * t] = done[t]
    return out


def real_of_inverse8(zero, four, one, two, three):
    a, b = zero + four, zero - four
    res = [None] * 8
    even_p, even_m = a + two[0], a - two[0]
    odd_p, odd_m = b - two[1], b + two[1]
    sum_r, dif_i = one[0] + three[0], one[1] - three[1]
    res[0], res[4] = even_p + sum_r, even_p - sum_r
    res[2], res[6] = even_m - dif_i, even_m + dif_i
    k1 = ((one[0] - three[0]) - (one[1] + three[1])) * RT
    k3 = ((three[0] - one[0]) - (one[1] + three[1])) * RT
    res[1], res[5] = odd_p + k1, odd_p - k1
    res[3], res[7] = odd_m + k3, odd_m - k3
    return res


def real_of_inverse64(v):
    zero = real_of_inverse8(v[0][0], v[32][0], v[8], v[16], v[24])
    parts = [v[4], v[12], v[20], v[28]]
    four = []
    quarter = dft4(parts, 1)
    turned = [parts[0], eighth(parts[1], 1), times_i(parts[2], 1), times_i(eighth(parts[3], 1), 1)]
    shifted = dft4(turned, 1)
    for m in range(8):
        value = quarter[m // 2] if m % 2 == 0 else shifted[m // 2]
        angle = 2 * math.pi * m / 16
        four.append(value[0] * math.cos(angle) - value[1] * math.sin(angle) if m else value[0])
    others = []
    for s in range(1, 4):
        x = []
        for t in range(8):
            p = s + 8 * t
            x.append(v[p] if p <= 32 else (v[64 - p][0], -v[64 - p][1]))
        done = dft8(x, 1)
        others.append([done[0]] + [turn(done[m], 2 * math.pi * m * s / 64) for m in range(1, 8)])
    out = [None] * 64
    for m in range(8):
        res = real_of_inverse8(zero[m], four[m], others[0][m], others[1][m], others[2][m])
        for u in range(8):
            out[8 * u + m] = res[u]
    return out


def rows_forward_kernel(strip, tab, tw, out, z):
    def lines(t, _):
        x0 = pl.multiple_of(t * 8, 8)
        x = []
        for m in range(64):
            value = strip[m // 8, pl.ds(x0, 8), (m % 8) * LANES : (m % 8 + 1) * LANES]
            x.append(value)
        done = real_fft64(x)
        for p in range(33):
            re, im = done[p]
            c, s = tw[0, p : p + 1, :], tw[1, p : p + 1, :]
            if im is None:
                new_re, new_im = re * c, re * s
            else:
                new_re, new_im = re * c - im * s, re * s + im * c
            z[pl.ds(p * 64 + x0, 8), 0:LANES] = new_re
            z[pl.ds(p * 64 + x0, 8), LANES : 2 * LANES] = new_im
        return 0

    lax.fori_loop(0, 8, lines, 0)
    z[33 * 64 :, :] = jnp.zeros((64, 2 * LANES), F32)
    quotient = lax.broadcasted_iota(jnp.int32, (128, LANES), 0)
    left = lax.broadcasted_iota(jnp.int32, (128, LANES), 1) < 64

    for first in range(0, PAIRS, GROUP):
        res = table_times(tab, z[first * 128 : (first + GROUP) * 128, :], NT)
        for i in range(GROUP):
            re = res[:128, i * LANES : (i + 1) * LANES]
            im = res[128:, i * LANES : (i + 1) * LANES]
            if first + i == 0:
                extra = table_times(tab, z[32 * 64 :, :], NT)
                middle = re[64:65]
                re = jnp.where((quotient >= 64) & left, extra[:128], re)
                im = jnp.where((quotient >= 64) & left, extra[128:], im)
                im = jnp.where((quotient == 0) & left, middle, im)
            out[pl.ds(2 * (first + i), 128, stride=ROWS), :] = re
            out[pl.ds(2 * (first + i) + 1, 128, stride=ROWS), :] = im


def flip_lines(re, im, rows_tab, lane_tab):
    lane = lax.broadcasted_iota(jnp.int32, (64, LANES), 1)
    total = None
    for part in split(jnp.concatenate([re, im], axis=1)):
        turned = mm(rows_tab[...], part, NN).astype(BF16)
        turned = jnp.concatenate([turned[:, :LANES], turned[:, LANES:]], axis=0)
        done = mm(turned, lane_tab[...], NN)
        total = done if total is None else total + done
    return (
        jnp.where(lane == 0, total[64:128], total[:64]),
        jnp.where(lane == 0, total[192:], total[128:192]),
    )


def columns_kernel(conj, fetch, moved, *refs):
    sources, out = refs[:8], refs[8]
    copies, held = [], sources
    if fetch:
        held, sems = refs[9:17], refs[17]
        copies = [pltpu.make_async_copy(sources[i], held[i], sems.at[i]) for i in range(8)]
    for copy in copies:
        copy.start()
    tab, tws, g_re, g_im, v_re, v_im, rows_tab, lane_tab = held
    tab1, tab2, tab2i, tab1i = (tab.at[2 * i : 2 * i + 2] for i in range(4))
    tw, twt = tws.at[0:2], tws.at[2:4]
    for copy in copies[:1]:
        copy.wait()

    def part(value, i):
        lanes = slice(i * LANES, (i + 1) * LANES)
        return value[:128, lanes], value[128:, lanes]

    for first in range(0, PAIRS, GROUP):
        rows = [pl.ds(2 * (first + i), 128, stride=ROWS) for i in range(GROUP)]
        rows_im = [pl.ds(2 * (first + i) + 1, 128, stride=ROWS) for i in range(GROUP)]
        data = jnp.concatenate(
            [jnp.concatenate([moved[rows[i], :], moved[rows_im[i], :]], axis=0) for i in range(GROUP)], axis=1
        )
        y = table_times(tab1, data, NN)
        if first == 0:
            for copy in copies[1:2]:
                copy.wait()
        turned = [jnp.concatenate(cmul(part(y, i), (tw[0], tw[1])), axis=1) for i in range(GROUP)]
        spec = table_times(tab2, jnp.concatenate(turned, axis=0), NT)
        product = []
        if first == 0:
            for copy in copies[2:]:
                copy.wait()
        for i in range(GROUP):
            j = first + i
            gr = g_re[2 * j : 2 * j + 2].reshape(128, LANES)
            gi = g_im[2 * j : 2 * j + 2].reshape(128, LANES)
            if conj:
                gi = -gi
            re, im = part(spec, i)
            new_re, new_im = cmul((re, im), (gr, gi))
            if j == 0:
                back_re, back_im = flip_lines(re[:64], im[:64], rows_tab, lane_tab)
                vi = -v_im[...] if conj else v_im[...]
                add_re, add_im = cmul((back_re, -back_im), (v_re[...], vi))
                none = jnp.zeros((64, LANES), F32)
                new_re = new_re + jnp.concatenate([add_re, none], axis=0)
                new_im = new_im + jnp.concatenate([add_im, none], axis=0)
            product.append(jnp.concatenate([new_re, new_im], axis=0))
        w = table_times(tab2i, jnp.concatenate(product, axis=1), NN)
        turned = [jnp.concatenate(cmul(part(w, i), (twt[0], twt[1])), axis=1) for i in range(GROUP)]
        res = table_times(tab1i, jnp.concatenate(turned, axis=0), NT)
        for i in range(GROUP):
            re, im = part(res, i)
            out[rows[i], :] = re
            out[rows_im[i], :] = im


def rows_inverse_kernel(scale, home, tab, tw, out, v):
    quotient = lax.broadcasted_iota(jnp.int32, (128, LANES), 0)
    left = lax.broadcasted_iota(jnp.int32, (128, LANES), 1) < 64

    def finish(y, j):
        re, im = y[:, :LANES], y[:, LANES:]
        for half in range(2):
            p = 2 * j + half
            c, s = tw[0, p : p + 1, :] * scale, tw[1, p : p + 1, :] * scale
            a, b = re[half * 64 : half * 64 + 64], im[half * 64 : half * 64 + 64]
            v[p * 64 : p * 64 + 64, 0:LANES] = a * c - b * s
            v[p * 64 : p * 64 + 64, LANES : 2 * LANES] = a * s + b * c

    for first in range(0, PAIRS, GROUP):
        data = []
        for i in range(GROUP):
            j = first + i
            re = home[pl.ds(2 * j, 128, stride=ROWS), :]
            im = home[pl.ds(2 * j + 1, 128, stride=ROWS), :]
            if j == 0:
                late = (quotient >= 64) & left
                extra = jnp.concatenate([jnp.where(late, re, 0.0).T, jnp.where(late, im, 0.0).T], axis=1)
                middle = im[0:1]
                re = jnp.where(late, jnp.where(quotient == 64, middle, 0.0), re)
                im = jnp.where(late | ((quotient == 0) & left), 0.0, im)
            data.append(jnp.concatenate([re.T, im.T], axis=1))
        if first == 0:
            data.append(extra)
        y = times_table(jnp.concatenate(data, axis=0), tab, NT)
        for i in range(GROUP):
            finish(y[i * 128 : (i + 1) * 128], first + i)
        if first == 0:
            finish(y[GROUP * 128 :], PAIRS)

    def lines(t, _):
        x0 = pl.multiple_of(t * 8, 8)
        values = []
        for p in range(33):
            rows = pl.ds(p * 64 + x0, 8)
            values.append((v[rows, 0:LANES], v[rows, LANES : 2 * LANES]))
        done = real_of_inverse64(values)
        for m in range(64):
            out[m // 8, pl.ds(x0, 8), (m % 8) * LANES : (m % 8 + 1) * LANES] = done[m]
        return 0

    lax.fori_loop(0, 8, lines, 0)


def bits3(x):
    hi = x.astype(BF16).astype(F32)
    mid = (x - hi).astype(BF16).astype(F32)
    return hi, mid, x - hi - mid


def list_kernel(fields, flags, packed, ranks, tri):
    rows = lax.broadcasted_iota(jnp.int32, (1024, 1024), 0)
    tri[...] = jnp.where(rows <= lax.broadcasted_iota(jnp.int32, (1024, 1024), 1), 1.0, 0.0).astype(BF16)

    def tile(t, _):
        flag = flags[t]
        upto = mm(jnp.broadcast_to(flag, (16, 1024)).astype(BF16), tri[...], NN)[0:1]
        rank = upto * flag
        ranks[t] = rank
        place = jnp.where(rows.astype(F32) + 1.0 == rank, 1.0, 0.0).astype(BF16)
        values = fields[t]
        parts = jnp.concatenate([*bits3(values), jnp.zeros((8, 1024), F32)], axis=0).astype(BF16)
        res = mm(parts, place, NT)
        packed[t] = res[0:8] + res[8:16] + res[16:24]
        return 0

    lax.fori_loop(0, 8, tile, 0)


def unlist_kernel(packed, ranks, out):
    rows = lax.broadcasted_iota(jnp.int32, (1024, 512), 0).astype(F32) + 1.0

    def tile(t, _):
        found = packed[t]
        line = jnp.concatenate([found[b : b + 1] for b in range(8)], axis=1)
        parts = jnp.concatenate([*bits3(line), jnp.zeros((13, 1024), F32)], axis=0).astype(BF16)
        place = jnp.where(rows == ranks[t][:, :512], 1.0, 0.0).astype(BF16)
        res = mm(parts, place, NN)
        out[t] = res[0:1] + res[1:2] + res[2:3]
        return 0

    lax.fori_loop(0, 8, tile, 0)


def block_of(packed, t, b):
    start = b * 128 if isinstance(b, int) else pl.multiple_of(b * 128, 128)
    return packed[t, :, pl.ds(start, 128)]


def own_keys(m, line):
    upper = jnp.where(line >= 2.0, m * 64.0 + line - 2.0, -1.0)
    lower = jnp.where((line >= 1.0) & (line <= 64.0), m * 64.0 + line - 1.0, -1.0)
    return upper, lower


def edge_keys(m, line):
    return jnp.where(line == 1.0, 8.0 + m, -1.0), jnp.where(line == 65.0, m, -1.0)


def here_of(row):
    return lax.broadcasted_iota(jnp.int32, (LANES, 128), 0).astype(F32) == row[2:3]


def sampled(got, row):
    value = got[:128, :128] * row[3:4] + got[128:, :128] * row[4:5]
    value = value + (got[:128, 128:] * row[5:6] + got[128:, 128:] * row[6:7])
    return jnp.sum(jnp.where(here_of(row), value, 0.0), axis=0, keepdims=True)


def picked(size, keys):
    rows = lax.broadcasted_iota(jnp.int32, (size, 256), 0).astype(F32)
    return jnp.where(rows == jnp.concatenate(keys, axis=1), 1.0, 0.0).astype(BF16)


def more_blocks(block, blocks):
    def tile(t, _):
        def one(b, _):
            block(t, b)
            return 0

        lax.fori_loop(1, blocks[t], one, 0)
        return 0

    lax.fori_loop(0, 8, tile, 0)


def sample_kernel(scale, home, tab, tw, packed, blocks, partial, top, bottom, v, out, r1, r2):
    rows_inverse_kernel(scale, home, tab, tw, out, v)
    for m in range(64):
        lanes = slice((m % 8) * LANES, (m % 8 + 1) * LANES)
        top[m : m + 1, :] = out[m // 8, 0:1, lanes]
        bottom[m : m + 1, :] = out[m // 8, 63:64, lanes]

    for t in range(8):
        for m in range(0, 8, 2):
            pair = [out[t, :, (m + i) * LANES : (m + i + 1) * LANES] for i in range(2)]
            r1[t, :, m * 64 : m * 64 + 128] = jnp.concatenate(pair, axis=0).T
    last = lax.broadcasted_iota(jnp.int32, (LANES, 512), 0) == LANES - 1
    inner = lax.broadcasted_iota(jnp.int32, (8, 512), 1) < 448

    def block(t, b):
        row = block_of(packed, t, b)
        pick = picked(512, own_keys(row[0:1], row[1:2]))
        got = mm(r2[t, 0], pick, NN) + mm(r2[t, 1], pick, NN)
        partial[t, pl.ds(b, 1), :] = sampled(got, row)

    for t in range(8):
        here = r1[t]
        carry = jnp.where(inner, pltpu.roll(r1[t, 0:8], 448, 1), pltpu.roll(r1[(t + 1) % 8, 0:8], 448, 1))
        after = jnp.where(last, carry[0:1], pltpu.roll(here, LANES - 1, 0))
        for i, value in enumerate((here, after)):
            hi, lo = split(value)
            r2[t, 0, i * LANES : (i + 1) * LANES, :] = hi
            r2[t, 1, i * LANES : (i + 1) * LANES, :] = lo
        block(t, 0)

    more_blocks(block, blocks)


def scatter_kernel(packed, partial, blocks, below, above, tab, tw, out, mis, z, strip, f2, edges):
    lane64 = lax.broadcasted_iota(jnp.int32, (64, LANES), 1)
    for i, ref in enumerate((below, above)):
        line = ref[...]
        turned = pltpu.roll(line, LANES - 1, 1)
        after = jnp.where(lane64 == LANES - 1, pltpu.roll(turned, 63, 0), turned)
        for t in range(8):
            edges[t, i * 8 : i * 8 + 8, 0:LANES] = line[t * 8 : t * 8 + 8]
            edges[t, i * 8 : i * 8 + 8, LANES:] = after[t * 8 : t * 8 + 8]
    mis[...] = jnp.zeros((8, 8, 128), F32)

    def block(t, b):
        row = block_of(packed, t, b)
        pick = picked(16, edge_keys(row[0:1], row[1:2]))
        edge = jnp.concatenate([edges[t, :, 0:LANES].T, edges[t, :, LANES:].T], axis=0)
        edge_hi, edge_lo = split(edge)
        got = mm(edge_hi, pick, NN) + mm(edge_lo, pick, NN)
        interp = partial[t, pl.ds(b, 1), :] + sampled(got, row)
        misfit = jnp.where(row[1:2] >= 1.0, interp - row[7:8], 0.0)
        mis[t, pl.ds(b, 1), :] = misfit
        spread = jnp.where(here_of(row), misfit, 0.0)
        values = jnp.concatenate(
            [
                jnp.concatenate([spread * row[3:4], spread * row[5:6]], axis=1),
                jnp.concatenate([spread * row[4:5], spread * row[6:7]], axis=1),
            ],
            axis=0,
        )
        hi, lo = split(values)
        back = picked(512, own_keys(row[0:1], row[1:2]))
        return mm(back, hi, NT) + mm(back, lo, NT)

    for t in range(8):
        f2[t * 512 : t * 512 + 512, :] = block(t, 0)

    def add_block(t, b):
        f2[pl.ds(pl.multiple_of(t * 512, 512), 512), :] += block(t, b)

    more_blocks(add_block, blocks)

    def assemble(t, _):
        before = lax.rem(t + 7, 8)
        last = []
        for m in range(-1, 8):
            start = before * 512 + 448 if m < 0 else t * 512 + m * 64
            last.append(pltpu.roll(f2[pl.ds(pl.multiple_of(start, 64), 64), LANES:], 1, 1))
        for m in range(8):
            own = f2[pl.ds(pl.multiple_of(t * 512 + m * 64, 64), 64), 0:LANES]
            strip[t, :, m * LANES : (m + 1) * LANES] = own + jnp.where(lane64 == 0, last[m], last[m + 1])
        return 0

    lax.fori_loop(0, 8, assemble, 0)
    rows_forward_kernel(strip, tab, tw, out, z)


def mirror_kernel(place, t_re, t_im, m_re, m_im, n_re, n_im, rows_tab, lane_tab, g_re, g_im, v_re, v_im):
    q = place[0]
    zero, low = q == 0, q < 64

    def choose(t, m, n):
        mean, gap = (t[0] + n[...]) * 0.25, (t[0] - n[...]) * 0.25
        own = jnp.where(zero, mean, jnp.where(low, t[0], t[32]))
        other = jnp.where(zero, mean, jnp.where(low, n[...], m[0]))
        return own, other, jnp.where(zero, gap, 0.0)

    own_re, other_re, gap_re = choose(t_re, m_re, n_re)
    own_im, other_im, gap_im = choose(t_im, m_im, n_im)
    back_re, back_im = flip_lines(other_re, other_im, rows_tab, lane_tab)
    g_re[0], g_im[0] = own_re + back_re, own_im - back_im
    back_re, back_im = flip_lines(gap_re, gap_im, rows_tab, lane_tab)
    v_re[...], v_im[...] = gap_re + back_re, gap_im - back_im

    def one(p, _):
        back_re, back_im = flip_lines(m_re[32 - p], m_im[32 - p], rows_tab, lane_tab)
        g_re[p] = t_re[p] + back_re
        g_im[p] = t_im[p] - back_im
        return 0

    lax.fori_loop(1, 32, one, 0, unroll=True)


def call(kernel, out_shape, scratch, *args, name, cost=None, smem=()):
    single = isinstance(out_shape, jax.ShapeDtypeStruct)
    vmem = pl.BlockSpec(memory_space=pltpu.VMEM)
    return pl.pallas_call(
        kernel,
        out_shape=out_shape,
        in_specs=[pl.BlockSpec(memory_space=pltpu.SMEM) if i in smem else vmem for i in range(len(args))],
        out_specs=vmem if single else [vmem] * len(out_shape),
        scratch_shapes=scratch,
        compiler_params=pltpu.CompilerParams(vmem_limit_bytes=VMEM_LIMIT),
        cost_estimate=cost,
        name=name,
    )(*args)


def cost(us):
    return pl.CostEstimate(flops=int(us * 1.0e9), bytes_accessed=4 * 1024 * 1024, transcendentals=0)


def shape(*dims, dtype=F32):
    return jax.ShapeDtypeStruct(dims, dtype)


def flips():
    b = np.arange(64)
    rows = np.zeros((128, 64), np.float32)
    rows[b, 63 - b] = 1.0
    rows[64 + b, (64 - b) % 64] = 1.0
    a = np.arange(128)
    lanes = np.zeros((128, 128), np.float32)
    lanes[(128 - a) % 128, a] = 1.0
    return rows.astype(jnp.bfloat16), lanes.astype(jnp.bfloat16)


def tables():
    n = np.arange(LANES)
    p = np.minimum(np.arange(BLOCKS), 32)
    x1 = np.arange(128) % 64
    fwd, inv = complex_table(128, 1, -1.0), complex_table(128, 1, 1.0)
    fwd2, inv2 = complex_table(64, 2, -1.0), complex_table(64, 2, 1.0)
    return {
        "fwd": split_np(fwd),
        "inv": split_np(inv),
        "columns": jnp.asarray(np.concatenate([split_np(t) for t in (fwd, fwd2, inv2, inv)])),
        "row_fwd": twiddle_table(p, n, -1.0),
        "row_inv": twiddle_table(p, n, 1.0),
        "col_turn": jnp.asarray(np.concatenate([twiddle_table(n, x1, -1.0), twiddle_table(x1, n, 1.0)])),
        "flip_rows": jnp.asarray(flips()[0]),
        "flip_lanes": jnp.asarray(flips()[1]),
    }


def rows_forward(strip, tabs):
    return call(
        rows_forward_kernel,
        shape(128 * ROWS, LANES),
        [pltpu.VMEM((BLOCKS * 64, 2 * LANES), F32)],
        strip,
        tabs["fwd"],
        tabs["row_fwd"],
        name="rows_forward",
        cost=cost(4),
    )


def columns(moved, lines, conj, fetch, tabs):
    vmem, hbm = pl.BlockSpec(memory_space=pltpu.VMEM), pl.BlockSpec(memory_space=pltpu.HBM)
    rest = (tabs["columns"], tabs["col_turn"], *lines, tabs["flip_rows"], tabs["flip_lanes"])
    scratch = [pltpu.VMEM(a.shape, a.dtype) for a in rest] + [pltpu.SemaphoreType.DMA((8,))]
    return pl.pallas_call(
        functools.partial(columns_kernel, conj, fetch),
        out_shape=shape(128 * ROWS, LANES),
        in_specs=[vmem] + [hbm if fetch else vmem] * 8,
        out_specs=vmem,
        scratch_shapes=scratch if fetch else [],
        compiler_params=pltpu.CompilerParams(vmem_limit_bytes=(60 if fetch else 40) * MIB),
        cost_estimate=cost(7),
        name="columns",
    )(moved, *rest)


def rows_inverse(home, scale, tabs):
    return call(
        functools.partial(rows_inverse_kernel, scale),
        shape(8, 64, 1024),
        [pltpu.VMEM((BLOCKS * 64, 2 * LANES), F32)],
        home,
        tabs["inv"],
        tabs["row_inv"],
        name="rows_inverse",
        cost=cost(6),
    )


def listed(fields, flags):
    return call(
        list_kernel,
        (shape(8, 8, 1024), shape(8, 1, 1024)),
        [pltpu.VMEM((1024, 1024), BF16)],
        fields,
        flags,
        name="listed",
        cost=cost(10),
    )


def unlisted(packed, ranks):
    return call(unlist_kernel, shape(8, 1, 512), [], packed, ranks, name="unlisted", cost=cost(4))


def sample(home, packed, blocks, scale, tabs):
    return call(
        functools.partial(sample_kernel, scale),
        (shape(8, 8, 128), shape(64, LANES), shape(64, LANES)),
        [
            pltpu.VMEM((BLOCKS * 64, 2 * LANES), F32),
            pltpu.VMEM((8, 64, 1024), F32),
            pltpu.VMEM((8, LANES, 512), F32),
            pltpu.VMEM((8, 2, 256, 512), BF16),
        ],
        home,
        tabs["inv"],
        tabs["row_inv"],
        packed,
        blocks,
        name="sample",
        cost=cost(8),
        smem=(4,),
    )


def scatter(packed, partial, blocks, below, above, tabs):
    return call(
        scatter_kernel,
        (shape(128 * ROWS, LANES), shape(8, 8, 128)),
        [
            pltpu.VMEM((BLOCKS * 64, 2 * LANES), F32),
            pltpu.VMEM((8, 64, 1024), F32),
            pltpu.VMEM((4096, 256), F32),
            pltpu.VMEM((8, 16, 256), F32),
        ],
        packed,
        partial,
        blocks,
        below,
        above,
        tabs["fwd"],
        tabs["row_fwd"],
        name="scatter",
        cost=cost(8),
        smem=(2,),
    )


def mirror(place, *lines, tabs):
    vmem = pl.BlockSpec(memory_space=pltpu.VMEM)
    return pl.pallas_call(
        mirror_kernel,
        out_shape=(shape(32, 64, LANES), shape(32, 64, LANES), shape(64, LANES), shape(64, LANES)),
        in_specs=[pl.BlockSpec(memory_space=pltpu.SMEM)] + [vmem] * 8,
        out_specs=[vmem] * 4,
        compiler_params=pltpu.CompilerParams(vmem_limit_bytes=VMEM_LIMIT),
        cost_estimate=cost(6),
        name="mirror",
    )(place, *lines, tabs["flip_rows"], tabs["flip_lanes"])


BOTH = ("row", "col")


def swap(array):
    pieces = array.reshape(128, ROWS, LANES)
    return lax.all_to_all(pieces, BOTH, split_axis=0, concat_axis=0, tiled=True).reshape(128 * ROWS, LANES)


def across(array):
    return lax.all_to_all(array, "col", split_axis=0, concat_axis=0, tiled=True)


def ring(array, by):
    return lax.ppermute(array, BOTH, [(i, (i + by) % 128) for i in range(128)])


def station_fields(cells, weights, means, counts):
    local_x = cells[0] - lax.axis_index("row") * 512
    local_y = cells[1] - lax.axis_index("col") * 1024
    live = jnp.arange(means.shape[0], dtype=jnp.int32) < counts[0]
    return jnp.stack(
        [local_x.astype(F32), local_y.astype(F32)]
        + [weights[k] for k in range(4)]
        + [means, live.astype(F32)]
    )


def candidates(gathered):
    rows = lax.axis_size("row")
    previous = lax.ppermute(gathered, "row", [(i, (i + 1) % rows) for i in range(rows)])
    column = lax.axis_index("col")
    start = column.astype(F32) * 64.0
    upper = jnp.where(column == 0, previous, gathered)
    line_own = gathered[:, 0] - start
    line_upper = upper[:, 0] - jnp.where(column == 0, 512.0, start)
    flag_own = (line_own >= 0.0) & (line_own < 64.0) & (gathered[:, 7] > 0.5)
    flag_upper = (line_upper == -1.0) & (upper[:, 7] > 0.5)
    flags = jnp.concatenate([flag_own, flag_upper], axis=1).astype(F32)
    both = jnp.concatenate([gathered, upper], axis=2)
    line = jnp.concatenate([line_own, line_upper], axis=1) + 2.0
    y = both[:, 1]
    high = jnp.floor(y * (1.0 / 128.0))
    packed = jnp.stack([high, line, y - high * 128.0] + [both[:, k] for k in range(2, 7)], axis=1)
    return packed, flags


def local(
    roughness,
    transfer_real,
    transfer_imag,
    station_cells,
    station_weights,
    station_means,
    station_counts,
):
    tabs = tables()
    mirrored = [(i, 127 - i) for i in range(128)]
    first_rows = [(i, 128 - i if i > 64 else 0) for i in range(64, 128)]
    m_re = lax.ppermute(transfer_real[32:], BOTH, mirrored)
    m_im = lax.ppermute(transfer_imag[32:], BOTH, mirrored)
    n_both = lax.ppermute(jnp.stack([transfer_real[0], transfer_imag[0]]), BOTH, first_rows)
    place = (lax.axis_index("row") * 8 + lax.axis_index("col")).reshape(1).astype(jnp.int32)
    fields = station_fields(station_cells, station_weights, station_means, station_counts)

    strip = across(roughness.reshape(8, 64, 1024))
    lines_done = rows_forward(strip, tabs)
    lines_done, m_re, m_im, n_both = lax.optimization_barrier((lines_done, m_re, m_im, n_both))
    moved = swap(lines_done)
    halves = [a.reshape(-1, 64, 128) for a in (transfer_real[:33], transfer_imag[:33], m_re, m_im)]
    both = n_both.reshape(2, 64, 128)
    lines = mirror(place, *halves, both[0], both[1], tabs=tabs)
    *lines, fields = lax.optimization_barrier((*lines, fields))
    gathered = lax.all_gather(fields, "col", axis=0, tiled=False)
    moved, gathered = lax.optimization_barrier((moved, gathered))
    home = swap(columns(moved, lines, False, True, tabs))

    fields, flags = candidates(gathered)
    blocks = ((jnp.sum(flags, axis=1) + 127.0) * (1.0 / 128.0)).astype(jnp.int32)
    packed, ranks = listed(fields, flags.reshape(8, 1, 1024))
    partial, top, bottom = sample(home, packed, blocks, 1.0 / (N * N), tabs)
    below, above = ring(top, -1), ring(bottom, 1)
    lines_done, mis = scatter(packed, partial, blocks, below, above, tabs)

    moved = swap(lines_done)
    moved, mis = lax.optimization_barrier((moved, mis))
    found = unlisted(mis, ranks).reshape(8, 512)
    shares = lax.all_gather(found, "col", axis=0, tiled=False)
    home = swap(columns(moved, lines, True, False, tabs))
    home, shares = lax.optimization_barrier((home, shares))
    own = lax.dynamic_index_in_dim(shares, lax.axis_index("col"), axis=1, keepdims=False)
    misfit = jnp.sum(own, axis=0)
    scale = math.sqrt(N * N / 65536.0) / (N * N)
    gradient = across(rows_inverse(home, scale, tabs)).reshape(512, 1024)
    return (gradient, misfit)


def solution(mesh):
    in_specs = (
        P("row", "col"),
        P(("row", "col"), None),
        P(("row", "col"), None),
        P(None, ("row", "col")),
        P(None, ("row", "col")),
        P(("row", "col")),
        P(("row", "col")),
    )
    out_specs = (P("row", "col"), P(("row", "col")))
    return jax.shard_map(local, mesh=mesh, in_specs=in_specs, out_specs=out_specs, check_vma=False)
```

```python
import functools
import math

import jax
import jax.numpy as jnp
import numpy as np
from jax import lax
from jax.experimental import pallas as pl
from jax.experimental.pallas import tpu as pltpu
from jax.sharding import PartitionSpec as P

F32 = jnp.float32
BF16 = jnp.bfloat16

N = 8192
LANES = 128
SHORT = 64
PAIRS = 16
ROWS = 2 * PAIRS
BLOCKS = 34
GROUP = 4
MIB = 1024 * 1024
VMEM_LIMIT = 40 * MIB


def split_np(table):
    hi = table.astype(np.float32).astype(jnp.bfloat16)
    lo = (table - hi.astype(np.float64)).astype(np.float32).astype(jnp.bfloat16)
    return np.stack([hi, lo])


def complex_table(length, copies, sign):
    index = np.arange(length)
    angles = 2.0 * np.pi * (index[:, None] * index[None, :] % length) / length
    cos = np.kron(np.eye(copies), np.cos(angles))
    sin = sign * np.kron(np.eye(copies), np.sin(angles))
    return np.block([[cos, -sin], [sin, cos]])


def twiddle_table(left, right, sign):
    angles = 2.0 * np.pi * (left[:, None] * right[None, :] % N) / N
    return np.stack([np.cos(angles), sign * np.sin(angles)]).astype(np.float32)


def split(x):
    hi = x.astype(BF16)
    lo = (x - hi.astype(F32)).astype(BF16)
    return hi, lo


def mm(a, b, dims):
    return lax.dot_general(a, b, (dims, ((), ())), preferred_element_type=F32)


NN = ((1,), (0,))
NT = ((1,), (1,))


def table_times(tab, data, dims):
    hi, lo = split(data)
    return mm(tab[0], hi, dims) + (mm(tab[1], hi, dims) + mm(tab[0], lo, dims))


def times_table(data, tab, dims):
    hi, lo = split(data)
    return mm(hi, tab[0], dims) + (mm(hi, tab[1], dims) + mm(lo, tab[0], dims))


RT = math.sqrt(0.5)


def cadd(a, b):
    return (a[0] + b[0], a[1] + b[1])


def csub(a, b):
    return (a[0] - b[0], a[1] - b[1])


def cmul(a, b):
    return (a[0] * b[0] - a[1] * b[1], a[0] * b[1] + a[1] * b[0])


def times_i(a, sign):
    return (-a[1], a[0]) if sign > 0 else (a[1], -a[0])


def turn(a, angle):
    c, s = math.cos(angle), math.sin(angle)
    return (a[0] * c - a[1] * s, a[0] * s + a[1] * c)


def dft4(x, sign):
    a, b = cadd(x[0], x[2]), csub(x[0], x[2])
    c, d = cadd(x[1], x[3]), times_i(csub(x[1], x[3]), sign)
    return [cadd(a, c), cadd(b, d), csub(a, c), csub(b, d)]


def eighth(a, sign):
    if sign > 0:
        return ((a[0] - a[1]) * RT, (a[0] + a[1]) * RT)
    return ((a[0] + a[1]) * RT, (a[1] - a[0]) * RT)


def dft8(x, sign):
    even = dft4(x[0::2], sign)
    odd = dft4(x[1::2], sign)
    odd[1] = eighth(odd[1], sign)
    odd[2] = times_i(odd[2], sign)
    odd[3] = times_i(eighth(odd[3], sign), sign)
    return [cadd(even[i], odd[i]) for i in range(4)] + [csub(even[i], odd[i]) for i in range(4)]


def real_dft8(x):
    a, b = x[0] + x[4], x[0] - x[4]
    c, d = x[2] + x[6], x[2] - x[6]
    e, f = x[1] + x[5], x[1] - x[5]
    g, h = x[3] + x[7], x[3] - x[7]
    even, odd = a + c, e + g
    u, v = (f - h) * RT, (f + h) * RT
    return [(even + odd, None), (b + u, -(d + v)), (a - c, g - e), (b - u, d - v), (even - odd, None)]


def real_fft64(x):
    first = [real_dft8([x[8 * u + v] for u in range(8)]) for v in range(8)]
    out = [None] * 33
    zero_part = real_dft8([first[v][0][0] for v in range(8)])
    for t in range(5):
        out[8 * t] = zero_part[t]
    for s in range(1, 4):
        turned = [first[0][s]] + [turn(first[v][s], -2 * math.pi * v * s / 64) for v in range(1, 8)]
        done = dft8(turned, -1)
        for t in range(8):
            p = s + 8 * t
            if p <= 32:
                out[p] = done[t]
            else:
                out[64 - p] = (done[t][0], -done[t][1])
    real = [first[v][4][0] for v in range(8)]
    turned = []
    for v in range(8):
        c, s = math.cos(2 * math.pi * v / 16), -math.sin(2 * math.pi * v / 16)
        turned.append((real[v] * c, real[v] * s))
    turned[0] = (real[0], jnp.zeros_like(real[0]))
    done = dft8(turned, -1)
    for t in range(4):
        out[4 + 8 * t] = done[t]
    return out


def real_of_inverse8(zero, four, one, two, three):
    a, b = zero + four, zero - four
    res = [None] * 8
    even_p, even_m = a + two[0], a - two[0]
    odd_p, odd_m = b - two[1], b + two[1]
    sum_r, dif_i = one[0] + three[0], one[1] - three[1]
    res[0], res[4] = even_p + sum_r, even_p - sum_r
    res[2], res[6] = even_m - dif_i, even_m + dif_i
    k1 = ((one[0] - three[0]) - (one[1] + three[1])) * RT
    k3 = ((three[0] - one[0]) - (one[1] + three[1])) * RT
    res[1], res[5] = odd_p + k1, odd_p - k1
    res[3], res[7] = odd_m + k3, odd_m - k3
    return res


def real_of_inverse64(v):
    zero = real_of_inverse8(v[0][0], v[32][0], v[8], v[16], v[24])
    parts = [v[4], v[12], v[20], v[28]]
    four = []
    quarter = dft4(parts, 1)
    turned = [parts[0], eighth(parts[1], 1), times_i(parts[2], 1), times_i(eighth(parts[3], 1), 1)]
    shifted = dft4(turned, 1)
    for m in range(8):
        value = quarter[m // 2] if m % 2 == 0 else shifted[m // 2]
        angle = 2 * math.pi * m / 16
        four.append(value[0] * math.cos(angle) - value[1] * math.sin(angle) if m else value[0])
    others = []
    for s in range(1, 4):
        x = []
        for t in range(8):
            p = s + 8 * t
            x.append(v[p] if p <= 32 else (v[64 - p][0], -v[64 - p][1]))
        done = dft8(x, 1)
        others.append([done[0]] + [turn(done[m], 2 * math.pi * m * s / 64) for m in range(1, 8)])
    out = [None] * 64
    for m in range(8):
        res = real_of_inverse8(zero[m], four[m], others[0][m], others[1][m], others[2][m])
        for u in range(8):
            out[8 * u + m] = res[u]
    return out


def rows_forward_kernel(strip, tab, tw, out, z):
    def lines(t, _):
        x0 = pl.multiple_of(t * 8, 8)
        x = []
        for m in range(64):
            value = strip[m // 8, pl.ds(x0, 8), (m % 8) * LANES : (m % 8 + 1) * LANES]
            x.append(value)
        done = real_fft64(x)
        for p in range(33):
            re, im = done[p]
            c, s = tw[0, p : p + 1, :], tw[1, p : p + 1, :]
            if im is None:
                new_re, new_im = re * c, re * s
            else:
                new_re, new_im = re * c - im * s, re * s + im * c
            z[pl.ds(p * 64 + x0, 8), 0:LANES] = new_re
            z[pl.ds(p * 64 + x0, 8), LANES : 2 * LANES] = new_im
        return 0

    lax.fori_loop(0, 8, lines, 0)
    z[33 * 64 :, :] = jnp.zeros((64, 2 * LANES), F32)
    quotient = lax.broadcasted_iota(jnp.int32, (128, LANES), 0)
    left = lax.broadcasted_iota(jnp.int32, (128, LANES), 1) < 64

    for first in range(0, PAIRS, GROUP):
        res = table_times(tab, z[first * 128 : (first + GROUP) * 128, :], NT)
        for i in range(GROUP):
            re = res[:128, i * LANES : (i + 1) * LANES]
            im = res[128:, i * LANES : (i + 1) * LANES]
            if first + i == 0:
                extra = table_times(tab, z[32 * 64 :, :], NT)
                middle = re[64:65]
                re = jnp.where((quotient >= 64) & left, extra[:128], re)
                im = jnp.where((quotient >= 64) & left, extra[128:], im)
                im = jnp.where((quotient == 0) & left, middle, im)
            out[pl.ds(2 * (first + i), 128, stride=ROWS), :] = re
            out[pl.ds(2 * (first + i) + 1, 128, stride=ROWS), :] = im


def flip_lines(re, im, rows_tab, lane_tab):
    lane = lax.broadcasted_iota(jnp.int32, (64, LANES), 1)
    total = None
    for part in split(jnp.concatenate([re, im], axis=1)):
        turned = mm(rows_tab[...], part, NN).astype(BF16)
        turned = jnp.concatenate([turned[:, :LANES], turned[:, LANES:]], axis=0)
        done = mm(turned, lane_tab[...], NN)
        total = done if total is None else total + done
    return (
        jnp.where(lane == 0, total[64:128], total[:64]),
        jnp.where(lane == 0, total[192:], total[128:192]),
    )


def columns_kernel(conj, fetched, moved, *refs):
    sources, out, scratch = refs[:8], refs[8], refs[9:]
    groups, width = PAIRS // GROUP, 2 * GROUP
    waits = {}

    def fetch(stage, source, target):
        copy = pltpu.make_async_copy(source, target, scratch[10].at[sum(map(len, waits.values()))])
        copy.start()
        waits.setdefault(stage, []).append(copy)

    def wait(stage):
        for copy in waits.get(stage, []):
            copy.wait()

    held = scratch[:8] if fetched else sources
    tab, tws, g_re, g_im, v_re, v_im, rows_tab, lane_tab = held
    given_rows, made_rows = moved, out
    if fetched:
        given, made = scratch[8:10]
        given_rows, made_rows = given.reshape(4096, LANES), made.reshape(4096, LANES)
        table = [(sources[0].at[2 * i : 2 * i + 2], tab.at[2 * i : 2 * i + 2]) for i in range(4)]
        fetch("0a", *table[0])
        for g in range(groups):
            slots = pl.ds(g * width, width)
            fetch(f"{g}a", moved.at[:, slots, :], given.at[g])
            if g == 0:
                fetch("0b", sources[1], tws)
                fetch("0b", *table[1])
            for i in (2, 3):
                fetch(f"{g}c", sources[i].at[slots], held[i].at[slots])
            if g == 0:
                for i in range(4, 8):
                    fetch("0c", sources[i], held[i])
                fetch("0d", *table[2])
                fetch("0d", *table[3])
    tab1, tab2, tab2i, tab1i = (tab.at[2 * i : 2 * i + 2] for i in range(4))
    tw, twt = tws.at[0:2], tws.at[2:4]

    def part(value, i):
        lanes = slice(i * LANES, (i + 1) * LANES)
        return value[:128, lanes], value[128:, lanes]

    for g in range(groups):
        first = g * GROUP
        base, stride = (g * 128 * width, width) if fetched else (g * width, ROWS)
        rows = [pl.ds(base + 2 * i, 128, stride=stride) for i in range(GROUP)]
        rows_im = [pl.ds(base + 2 * i + 1, 128, stride=stride) for i in range(GROUP)]
        wait(f"{g}a")
        pairs = [jnp.concatenate([given_rows[rows[i], :], given_rows[rows_im[i], :]], axis=0) for i in range(GROUP)]
        data = jnp.concatenate(pairs, axis=1)
        y = table_times(tab1, data, NN)
        wait(f"{g}b")
        turned = [jnp.concatenate(cmul(part(y, i), (tw[0], tw[1])), axis=1) for i in range(GROUP)]
        spec = table_times(tab2, jnp.concatenate(turned, axis=0), NT)
        product = []
        wait(f"{g}c")
        for i in range(GROUP):
            j = first + i
            gr = g_re[2 * j : 2 * j + 2].reshape(128, LANES)
            gi = g_im[2 * j : 2 * j + 2].reshape(128, LANES)
            if conj:
                gi = -gi
            re, im = part(spec, i)
            new_re, new_im = cmul((re, im), (gr, gi))
            if j == 0:
                back_re, back_im = flip_lines(re[:64], im[:64], rows_tab, lane_tab)
                vi = -v_im[...] if conj else v_im[...]
                add_re, add_im = cmul((back_re, -back_im), (v_re[...], vi))
                none = jnp.zeros((64, LANES), F32)
                new_re = new_re + jnp.concatenate([add_re, none], axis=0)
                new_im = new_im + jnp.concatenate([add_im, none], axis=0)
            product.append(jnp.concatenate([new_re, new_im], axis=0))
        wait(f"{g}d")
        w = table_times(tab2i, jnp.concatenate(product, axis=1), NN)
        turned = [jnp.concatenate(cmul(part(w, i), (twt[0], twt[1])), axis=1) for i in range(GROUP)]
        res = table_times(tab1i, jnp.concatenate(turned, axis=0), NT)
        for i in range(GROUP):
            re, im = part(res, i)
            made_rows[rows[i], :] = re
            made_rows[rows_im[i], :] = im
        if fetched:
            fetch("end", made.at[g], out.at[:, pl.ds(g * width, width), :])
    wait("end")


def rows_inverse_kernel(scale, home, tab, tw, out, v):
    quotient = lax.broadcasted_iota(jnp.int32, (128, LANES), 0)
    left = lax.broadcasted_iota(jnp.int32, (128, LANES), 1) < 64

    def finish(y, j):
        re, im = y[:, :LANES], y[:, LANES:]
        for half in range(2):
            p = 2 * j + half
            c, s = tw[0, p : p + 1, :] * scale, tw[1, p : p + 1, :] * scale
            a, b = re[half * 64 : half * 64 + 64], im[half * 64 : half * 64 + 64]
            v[p * 64 : p * 64 + 64, 0:LANES] = a * c - b * s
            v[p * 64 : p * 64 + 64, LANES : 2 * LANES] = a * s + b * c

    for first in range(0, PAIRS, GROUP):
        data = []
        for i in range(GROUP):
            j = first + i
            re = home[pl.ds(2 * j, 128, stride=ROWS), :]
            im = home[pl.ds(2 * j + 1, 128, stride=ROWS), :]
            if j == 0:
                late = (quotient >= 64) & left
                extra = jnp.concatenate([jnp.where(late, re, 0.0).T, jnp.where(late, im, 0.0).T], axis=1)
                middle = im[0:1]
                re = jnp.where(late, jnp.where(quotient == 64, middle, 0.0), re)
                im = jnp.where(late | ((quotient == 0) & left), 0.0, im)
            data.append(jnp.concatenate([re.T, im.T], axis=1))
        if first == 0:
            data.append(extra)
        y = times_table(jnp.concatenate(data, axis=0), tab, NT)
        for i in range(GROUP):
            finish(y[i * 128 : (i + 1) * 128], first + i)
        if first == 0:
            finish(y[GROUP * 128 :], PAIRS)

    def lines(t, _):
        x0 = pl.multiple_of(t * 8, 8)
        values = []
        for p in range(33):
            rows = pl.ds(p * 64 + x0, 8)
            values.append((v[rows, 0:LANES], v[rows, LANES : 2 * LANES]))
        done = real_of_inverse64(values)
        for m in range(64):
            out[m // 8, pl.ds(x0, 8), (m % 8) * LANES : (m % 8 + 1) * LANES] = done[m]
        return 0

    lax.fori_loop(0, 8, lines, 0)


def bits3(x):
    hi = x.astype(BF16).astype(F32)
    mid = (x - hi).astype(BF16).astype(F32)
    return hi, mid, x - hi - mid


def list_kernel(fields, flags, packed, ranks, tri):
    rows = lax.broadcasted_iota(jnp.int32, (1024, 1024), 0)
    tri[...] = jnp.where(rows <= lax.broadcasted_iota(jnp.int32, (1024, 1024), 1), 1.0, 0.0).astype(BF16)

    def tile(t, _):
        flag = flags[t]
        upto = mm(jnp.broadcast_to(flag, (16, 1024)).astype(BF16), tri[...], NN)[0:1]
        rank = upto * flag
        ranks[t] = rank
        place = jnp.where(rows.astype(F32) + 1.0 == rank, 1.0, 0.0).astype(BF16)
        values = fields[t]
        parts = jnp.concatenate([*bits3(values), jnp.zeros((8, 1024), F32)], axis=0).astype(BF16)
        res = mm(parts, place, NT)
        packed[t] = res[0:8] + res[8:16] + res[16:24]
        return 0

    lax.fori_loop(0, 8, tile, 0)


def unlist_kernel(packed, ranks, out):
    rows = lax.broadcasted_iota(jnp.int32, (1024, 512), 0).astype(F32) + 1.0

    def tile(t, _):
        found = packed[t]
        line = jnp.concatenate([found[b : b + 1] for b in range(8)], axis=1)
        parts = jnp.concatenate([*bits3(line), jnp.zeros((13, 1024), F32)], axis=0).astype(BF16)
        place = jnp.where(rows == ranks[t][:, :512], 1.0, 0.0).astype(BF16)
        res = mm(parts, place, NN)
        out[t] = res[0:1] + res[1:2] + res[2:3]
        return 0

    lax.fori_loop(0, 8, tile, 0)


def block_of(packed, t, b):
    start = b * 128 if isinstance(b, int) else pl.multiple_of(b * 128, 128)
    return packed[t, :, pl.ds(start, 128)]


def own_keys(m, line):
    upper = jnp.where(line >= 2.0, m * 64.0 + line - 2.0, -1.0)
    lower = jnp.where((line >= 1.0) & (line <= 64.0), m * 64.0 + line - 1.0, -1.0)
    return upper, lower


def edge_keys(m, line):
    return jnp.where(line == 1.0, 8.0 + m, -1.0), jnp.where(line == 65.0, m, -1.0)


def here_of(row):
    return lax.broadcasted_iota(jnp.int32, (LANES, 128), 0).astype(F32) == row[2:3]


def sampled(got, row):
    value = got[:128, :128] * row[3:4] + got[128:, :128] * row[4:5]
    value = value + (got[:128, 128:] * row[5:6] + got[128:, 128:] * row[6:7])
    return jnp.sum(jnp.where(here_of(row), value, 0.0), axis=0, keepdims=True)


def picked(size, keys):
    rows = lax.broadcasted_iota(jnp.int32, (size, 256), 0).astype(F32)
    return jnp.where(rows == jnp.concatenate(keys, axis=1), 1.0, 0.0).astype(BF16)


def more_blocks(block, blocks):
    def tile(t, _):
        def one(b, _):
            block(t, b)
            return 0

        lax.fori_loop(1, blocks[t], one, 0)
        return 0

    lax.fori_loop(0, 8, tile, 0)


def sample_kernel(scale, home, tab, tw, packed, blocks, partial, top, bottom, v, out, r1, r2):
    rows_inverse_kernel(scale, home, tab, tw, out, v)
    for m in range(64):
        lanes = slice((m % 8) * LANES, (m % 8 + 1) * LANES)
        top[m : m + 1, :] = out[m // 8, 0:1, lanes]
        bottom[m : m + 1, :] = out[m // 8, 63:64, lanes]

    for t in range(8):
        for m in range(0, 8, 2):
            pair = [out[t, :, (m + i) * LANES : (m + i + 1) * LANES] for i in range(2)]
            r1[t, :, m * 64 : m * 64 + 128] = jnp.concatenate(pair, axis=0).T
    last = lax.broadcasted_iota(jnp.int32, (LANES, 512), 0) == LANES - 1
    inner = lax.broadcasted_iota(jnp.int32, (8, 512), 1) < 448

    def block(t, b):
        row = block_of(packed, t, b)
        pick = picked(512, own_keys(row[0:1], row[1:2]))
        got = mm(r2[t, 0], pick, NN) + mm(r2[t, 1], pick, NN)
        partial[t, pl.ds(b, 1), :] = sampled(got, row)

    for t in range(8):
        here = r1[t]
        carry = jnp.where(inner, pltpu.roll(r1[t, 0:8], 448, 1), pltpu.roll(r1[(t + 1) % 8, 0:8], 448, 1))
        after = jnp.where(last, carry[0:1], pltpu.roll(here, LANES - 1, 0))
        for i, value in enumerate((here, after)):
            hi, lo = split(value)
            r2[t, 0, i * LANES : (i + 1) * LANES, :] = hi
            r2[t, 1, i * LANES : (i + 1) * LANES, :] = lo
        block(t, 0)

    more_blocks(block, blocks)


def scatter_kernel(packed, partial, blocks, below, above, tab, tw, out, mis, z, strip, f2, edges):
    lane64 = lax.broadcasted_iota(jnp.int32, (64, LANES), 1)
    for i, ref in enumerate((below, above)):
        line = ref[...]
        turned = pltpu.roll(line, LANES - 1, 1)
        after = jnp.where(lane64 == LANES - 1, pltpu.roll(turned, 63, 0), turned)
        for t in range(8):
            edges[t, i * 8 : i * 8 + 8, 0:LANES] = line[t * 8 : t * 8 + 8]
            edges[t, i * 8 : i * 8 + 8, LANES:] = after[t * 8 : t * 8 + 8]
    mis[...] = jnp.zeros((8, 8, 128), F32)

    def block(t, b):
        row = block_of(packed, t, b)
        pick = picked(16, edge_keys(row[0:1], row[1:2]))
        edge = jnp.concatenate([edges[t, :, 0:LANES].T, edges[t, :, LANES:].T], axis=0)
        edge_hi, edge_lo = split(edge)
        got = mm(edge_hi, pick, NN) + mm(edge_lo, pick, NN)
        interp = partial[t, pl.ds(b, 1), :] + sampled(got, row)
        misfit = jnp.where(row[1:2] >= 1.0, interp - row[7:8], 0.0)
        mis[t, pl.ds(b, 1), :] = misfit
        spread = jnp.where(here_of(row), misfit, 0.0)
        values = jnp.concatenate(
            [
                jnp.concatenate([spread * row[3:4], spread * row[5:6]], axis=1),
                jnp.concatenate([spread * row[4:5], spread * row[6:7]], axis=1),
            ],
            axis=0,
        )
        hi, lo = split(values)
        back = picked(512, own_keys(row[0:1], row[1:2]))
        return mm(back, hi, NT) + mm(back, lo, NT)

    for t in range(8):
        f2[t * 512 : t * 512 + 512, :] = block(t, 0)

    def add_block(t, b):
        f2[pl.ds(pl.multiple_of(t * 512, 512), 512), :] += block(t, b)

    more_blocks(add_block, blocks)

    def assemble(t, _):
        before = lax.rem(t + 7, 8)
        last = []
        for m in range(-1, 8):
            start = before * 512 + 448 if m < 0 else t * 512 + m * 64
            last.append(pltpu.roll(f2[pl.ds(pl.multiple_of(start, 64), 64), LANES:], 1, 1))
        for m in range(8):
            own = f2[pl.ds(pl.multiple_of(t * 512 + m * 64, 64), 64), 0:LANES]
            strip[t, :, m * LANES : (m + 1) * LANES] = own + jnp.where(lane64 == 0, last[m], last[m + 1])
        return 0

    lax.fori_loop(0, 8, assemble, 0)
    rows_forward_kernel(strip, tab, tw, out, z)


def mirror_kernel(place, t_re, t_im, m_re, m_im, n_re, n_im, rows_tab, lane_tab, g_re, g_im, v_re, v_im):
    q = place[0]
    zero, low = q == 0, q < 64

    def choose(t, m, n):
        mean, gap = (t[0] + n[...]) * 0.25, (t[0] - n[...]) * 0.25
        own = jnp.where(zero, mean, jnp.where(low, t[0], t[32]))
        other = jnp.where(zero, mean, jnp.where(low, n[...], m[0]))
        return own, other, jnp.where(zero, gap, 0.0)

    own_re, other_re, gap_re = choose(t_re, m_re, n_re)
    own_im, other_im, gap_im = choose(t_im, m_im, n_im)
    back_re, back_im = flip_lines(other_re, other_im, rows_tab, lane_tab)
    g_re[0], g_im[0] = own_re + back_re, own_im - back_im
    back_re, back_im = flip_lines(gap_re, gap_im, rows_tab, lane_tab)
    v_re[...], v_im[...] = gap_re + back_re, gap_im - back_im

    def one(p, _):
        back_re, back_im = flip_lines(m_re[32 - p], m_im[32 - p], rows_tab, lane_tab)
        g_re[p] = t_re[p] + back_re
        g_im[p] = t_im[p] - back_im
        return 0

    lax.fori_loop(1, 32, one, 0, unroll=True)


def call(kernel, out_shape, scratch, *args, name, cost=None, smem=()):
    single = isinstance(out_shape, jax.ShapeDtypeStruct)
    vmem = pl.BlockSpec(memory_space=pltpu.VMEM)
    return pl.pallas_call(
        kernel,
        out_shape=out_shape,
        in_specs=[pl.BlockSpec(memory_space=pltpu.SMEM) if i in smem else vmem for i in range(len(args))],
        out_specs=vmem if single else [vmem] * len(out_shape),
        scratch_shapes=scratch,
        compiler_params=pltpu.CompilerParams(vmem_limit_bytes=VMEM_LIMIT),
        cost_estimate=cost,
        name=name,
    )(*args)


def cost(us):
    return pl.CostEstimate(flops=int(us * 1.0e9), bytes_accessed=4 * 1024 * 1024, transcendentals=0)


def shape(*dims, dtype=F32):
    return jax.ShapeDtypeStruct(dims, dtype)


def flips():
    b = np.arange(64)
    rows = np.zeros((128, 64), np.float32)
    rows[b, 63 - b] = 1.0
    rows[64 + b, (64 - b) % 64] = 1.0
    a = np.arange(128)
    lanes = np.zeros((128, 128), np.float32)
    lanes[(128 - a) % 128, a] = 1.0
    return rows.astype(jnp.bfloat16), lanes.astype(jnp.bfloat16)


def tables():
    n = np.arange(LANES)
    p = np.minimum(np.arange(BLOCKS), 32)
    x1 = np.arange(128) % 64
    fwd, inv = complex_table(128, 1, -1.0), complex_table(128, 1, 1.0)
    fwd2, inv2 = complex_table(64, 2, -1.0), complex_table(64, 2, 1.0)
    return {
        "fwd": split_np(fwd),
        "inv": split_np(inv),
        "columns": jnp.asarray(np.concatenate([split_np(t) for t in (fwd, fwd2, inv2, inv)])),
        "row_fwd": twiddle_table(p, n, -1.0),
        "row_inv": twiddle_table(p, n, 1.0),
        "col_turn": jnp.asarray(np.concatenate([twiddle_table(n, x1, -1.0), twiddle_table(x1, n, 1.0)])),
        "flip_rows": jnp.asarray(flips()[0]),
        "flip_lanes": jnp.asarray(flips()[1]),
    }


def rows_forward(strip, tabs):
    return call(
        rows_forward_kernel,
        shape(128 * ROWS, LANES),
        [pltpu.VMEM((BLOCKS * 64, 2 * LANES), F32)],
        strip,
        tabs["fwd"],
        tabs["row_fwd"],
        name="rows_forward",
        cost=cost(4),
    )


def columns(moved, lines, conj, fetched, tabs):
    spec = pl.BlockSpec(memory_space=pltpu.HBM if fetched else pltpu.VMEM)
    rest = (tabs["columns"], tabs["col_turn"], *lines, tabs["flip_rows"], tabs["flip_lanes"])
    buffer = pltpu.VMEM((PAIRS // GROUP, 128, 2 * GROUP, LANES), F32)
    scratch = [pltpu.VMEM(a.shape, a.dtype) for a in rest] + [buffer, buffer, pltpu.SemaphoreType.DMA((25,))]
    dims = (128, ROWS, LANES) if fetched else (128 * ROWS, LANES)
    return pl.pallas_call(
        functools.partial(columns_kernel, conj, fetched),
        out_shape=shape(*dims),
        in_specs=[spec] * 9,
        out_specs=spec,
        scratch_shapes=scratch if fetched else [],
        compiler_params=pltpu.CompilerParams(vmem_limit_bytes=(60 if fetched else 40) * MIB),
        cost_estimate=cost(7),
        name="columns",
    )(moved.reshape(dims), *rest)


def rows_inverse(home, scale, tabs):
    return call(
        functools.partial(rows_inverse_kernel, scale),
        shape(8, 64, 1024),
        [pltpu.VMEM((BLOCKS * 64, 2 * LANES), F32)],
        home,
        tabs["inv"],
        tabs["row_inv"],
        name="rows_inverse",
        cost=cost(6),
    )


def listed(fields, flags):
    return call(
        list_kernel,
        (shape(8, 8, 1024), shape(8, 1, 1024)),
        [pltpu.VMEM((1024, 1024), BF16)],
        fields,
        flags,
        name="listed",
        cost=cost(10),
    )


def unlisted(packed, ranks):
    return call(unlist_kernel, shape(8, 1, 512), [], packed, ranks, name="unlisted", cost=cost(4))


def sample(home, packed, blocks, scale, tabs):
    return call(
        functools.partial(sample_kernel, scale),
        (shape(8, 8, 128), shape(64, LANES), shape(64, LANES)),
        [
            pltpu.VMEM((BLOCKS * 64, 2 * LANES), F32),
            pltpu.VMEM((8, 64, 1024), F32),
            pltpu.VMEM((8, LANES, 512), F32),
            pltpu.VMEM((8, 2, 256, 512), BF16),
        ],
        home,
        tabs["inv"],
        tabs["row_inv"],
        packed,
        blocks,
        name="sample",
        cost=cost(8),
        smem=(4,),
    )


def scatter(packed, partial, blocks, below, above, tabs):
    return call(
        scatter_kernel,
        (shape(128 * ROWS, LANES), shape(8, 8, 128)),
        [
            pltpu.VMEM((BLOCKS * 64, 2 * LANES), F32),
            pltpu.VMEM((8, 64, 1024), F32),
            pltpu.VMEM((4096, 256), F32),
            pltpu.VMEM((8, 16, 256), F32),
        ],
        packed,
        partial,
        blocks,
        below,
        above,
        tabs["fwd"],
        tabs["row_fwd"],
        name="scatter",
        cost=cost(8),
        smem=(2,),
    )


def mirror(place, *lines, tabs):
    vmem = pl.BlockSpec(memory_space=pltpu.VMEM)
    return pl.pallas_call(
        mirror_kernel,
        out_shape=(shape(32, 64, LANES), shape(32, 64, LANES), shape(64, LANES), shape(64, LANES)),
        in_specs=[pl.BlockSpec(memory_space=pltpu.SMEM)] + [vmem] * 8,
        out_specs=[vmem] * 4,
        compiler_params=pltpu.CompilerParams(vmem_limit_bytes=VMEM_LIMIT),
        cost_estimate=cost(6),
        name="mirror",
    )(place, *lines, tabs["flip_rows"], tabs["flip_lanes"])


BOTH = ("row", "col")


def swap(array):
    pieces = array.reshape(128, ROWS, LANES)
    return lax.all_to_all(pieces, BOTH, split_axis=0, concat_axis=0, tiled=True).reshape(128 * ROWS, LANES)


def across(array):
    return lax.all_to_all(array, "col", split_axis=0, concat_axis=0, tiled=True)


def ring(array, by):
    return lax.ppermute(array, BOTH, [(i, (i + by) % 128) for i in range(128)])


def station_fields(cells, weights, means, counts):
    local_x = cells[0] - lax.axis_index("row") * 512
    local_y = cells[1] - lax.axis_index("col") * 1024
    live = jnp.arange(means.shape[0], dtype=jnp.int32) < counts[0]
    return jnp.stack(
        [local_x.astype(F32), local_y.astype(F32)]
        + [weights[k] for k in range(4)]
        + [means, live.astype(F32)]
    )


def candidates(gathered):
    gathered, previous = gathered[:, 0], gathered[:, 1]
    column = lax.axis_index("col")
    start = column.astype(F32) * 64.0
    upper = jnp.where(column == 0, previous, gathered)
    line_own = gathered[:, 0] - start
    line_upper = upper[:, 0] - jnp.where(column == 0, 512.0, start)
    flag_own = (line_own >= 0.0) & (line_own < 64.0) & (gathered[:, 7] > 0.5)
    flag_upper = (line_upper == -1.0) & (upper[:, 7] > 0.5)
    flags = jnp.concatenate([flag_own, flag_upper], axis=1).astype(F32)
    both = jnp.concatenate([gathered, upper], axis=2)
    line = jnp.concatenate([line_own, line_upper], axis=1) + 2.0
    y = both[:, 1]
    high = jnp.floor(y * (1.0 / 128.0))
    packed = jnp.stack([high, line, y - high * 128.0] + [both[:, k] for k in range(2, 7)], axis=1)
    return packed, flags


def local(
    roughness,
    transfer_real,
    transfer_imag,
    station_cells,
    station_weights,
    station_means,
    station_counts,
):
    tabs = tables()
    mirrored = [(i, 127 - i) for i in range(128)]
    first_rows = [(i, 128 - i if i > 64 else 0) for i in range(64, 128)]
    m_re = lax.ppermute(transfer_real[32:], BOTH, mirrored)
    m_im = lax.ppermute(transfer_imag[32:], BOTH, mirrored)
    n_both = lax.ppermute(jnp.stack([transfer_real[0], transfer_imag[0]]), BOTH, first_rows)
    place = (lax.axis_index("row") * 8 + lax.axis_index("col")).reshape(1).astype(jnp.int32)
    fields = station_fields(station_cells, station_weights, station_means, station_counts)
    previous = lax.ppermute(fields, "row", [(i, (i + 1) % 16) for i in range(16)])

    strip = across(roughness.reshape(8, 64, 1024))
    lines_done = rows_forward(strip, tabs)
    lines_done, m_re, m_im, n_both, previous = lax.optimization_barrier((lines_done, m_re, m_im, n_both, previous))
    moved = swap(lines_done)
    halves = [a.reshape(-1, 64, 128) for a in (transfer_real[:33], transfer_imag[:33], m_re, m_im)]
    both = n_both.reshape(2, 64, 128)
    lines = mirror(place, *halves, both[0], both[1], tabs=tabs)
    *lines, fields = lax.optimization_barrier((*lines, jnp.stack([fields, previous])))
    gathered = lax.all_gather(fields, "col", axis=0, tiled=False)
    moved, gathered = lax.optimization_barrier((moved, gathered))
    home = swap(columns(moved, lines, False, True, tabs))

    fields, flags = candidates(gathered)
    blocks = ((jnp.sum(flags, axis=1) + 127.0) * (1.0 / 128.0)).astype(jnp.int32)
    packed, ranks = listed(fields, flags.reshape(8, 1, 1024))
    partial, top, bottom = sample(home, packed, blocks, 1.0 / (N * N), tabs)
    below, above = ring(top, -1), ring(bottom, 1)
    lines_done, mis = scatter(packed, partial, blocks, below, above, tabs)

    moved = swap(lines_done)
    moved, mis = lax.optimization_barrier((moved, mis))
    found = unlisted(mis, ranks).reshape(8, 512)
    shares = lax.all_gather(found, "col", axis=0, tiled=False)
    home = swap(columns(moved, lines, True, False, tabs))
    home, shares = lax.optimization_barrier((home, shares))
    own = lax.dynamic_index_in_dim(shares, lax.axis_index("col"), axis=1, keepdims=False)
    misfit = jnp.sum(own, axis=0)
    scale = math.sqrt(N * N / 65536.0) / (N * N)
    gradient = across(rows_inverse(home, scale, tabs)).reshape(512, 1024)
    return (gradient, misfit)


def solution(mesh):
    in_specs = (
        P("row", "col"),
        P(("row", "col"), None),
        P(("row", "col"), None),
        P(None, ("row", "col")),
        P(None, ("row", "col")),
        P(("row", "col")),
        P(("row", "col")),
    )
    out_specs = (P("row", "col"), P(("row", "col")))
    return jax.shard_map(local, mesh=mesh, in_specs=in_specs, out_specs=out_specs, check_vma=False)
```

```python
import functools
import math

import jax
import jax.numpy as jnp
import numpy as np
from jax import lax
from jax.experimental import pallas as pl
from jax.experimental.pallas import tpu as pltpu
from jax.sharding import PartitionSpec as P

F32 = jnp.float32
BF16 = jnp.bfloat16

N = 8192
LANES = 128
SHORT = 64
PAIRS = 16
ROWS = 2 * PAIRS
BLOCKS = 34
GROUP = 4
MIB = 1024 * 1024
VMEM_LIMIT = 40 * MIB


def split_np(table):
    hi = table.astype(np.float32).astype(jnp.bfloat16)
    lo = (table - hi.astype(np.float64)).astype(np.float32).astype(jnp.bfloat16)
    return np.stack([hi, lo])


def complex_table(length, copies, sign):
    index = np.arange(length)
    angles = 2.0 * np.pi * (index[:, None] * index[None, :] % length) / length
    cos = np.kron(np.eye(copies), np.cos(angles))
    sin = sign * np.kron(np.eye(copies), np.sin(angles))
    return np.block([[cos, -sin], [sin, cos]])


def twiddle_table(left, right, sign):
    angles = 2.0 * np.pi * (left[:, None] * right[None, :] % N) / N
    return np.stack([np.cos(angles), sign * np.sin(angles)]).astype(np.float32)


def split(x):
    hi = x.astype(BF16)
    lo = (x - hi.astype(F32)).astype(BF16)
    return hi, lo


def mm(a, b, dims):
    return lax.dot_general(a, b, (dims, ((), ())), preferred_element_type=F32)


NN = ((1,), (0,))
NT = ((1,), (1,))


def table_times(tab, data, dims):
    hi, lo = split(data)
    return mm(tab[0], hi, dims) + (mm(tab[1], hi, dims) + mm(tab[0], lo, dims))


def times_table(data, tab, dims):
    hi, lo = split(data)
    return mm(hi, tab[0], dims) + (mm(hi, tab[1], dims) + mm(lo, tab[0], dims))


RT = math.sqrt(0.5)


def cadd(a, b):
    return (a[0] + b[0], a[1] + b[1])


def csub(a, b):
    return (a[0] - b[0], a[1] - b[1])


def cmul(a, b):
    return (a[0] * b[0] - a[1] * b[1], a[0] * b[1] + a[1] * b[0])


def times_i(a, sign):
    return (-a[1], a[0]) if sign > 0 else (a[1], -a[0])


def turn(a, angle):
    c, s = math.cos(angle), math.sin(angle)
    return (a[0] * c - a[1] * s, a[0] * s + a[1] * c)


def dft4(x, sign):
    a, b = cadd(x[0], x[2]), csub(x[0], x[2])
    c, d = cadd(x[1], x[3]), times_i(csub(x[1], x[3]), sign)
    return [cadd(a, c), cadd(b, d), csub(a, c), csub(b, d)]


def eighth(a, sign):
    if sign > 0:
        return ((a[0] - a[1]) * RT, (a[0] + a[1]) * RT)
    return ((a[0] + a[1]) * RT, (a[1] - a[0]) * RT)


def dft8(x, sign):
    even = dft4(x[0::2], sign)
    odd = dft4(x[1::2], sign)
    odd[1] = eighth(odd[1], sign)
    odd[2] = times_i(odd[2], sign)
    odd[3] = times_i(eighth(odd[3], sign), sign)
    return [cadd(even[i], odd[i]) for i in range(4)] + [csub(even[i], odd[i]) for i in range(4)]


def real_dft8(x):
    a, b = x[0] + x[4], x[0] - x[4]
    c, d = x[2] + x[6], x[2] - x[6]
    e, f = x[1] + x[5], x[1] - x[5]
    g, h = x[3] + x[7], x[3] - x[7]
    even, odd = a + c, e + g
    u, v = (f - h) * RT, (f + h) * RT
    return [(even + odd, None), (b + u, -(d + v)), (a - c, g - e), (b - u, d - v), (even - odd, None)]


def real_fft64(x):
    first = [real_dft8([x[8 * u + v] for u in range(8)]) for v in range(8)]
    out = [None] * 33
    zero_part = real_dft8([first[v][0][0] for v in range(8)])
    for t in range(5):
        out[8 * t] = zero_part[t]
    for s in range(1, 4):
        turned = [first[0][s]] + [turn(first[v][s], -2 * math.pi * v * s / 64) for v in range(1, 8)]
        done = dft8(turned, -1)
        for t in range(8):
            p = s + 8 * t
            if p <= 32:
                out[p] = done[t]
            else:
                out[64 - p] = (done[t][0], -done[t][1])
    real = [first[v][4][0] for v in range(8)]
    turned = []
    for v in range(8):
        c, s = math.cos(2 * math.pi * v / 16), -math.sin(2 * math.pi * v / 16)
        turned.append((real[v] * c, real[v] * s))
    turned[0] = (real[0], jnp.zeros_like(real[0]))
    done = dft8(turned, -1)
    for t in range(4):
        out[4 + 8 * t] = done[t]
    return out


def real_of_inverse8(zero, four, one, two, three):
    a, b = zero + four, zero - four
    res = [None] * 8
    even_p, even_m = a + two[0], a - two[0]
    odd_p, odd_m = b - two[1], b + two[1]
    sum_r, dif_i = one[0] + three[0], one[1] - three[1]
    res[0], res[4] = even_p + sum_r, even_p - sum_r
    res[2], res[6] = even_m - dif_i, even_m + dif_i
    k1 = ((one[0] - three[0]) - (one[1] + three[1])) * RT
    k3 = ((three[0] - one[0]) - (one[1] + three[1])) * RT
    res[1], res[5] = odd_p + k1, odd_p - k1
    res[3], res[7] = odd_m + k3, odd_m - k3
    return res


def real_of_inverse64(v):
    zero = real_of_inverse8(v[0][0], v[32][0], v[8], v[16], v[24])
    parts = [v[4], v[12], v[20], v[28]]
    four = []
    quarter = dft4(parts, 1)
    turned = [parts[0], eighth(parts[1], 1), times_i(parts[2], 1), times_i(eighth(parts[3], 1), 1)]
    shifted = dft4(turned, 1)
    for m in range(8):
        value = quarter[m // 2] if m % 2 == 0 else shifted[m // 2]
        angle = 2 * math.pi * m / 16
        four.append(value[0] * math.cos(angle) - value[1] * math.sin(angle) if m else value[0])
    others = []
    for s in range(1, 4):
        x = []
        for t in range(8):
            p = s + 8 * t
            x.append(v[p] if p <= 32 else (v[64 - p][0], -v[64 - p][1]))
        done = dft8(x, 1)
        others.append([done[0]] + [turn(done[m], 2 * math.pi * m * s / 64) for m in range(1, 8)])
    out = [None] * 64
    for m in range(8):
        res = real_of_inverse8(zero[m], four[m], others[0][m], others[1][m], others[2][m])
        for u in range(8):
            out[8 * u + m] = res[u]
    return out


def rows_forward_kernel(strip, tab, tw, out, z):
    def lines(t, _):
        x0 = pl.multiple_of(t * 8, 8)
        x = []
        for m in range(64):
            value = strip[m // 8, pl.ds(x0, 8), (m % 8) * LANES : (m % 8 + 1) * LANES]
            x.append(value)
        done = real_fft64(x)
        for p in range(33):
            re, im = done[p]
            c, s = tw[0, p : p + 1, :], tw[1, p : p + 1, :]
            if im is None:
                new_re, new_im = re * c, re * s
            else:
                new_re, new_im = re * c - im * s, re * s + im * c
            z[pl.ds(p * 64 + x0, 8), 0:LANES] = new_re
            z[pl.ds(p * 64 + x0, 8), LANES : 2 * LANES] = new_im
        return 0

    lax.fori_loop(0, 8, lines, 0)
    z[33 * 64 :, :] = jnp.zeros((64, 2 * LANES), F32)
    quotient = lax.broadcasted_iota(jnp.int32, (128, LANES), 0)
    left = lax.broadcasted_iota(jnp.int32, (128, LANES), 1) < 64

    for first in range(0, PAIRS, GROUP):
        res = table_times(tab, z[first * 128 : (first + GROUP) * 128, :], NT)
        for i in range(GROUP):
            re = res[:128, i * LANES : (i + 1) * LANES]
            im = res[128:, i * LANES : (i + 1) * LANES]
            if first + i == 0:
                extra = table_times(tab, z[32 * 64 :, :], NT)
                middle = re[64:65]
                re = jnp.where((quotient >= 64) & left, extra[:128], re)
                im = jnp.where((quotient >= 64) & left, extra[128:], im)
                im = jnp.where((quotient == 0) & left, middle, im)
            out[pl.ds(2 * (first + i), 128, stride=ROWS), :] = re
            out[pl.ds(2 * (first + i) + 1, 128, stride=ROWS), :] = im


def flip_lines(re, im, rows_tab, lane_tab):
    lane = lax.broadcasted_iota(jnp.int32, (64, LANES), 1)
    total = None
    for part in split(jnp.concatenate([re, im], axis=1)):
        turned = mm(rows_tab[...], part, NN).astype(BF16)
        turned = jnp.concatenate([turned[:, :LANES], turned[:, LANES:]], axis=0)
        done = mm(turned, lane_tab[...], NN)
        total = done if total is None else total + done
    return (
        jnp.where(lane == 0, total[64:128], total[:64]),
        jnp.where(lane == 0, total[192:], total[128:192]),
    )


def columns_kernel(conj, fetched, moved, *refs):
    sources, out, scratch = refs[:8], refs[8], refs[9:]
    groups, width = PAIRS // GROUP, 2 * GROUP
    waits = {}

    def fetch(stage, source, target):
        copy = pltpu.make_async_copy(source, target, scratch[10].at[sum(map(len, waits.values()))])
        copy.start()
        waits.setdefault(stage, []).append(copy)

    def wait(stage):
        for copy in waits.get(stage, []):
            copy.wait()

    held = scratch[:8] if fetched else sources
    tab, tws, g_re, g_im, v_re, v_im, rows_tab, lane_tab = held
    given_rows, made_rows = moved, out
    if fetched:
        given, made = scratch[8:10]
        given_rows, made_rows = given.reshape(4096, LANES), made.reshape(4096, LANES)
        table = [(sources[0].at[2 * i : 2 * i + 2], tab.at[2 * i : 2 * i + 2]) for i in range(4)]
        fetch("0a", *table[0])
        for g in range(groups):
            slots = pl.ds(g * width, width)
            fetch(f"{g}a", moved.at[:, slots, :], given.at[g])
            if g == 0:
                fetch("0b", sources[1], tws)
                fetch("0b", *table[1])
            for i in (2, 3):
                fetch(f"{g}c", sources[i].at[slots], held[i].at[slots])
            if g == 0:
                for i in range(4, 8):
                    fetch("0c", sources[i], held[i])
                fetch("0d", *table[2])
                fetch("0d", *table[3])
    tab1, tab2, tab2i, tab1i = (tab.at[2 * i : 2 * i + 2] for i in range(4))
    tw, twt = tws.at[0:2], tws.at[2:4]

    def part(value, i):
        lanes = slice(i * LANES, (i + 1) * LANES)
        return value[:128, lanes], value[128:, lanes]

    for g in range(groups):
        first = g * GROUP
        base, stride = (g * 128 * width, width) if fetched else (g * width, ROWS)
        rows = [pl.ds(base + 2 * i, 128, stride=stride) for i in range(GROUP)]
        rows_im = [pl.ds(base + 2 * i + 1, 128, stride=stride) for i in range(GROUP)]
        wait(f"{g}a")
        pairs = [jnp.concatenate([given_rows[rows[i], :], given_rows[rows_im[i], :]], axis=0) for i in range(GROUP)]
        data = jnp.concatenate(pairs, axis=1)
        y = table_times(tab1, data, NN)
        wait(f"{g}b")
        turned = [jnp.concatenate(cmul(part(y, i), (tw[0], tw[1])), axis=1) for i in range(GROUP)]
        spec = table_times(tab2, jnp.concatenate(turned, axis=0), NT)
        product = []
        wait(f"{g}c")
        for i in range(GROUP):
            j = first + i
            gr = g_re[2 * j : 2 * j + 2].reshape(128, LANES)
            gi = g_im[2 * j : 2 * j + 2].reshape(128, LANES)
            if conj:
                gi = -gi
            re, im = part(spec, i)
            new_re, new_im = cmul((re, im), (gr, gi))
            if j == 0:
                back_re, back_im = flip_lines(re[:64], im[:64], rows_tab, lane_tab)
                vi = -v_im[...] if conj else v_im[...]
                add_re, add_im = cmul((back_re, -back_im), (v_re[...], vi))
                none = jnp.zeros((64, LANES), F32)
                new_re = new_re + jnp.concatenate([add_re, none], axis=0)
                new_im = new_im + jnp.concatenate([add_im, none], axis=0)
            product.append(jnp.concatenate([new_re, new_im], axis=0))
        wait(f"{g}d")
        w = table_times(tab2i, jnp.concatenate(product, axis=1), NN)
        turned = [jnp.concatenate(cmul(part(w, i), (twt[0], twt[1])), axis=1) for i in range(GROUP)]
        res = table_times(tab1i, jnp.concatenate(turned, axis=0), NT)
        for i in range(GROUP):
            re, im = part(res, i)
            made_rows[rows[i], :] = re
            made_rows[rows_im[i], :] = im
        if fetched:
            fetch("end", made.at[g], out.at[:, pl.ds(g * width, width), :])
    wait("end")


def rows_inverse_kernel(scale, home, tab, tw, out, v):
    quotient = lax.broadcasted_iota(jnp.int32, (128, LANES), 0)
    left = lax.broadcasted_iota(jnp.int32, (128, LANES), 1) < 64

    def finish(y, j):
        re, im = y[:, :LANES], y[:, LANES:]
        for half in range(2):
            p = 2 * j + half
            c, s = tw[0, p : p + 1, :] * scale, tw[1, p : p + 1, :] * scale
            a, b = re[half * 64 : half * 64 + 64], im[half * 64 : half * 64 + 64]
            v[p * 64 : p * 64 + 64, 0:LANES] = a * c - b * s
            v[p * 64 : p * 64 + 64, LANES : 2 * LANES] = a * s + b * c

    for first in range(0, PAIRS, GROUP):
        data = []
        for i in range(GROUP):
            j = first + i
            re = home[pl.ds(2 * j, 128, stride=ROWS), :]
            im = home[pl.ds(2 * j + 1, 128, stride=ROWS), :]
            if j == 0:
                late = (quotient >= 64) & left
                extra = jnp.concatenate([jnp.where(late, re, 0.0).T, jnp.where(late, im, 0.0).T], axis=1)
                middle = im[0:1]
                re = jnp.where(late, jnp.where(quotient == 64, middle, 0.0), re)
                im = jnp.where(late | ((quotient == 0) & left), 0.0, im)
            data.append(jnp.concatenate([re.T, im.T], axis=1))
        if first == 0:
            data.append(extra)
        y = times_table(jnp.concatenate(data, axis=0), tab, NT)
        for i in range(GROUP):
            finish(y[i * 128 : (i + 1) * 128], first + i)
        if first == 0:
            finish(y[GROUP * 128 :], PAIRS)

    def lines(t, _):
        x0 = pl.multiple_of(t * 8, 8)
        values = []
        for p in range(33):
            rows = pl.ds(p * 64 + x0, 8)
            values.append((v[rows, 0:LANES], v[rows, LANES : 2 * LANES]))
        done = real_of_inverse64(values)
        for m in range(64):
            out[m // 8, pl.ds(x0, 8), (m % 8) * LANES : (m % 8 + 1) * LANES] = done[m]
        return 0

    lax.fori_loop(0, 8, lines, 0)


def bits3(x):
    hi = x.astype(BF16).astype(F32)
    mid = (x - hi).astype(BF16).astype(F32)
    return hi, mid, x - hi - mid


def list_kernel(fields, flags, packed, ranks, tri):
    rows = lax.broadcasted_iota(jnp.int32, (1024, 1024), 0)
    tri[...] = jnp.where(rows <= lax.broadcasted_iota(jnp.int32, (1024, 1024), 1), 1.0, 0.0).astype(BF16)

    def tile(t, _):
        flag = flags[t]
        upto = mm(jnp.broadcast_to(flag, (16, 1024)).astype(BF16), tri[...], NN)[0:1]
        rank = upto * flag
        ranks[t] = rank
        place = jnp.where(rows.astype(F32) + 1.0 == rank, 1.0, 0.0).astype(BF16)
        values = fields[t]
        parts = jnp.concatenate([*bits3(values), jnp.zeros((8, 1024), F32)], axis=0).astype(BF16)
        res = mm(parts, place, NT)
        packed[t] = res[0:8] + res[8:16] + res[16:24]
        return 0

    lax.fori_loop(0, 8, tile, 0)


def unlist_kernel(packed, ranks, out):
    rows = lax.broadcasted_iota(jnp.int32, (1024, 512), 0).astype(F32) + 1.0

    def tile(t, _):
        found = packed[t]
        line = jnp.concatenate([found[b : b + 1] for b in range(8)], axis=1)
        parts = jnp.concatenate([*bits3(line), jnp.zeros((13, 1024), F32)], axis=0).astype(BF16)
        place = jnp.where(rows == ranks[t][:, :512], 1.0, 0.0).astype(BF16)
        res = mm(parts, place, NN)
        out[t] = res[0:1] + res[1:2] + res[2:3]
        return 0

    lax.fori_loop(0, 8, tile, 0)


def block_of(packed, t, b):
    start = b * 128 if isinstance(b, int) else pl.multiple_of(b * 128, 128)
    return packed[t, :, pl.ds(start, 128)]


def own_keys(m, line):
    upper = jnp.where(line >= 2.0, m * 64.0 + line - 2.0, -1.0)
    lower = jnp.where((line >= 1.0) & (line <= 64.0), m * 64.0 + line - 1.0, -1.0)
    return upper, lower


def edge_keys(m, line):
    return jnp.where(line == 1.0, 8.0 + m, -1.0), jnp.where(line == 65.0, m, -1.0)


def here_of(row):
    return lax.broadcasted_iota(jnp.int32, (LANES, 128), 0).astype(F32) == row[2:3]


def sampled(got, row):
    value = got[:128, :128] * row[3:4] + got[128:, :128] * row[4:5]
    value = value + (got[:128, 128:] * row[5:6] + got[128:, 128:] * row[6:7])
    return jnp.sum(jnp.where(here_of(row), value, 0.0), axis=0, keepdims=True)


def picked(size, keys):
    rows = lax.broadcasted_iota(jnp.int32, (size, 256), 0).astype(F32)
    return jnp.where(rows == jnp.concatenate(keys, axis=1), 1.0, 0.0).astype(BF16)


def more_blocks(block, blocks):
    for first in range(0, 8, 4):
        most = blocks[first]
        for t in range(first + 1, first + 4):
            most = jnp.maximum(most, blocks[t])

        def some(b, _, first=first):
            for t in range(first, first + 4):
                block(t, b)
            return 0

        lax.fori_loop(1, most, some, 0)


def sample_kernel(scale, home, tab, tw, packed, blocks, partial, top, bottom, v, out, r1, r2):
    rows_inverse_kernel(scale, home, tab, tw, out, v)
    for m in range(64):
        lanes = slice((m % 8) * LANES, (m % 8 + 1) * LANES)
        top[m : m + 1, :] = out[m // 8, 0:1, lanes]
        bottom[m : m + 1, :] = out[m // 8, 63:64, lanes]

    for t in range(8):
        for m in range(0, 8, 2):
            pair = [out[t, :, (m + i) * LANES : (m + i + 1) * LANES] for i in range(2)]
            r1[t, :, m * 64 : m * 64 + 128] = jnp.concatenate(pair, axis=0).T
    last = lax.broadcasted_iota(jnp.int32, (LANES, 512), 0) == LANES - 1
    inner = lax.broadcasted_iota(jnp.int32, (8, 512), 1) < 448

    def block(t, b):
        row = block_of(packed, t, b)
        pick = picked(512, own_keys(row[0:1], row[1:2]))
        got = mm(r2[t, 0], pick, NN) + mm(r2[t, 1], pick, NN)
        partial[t, pl.ds(b, 1), :] = sampled(got, row)

    for t in range(8):
        here = r1[t]
        carry = jnp.where(inner, pltpu.roll(r1[t, 0:8], 448, 1), pltpu.roll(r1[(t + 1) % 8, 0:8], 448, 1))
        after = jnp.where(last, carry[0:1], pltpu.roll(here, LANES - 1, 0))
        for i, value in enumerate((here, after)):
            hi, lo = split(value)
            r2[t, 0, i * LANES : (i + 1) * LANES, :] = hi
            r2[t, 1, i * LANES : (i + 1) * LANES, :] = lo
        block(t, 0)

    more_blocks(block, blocks)


def scatter_kernel(packed, partial, blocks, below, above, tab, tw, out, mis, z, strip, f2, edges):
    lane64 = lax.broadcasted_iota(jnp.int32, (64, LANES), 1)
    for i, ref in enumerate((below, above)):
        line = ref[...]
        turned = pltpu.roll(line, LANES - 1, 1)
        after = jnp.where(lane64 == LANES - 1, pltpu.roll(turned, 63, 0), turned)
        for t in range(8):
            edges[t, i * 8 : i * 8 + 8, 0:LANES] = line[t * 8 : t * 8 + 8]
            edges[t, i * 8 : i * 8 + 8, LANES:] = after[t * 8 : t * 8 + 8]
    mis[...] = jnp.zeros((8, 8, 128), F32)

    def block(t, b):
        row = block_of(packed, t, b)
        pick = picked(16, edge_keys(row[0:1], row[1:2]))
        edge = jnp.concatenate([edges[t, :, 0:LANES].T, edges[t, :, LANES:].T], axis=0)
        edge_hi, edge_lo = split(edge)
        got = mm(edge_hi, pick, NN) + mm(edge_lo, pick, NN)
        interp = partial[t, pl.ds(b, 1), :] + sampled(got, row)
        misfit = jnp.where(row[1:2] >= 1.0, interp - row[7:8], 0.0)
        mis[t, pl.ds(b, 1), :] = misfit
        spread = jnp.where(here_of(row), misfit, 0.0)
        values = jnp.concatenate(
            [
                jnp.concatenate([spread * row[3:4], spread * row[5:6]], axis=1),
                jnp.concatenate([spread * row[4:5], spread * row[6:7]], axis=1),
            ],
            axis=0,
        )
        hi, lo = split(values)
        back = picked(512, own_keys(row[0:1], row[1:2]))
        return mm(back, hi, NT) + mm(back, lo, NT)

    for t in range(8):
        f2[t * 512 : t * 512 + 512, :] = block(t, 0)

    def add_block(t, b):
        f2[t * 512 : t * 512 + 512, :] += block(t, b)

    more_blocks(add_block, blocks)

    def assemble(t, _):
        before = lax.rem(t + 7, 8)
        last = []
        for m in range(-1, 8):
            start = before * 512 + 448 if m < 0 else t * 512 + m * 64
            last.append(pltpu.roll(f2[pl.ds(pl.multiple_of(start, 64), 64), LANES:], 1, 1))
        for m in range(8):
            own = f2[pl.ds(pl.multiple_of(t * 512 + m * 64, 64), 64), 0:LANES]
            strip[t, :, m * LANES : (m + 1) * LANES] = own + jnp.where(lane64 == 0, last[m], last[m + 1])
        return 0

    lax.fori_loop(0, 8, assemble, 0)
    rows_forward_kernel(strip, tab, tw, out, z)


def mirror_kernel(place, t_re, t_im, m_re, m_im, n_re, n_im, rows_tab, lane_tab, g_re, g_im, v_re, v_im, w_re, w_im):
    for source, work in ((m_re, w_re), (m_im, w_im)):
        for first in range(0, 32, 8):
            for b in range(64):
                part = source[first : first + 8, b * LANES : (b + 1) * LANES]
                work[pl.ds(first * 64 + b, 8, stride=64), :] = part
    q = place[0]
    zero, low = q == 0, q < 64

    def choose(t, m, n):
        mean, gap = (t[0] + n[...]) * 0.25, (t[0] - n[...]) * 0.25
        own = jnp.where(zero, mean, jnp.where(low, t[0], t[32]))
        other = jnp.where(zero, mean, jnp.where(low, n[...], m[0:64]))
        return own, other, jnp.where(zero, gap, 0.0)

    own_re, other_re, gap_re = choose(t_re, w_re, n_re)
    own_im, other_im, gap_im = choose(t_im, w_im, n_im)
    back_re, back_im = flip_lines(other_re, other_im, rows_tab, lane_tab)
    g_re[0], g_im[0] = own_re + back_re, own_im - back_im
    back_re, back_im = flip_lines(gap_re, gap_im, rows_tab, lane_tab)
    v_re[...], v_im[...] = gap_re + back_re, gap_im - back_im

    for p in range(1, 32):
        i = (32 - p) * 64
        back_re, back_im = flip_lines(w_re[i : i + 64], w_im[i : i + 64], rows_tab, lane_tab)
        g_re[p] = t_re[p] + back_re
        g_im[p] = t_im[p] - back_im


def call(kernel, out_shape, scratch, *args, name, cost=None, smem=()):
    single = isinstance(out_shape, jax.ShapeDtypeStruct)
    vmem = pl.BlockSpec(memory_space=pltpu.VMEM)
    return pl.pallas_call(
        kernel,
        out_shape=out_shape,
        in_specs=[pl.BlockSpec(memory_space=pltpu.SMEM) if i in smem else vmem for i in range(len(args))],
        out_specs=vmem if single else [vmem] * len(out_shape),
        scratch_shapes=scratch,
        compiler_params=pltpu.CompilerParams(vmem_limit_bytes=VMEM_LIMIT),
        cost_estimate=cost,
        name=name,
    )(*args)


def cost(us):
    return pl.CostEstimate(flops=int(us * 1.0e9), bytes_accessed=4 * 1024 * 1024, transcendentals=0)


def shape(*dims, dtype=F32):
    return jax.ShapeDtypeStruct(dims, dtype)


def flips():
    b = np.arange(64)
    rows = np.zeros((128, 64), np.float32)
    rows[b, 63 - b] = 1.0
    rows[64 + b, (64 - b) % 64] = 1.0
    a = np.arange(128)
    lanes = np.zeros((128, 128), np.float32)
    lanes[(128 - a) % 128, a] = 1.0
    return rows.astype(jnp.bfloat16), lanes.astype(jnp.bfloat16)


def tables():
    n = np.arange(LANES)
    p = np.minimum(np.arange(BLOCKS), 32)
    x1 = np.arange(128) % 64
    fwd, inv = complex_table(128, 1, -1.0), complex_table(128, 1, 1.0)
    fwd2, inv2 = complex_table(64, 2, -1.0), complex_table(64, 2, 1.0)
    return {
        "fwd": split_np(fwd),
        "inv": split_np(inv),
        "columns": jnp.asarray(np.concatenate([split_np(t) for t in (fwd, fwd2, inv2, inv)])),
        "row_fwd": twiddle_table(p, n, -1.0),
        "row_inv": twiddle_table(p, n, 1.0),
        "col_turn": jnp.asarray(np.concatenate([twiddle_table(n, x1, -1.0), twiddle_table(x1, n, 1.0)])),
        "flip_rows": jnp.asarray(flips()[0]),
        "flip_lanes": jnp.asarray(flips()[1]),
    }


def rows_forward(strip, tabs):
    return call(
        rows_forward_kernel,
        shape(128 * ROWS, LANES),
        [pltpu.VMEM((BLOCKS * 64, 2 * LANES), F32)],
        strip,
        tabs["fwd"],
        tabs["row_fwd"],
        name="rows_forward",
        cost=cost(4),
    )


def columns(moved, lines, conj, fetched, tabs):
    spec = pl.BlockSpec(memory_space=pltpu.HBM if fetched else pltpu.VMEM)
    rest = (tabs["columns"], tabs["col_turn"], *lines, tabs["flip_rows"], tabs["flip_lanes"])
    buffer = pltpu.VMEM((PAIRS // GROUP, 128, 2 * GROUP, LANES), F32)
    scratch = [pltpu.VMEM(a.shape, a.dtype) for a in rest] + [buffer, buffer, pltpu.SemaphoreType.DMA((25,))]
    dims = (128, ROWS, LANES) if fetched else (128 * ROWS, LANES)
    return pl.pallas_call(
        functools.partial(columns_kernel, conj, fetched),
        out_shape=shape(*dims),
        in_specs=[spec] * 9,
        out_specs=spec,
        scratch_shapes=scratch if fetched else [],
        compiler_params=pltpu.CompilerParams(vmem_limit_bytes=(60 if fetched else 40) * MIB),
        cost_estimate=cost(7),
        name="columns",
    )(moved.reshape(dims), *rest)


def rows_inverse(home, scale, tabs):
    return call(
        functools.partial(rows_inverse_kernel, scale),
        shape(8, 64, 1024),
        [pltpu.VMEM((BLOCKS * 64, 2 * LANES), F32)],
        home,
        tabs["inv"],
        tabs["row_inv"],
        name="rows_inverse",
        cost=cost(6),
    )


def listed(fields, flags):
    return call(
        list_kernel,
        (shape(8, 8, 1024), shape(8, 1, 1024)),
        [pltpu.VMEM((1024, 1024), BF16)],
        fields,
        flags,
        name="listed",
        cost=cost(10),
    )


def unlisted(packed, ranks):
    return call(unlist_kernel, shape(8, 1, 512), [], packed, ranks, name="unlisted", cost=cost(4))


def sample(home, packed, blocks, scale, tabs):
    return call(
        functools.partial(sample_kernel, scale),
        (shape(8, 8, 128), shape(64, LANES), shape(64, LANES)),
        [
            pltpu.VMEM((BLOCKS * 64, 2 * LANES), F32),
            pltpu.VMEM((8, 64, 1024), F32),
            pltpu.VMEM((8, LANES, 512), F32),
            pltpu.VMEM((8, 2, 256, 512), BF16),
        ],
        home,
        tabs["inv"],
        tabs["row_inv"],
        packed,
        blocks,
        name="sample",
        cost=cost(8),
        smem=(4,),
    )


def scatter(packed, partial, blocks, below, above, tabs):
    return call(
        scatter_kernel,
        (shape(128 * ROWS, LANES), shape(8, 8, 128)),
        [
            pltpu.VMEM((BLOCKS * 64, 2 * LANES), F32),
            pltpu.VMEM((8, 64, 1024), F32),
            pltpu.VMEM((4096, 256), F32),
            pltpu.VMEM((8, 16, 256), F32),
        ],
        packed,
        partial,
        blocks,
        below,
        above,
        tabs["fwd"],
        tabs["row_fwd"],
        name="scatter",
        cost=cost(8),
        smem=(2,),
    )


def mirror(place, *lines, tabs):
    vmem = pl.BlockSpec(memory_space=pltpu.VMEM)
    return pl.pallas_call(
        mirror_kernel,
        out_shape=(shape(32, 64, LANES), shape(32, 64, LANES), shape(64, LANES), shape(64, LANES)),
        in_specs=[pl.BlockSpec(memory_space=pltpu.SMEM)] + [vmem] * 8,
        out_specs=[vmem] * 4,
        scratch_shapes=[pltpu.VMEM((2048, LANES), F32)] * 2,
        compiler_params=pltpu.CompilerParams(vmem_limit_bytes=VMEM_LIMIT),
        cost_estimate=cost(6),
        name="mirror",
    )(place, *lines, tabs["flip_rows"], tabs["flip_lanes"])


BOTH = ("row", "col")


def swap(array):
    pieces = array.reshape(128, ROWS, LANES)
    return lax.all_to_all(pieces, BOTH, split_axis=0, concat_axis=0, tiled=True).reshape(128 * ROWS, LANES)


def across(array):
    return lax.all_to_all(array, "col", split_axis=0, concat_axis=0, tiled=True)


def ring(array, by):
    return lax.ppermute(array, BOTH, [(i, (i + by) % 128) for i in range(128)])


def station_fields(cells, weights, means, counts):
    local_x = cells[0] - lax.axis_index("row") * 512
    local_y = cells[1] - lax.axis_index("col") * 1024
    live = jnp.arange(means.shape[0], dtype=jnp.int32) < counts[0]
    return jnp.stack(
        [local_x.astype(F32), local_y.astype(F32)]
        + [weights[k] for k in range(4)]
        + [means, live.astype(F32)]
    )


def candidates(gathered):
    gathered, previous = gathered[:, 0], gathered[:, 1]
    column = lax.axis_index("col")
    start = column.astype(F32) * 64.0
    upper = jnp.where(column == 0, previous, gathered)
    line_own = gathered[:, 0] - start
    line_upper = upper[:, 0] - jnp.where(column == 0, 512.0, start)
    flag_own = (line_own >= 0.0) & (line_own < 64.0) & (gathered[:, 7] > 0.5)
    flag_upper = (line_upper == -1.0) & (upper[:, 7] > 0.5)
    flags = jnp.concatenate([flag_own, flag_upper], axis=1).astype(F32)
    both = jnp.concatenate([gathered, upper], axis=2)
    line = jnp.concatenate([line_own, line_upper], axis=1) + 2.0
    y = both[:, 1]
    high = jnp.floor(y * (1.0 / 128.0))
    packed = jnp.stack([high, line, y - high * 128.0] + [both[:, k] for k in range(2, 7)], axis=1)
    return packed, flags


def local(
    roughness,
    transfer_real,
    transfer_imag,
    station_cells,
    station_weights,
    station_means,
    station_counts,
):
    tabs = tables()
    mirrored = [(i, 127 - i) for i in range(128)]
    first_rows = [(i, 128 - i if i > 64 else 0) for i in range(64, 128)]
    m_re = lax.ppermute(transfer_real[32:], BOTH, mirrored)
    m_im = lax.ppermute(transfer_imag[32:], BOTH, mirrored)
    n_both = lax.ppermute(jnp.stack([transfer_real[0], transfer_imag[0]]), BOTH, first_rows)
    place = (lax.axis_index("row") * 8 + lax.axis_index("col")).reshape(1).astype(jnp.int32)
    fields = station_fields(station_cells, station_weights, station_means, station_counts)
    previous = lax.ppermute(fields, "row", [(i, (i + 1) % 16) for i in range(16)])

    strip = across(roughness.reshape(8, 64, 1024))
    lines_done = rows_forward(strip, tabs)
    lines_done, m_re, m_im, n_both, previous = lax.optimization_barrier((lines_done, m_re, m_im, n_both, previous))
    moved = swap(lines_done)
    halves = [a.reshape(-1, 64, 128) for a in (transfer_real[:33], transfer_imag[:33])]
    both = n_both.reshape(2, 64, 128)
    lines = mirror(place, *halves, m_re, m_im, both[0], both[1], tabs=tabs)
    *lines, fields = lax.optimization_barrier((*lines, jnp.stack([fields, previous])))
    gathered = lax.all_gather(fields, "col", axis=0, tiled=False)
    moved, gathered = lax.optimization_barrier((moved, gathered))
    home = swap(columns(moved, lines, False, True, tabs))

    fields, flags = candidates(gathered)
    blocks = ((jnp.sum(flags, axis=1) + 127.0) * (1.0 / 128.0)).astype(jnp.int32)
    packed, ranks = listed(fields, flags.reshape(8, 1, 1024))
    partial, top, bottom = sample(home, packed, blocks, 1.0 / (N * N), tabs)
    below, above = ring(top, -1), ring(bottom, 1)
    lines_done, mis = scatter(packed, partial, blocks, below, above, tabs)

    moved = swap(lines_done)
    moved, mis = lax.optimization_barrier((moved, mis))
    found = unlisted(mis, ranks).reshape(8, 512)
    shares = lax.all_gather(found, "col", axis=0, tiled=False)
    home = swap(columns(moved, lines, True, False, tabs))
    home, shares = lax.optimization_barrier((home, shares))
    own = lax.dynamic_index_in_dim(shares, lax.axis_index("col"), axis=1, keepdims=False)
    misfit = jnp.sum(own, axis=0)
    scale = math.sqrt(N * N / 65536.0) / (N * N)
    gradient = across(rows_inverse(home, scale, tabs)).reshape(512, 1024)
    return (gradient, misfit)


def solution(mesh):
    in_specs = (
        P("row", "col"),
        P(("row", "col"), None),
        P(("row", "col"), None),
        P(None, ("row", "col")),
        P(None, ("row", "col")),
        P(("row", "col")),
        P(("row", "col")),
    )
    out_specs = (P("row", "col"), P(("row", "col")))
    return jax.shard_map(local, mesh=mesh, in_specs=in_specs, out_specs=out_specs, check_vma=False)
```
